128 devices in a mesh: grp: 16 (over y, x), head: 8 (over z, core).
Axes of the slice: x: 4, y: 4, z: 4, core: 2. Of those that a mesh axis runs over, the one named last changes fastest.
Arguments:
- resident_cache: bfloat16 [16, 8, 1536, 576], P('grp'), may hold values from -4 to 4
- lengths: int32 [16, 8], P('grp'), may hold values from 1 to 1536, 7680 in all within a row
- slices: bfloat16 [256, 64, 576], P('grp'), may hold values from -4 to 4
- placement: int32 [256, 1], P('grp'), may hold values from 0 to 15; in each aligned block of 16 rows (0 to 15, 16 to 31, ...) at most 2 rows name the same one
- queries: bfloat16 [3, 16, 9, 24576], P(None, 'grp', None, 'head')
- latents: bfloat16 [3, 16, 9, 576], P(None, 'grp'), may hold values from -4 to 4
- w_key: bfloat16 [128, 128, 512], P('head'), may hold values from -0.5 to 0.5
- w_value: bfloat16 [128, 512, 128], P('head'), may hold values from -4 to 4
- w_out: bfloat16 [16384, 7168], P('head', 'grp'), may hold values from -0.046875 to 0.046875
Outputs:
- mixed: bfloat16 [3, 16, 9, 7168], P(None, 'grp', None, 'head')
The draws below stay inside these ranges and needn't reach their ends.
Inputs may be any that keep to these rules, and one draw needn't show every extreme that they name: `placement`: among the 16 slices of one owner no decode group is named more than 2 times, a bound that some block reaches. `lengths`: the largest length in each group equals 1536.
All inputs are finite; a program needn't handle non-finite values.
Results may differ from the reference program's by a relative error of at most 0.019.
Values may be sent and summed in bfloat16 or wider, within the bound.
A program may use at most 192 MiB of HBM per device.

```python
import math
import jax
import jax.numpy as jnp
import numpy as np
from jax import lax

H = 128
KV = 512
ROPE = 64
NOPE = 128
VD = 128
D = 7168
ROWS = 8
LRES = 1536
S = 16
SL = 64
CAP = 2
STEPS = 3
GROUPS = 16
SLICES = 256


def draw_queries(key, part):
    key = jax.random.fold_in(key, 11)
    shape = (STEPS, GROUPS, ROWS + 1, H, NOPE + ROPE)
    base = jnp.clip(jax.random.normal(key, shape, jnp.float32), -4.0, 4.0)
    return base.reshape(STEPS, GROUPS, ROWS + 1, H * (NOPE + ROPE)).astype(jnp.bfloat16)


def draw_latents(key, part):
    key = jax.random.fold_in(key, 12)
    shape = (STEPS, GROUPS, ROWS + 1, KV + ROPE)
    base = jnp.clip(jax.random.normal(key, shape, jnp.float32), -4.0, 4.0)
    return base.astype(jnp.bfloat16)


def draw_resident_cache(key, part):
    key = jax.random.fold_in(key, 13)
    shape = (GROUPS, ROWS, LRES, KV + ROPE)
    base = jnp.clip(jax.random.normal(key, shape, jnp.float32), -4.0, 4.0)
    return base.astype(jnp.bfloat16)


def draw_slices(key, part):
    key = jax.random.fold_in(key, 14)
    shape = (SLICES, SL, KV + ROPE)
    base = jnp.clip(jax.random.normal(key, shape, jnp.float32), -4.0, 4.0)
    return base.astype(jnp.bfloat16)


def levels(stream_key, dims, cuts, least, high):
    gain = 1.0
    for axis_at, shards_of in cuts:
        draws = jax.random.uniform(jax.random.fold_in(jax.random.fold_in(stream_key, 6), axis_at), (shards_of,), jnp.float32, least / len(cuts), high / len(cuts))
        gain = gain * jnp.repeat(jnp.exp(draws), dims[axis_at] // shards_of).reshape((-1,) + (1,) * (len(dims) - 1 - axis_at))
    return gain


def length_profile(number_of, total, limit, skew):
    loads = [(1 << 20) // math.isqrt(rank ** skew) + 1 for rank in range(2, number_of + 1)]
    surplus, holding = total - limit - (number_of - 1), [1] * (number_of - 1)
    while surplus > 0:
        candidates = [i for i in range(number_of - 1) if holding[i] < limit]
        pool, left = sum([loads[i] for i in candidates]), surplus
        for i in candidates:
            addition = min(limit - holding[i], max(1, left * loads[i] // pool), surplus)
            holding[i] = holding[i] + addition
            surplus = surplus - addition
    return np.array([limit] + holding)


def uneven_parts(key, count, total, bound, slope):
    if count == 2:
        one = jax.random.randint(key, (), max(1, total - bound), min(bound, total - 1) + 1)
        return jnp.stack([one, total - one])
    sizes = jnp.asarray(length_profile(count, total, bound, slope), jnp.int32)
    couples = (count - 1) // 2
    donor, taker = sizes[1:1 + 2 * couples:2], sizes[2:2 + 2 * couples:2]
    margin = jnp.minimum(donor - 1, bound - taker)
    passed = jax.random.randint(jax.random.fold_in(key, 1), (couples,), 0, 1 << 20) % (margin + 1)
    sizes = sizes.at[1:1 + 2 * couples:2].set(donor - passed).at[2:2 + 2 * couples:2].set(taker + passed)
    return sizes[jax.random.permutation(jax.random.fold_in(key, 2), count)]


def deal_out(own_key, own, number, rows, count, top, limit, slope):
    sequence = jax.random.permutation(own_key, count)
    crowded, common = portions_of(count, rows * top, limit, slope, True), portions_of(count, rows * top, limit, slope, False)
    places = jnp.arange(count)

    def named(sizes, turn):
        used = int((sizes > 0).sum())
        fixed = max(1, used // 4)
        passed = fixed + (places - fixed + turn * (used - fixed)) % max(1, count - fixed)
        return jnp.zeros((count,), jnp.int32).at[sequence[jnp.where(places < fixed, places, passed)]].set(jnp.asarray(sizes, jnp.int32))

    sizes = jnp.where(number % 4 == 0, named(crowded, number // 4), named(common, number - number // 4 - 1))
    mixed = jax.random.permutation(jax.random.fold_in(own, 3), count)
    source_of, sink = mixed[0:count // 2 * 2:2], mixed[1:count // 2 * 2:2]
    margin = jnp.minimum(sizes[source_of] - 1, limit - sizes[sink]) // 2
    margin = jnp.where((source_of == sequence[0]) | (sink == sequence[0]) | (sizes[sink] == 0), 0, jnp.maximum(margin, 0))
    passed = jax.random.randint(jax.random.fold_in(own, 4), (count // 2,), 0, 1 << 20) % (margin + 1)
    sizes = sizes.at[source_of].add(-passed).at[sink].add(passed)
    members = jnp.searchsorted(jnp.cumsum(sizes), jnp.arange(rows * top), side="right").astype(jnp.int32)
    table = members.reshape(top, rows).T
    table = table[jax.random.permutation(jax.random.fold_in(own, 1), rows)]
    turn = jax.random.randint(jax.random.fold_in(own, 2), (rows, 1), 0, top)
    return jnp.take_along_axis(table, (jnp.arange(top)[None, :] + turn) % top, axis=1)


def portions_of(number_of, total, limit, slope, full):
    loads = [(1 << 20) // math.isqrt(grade ** slope) + 1 for grade in range(1, number_of + 1)]
    largest = limit if full else min(limit, max(-(-total // number_of), total * loads[0] // sum(loads)))
    least = 1 if total - largest >= number_of - 1 else 0
    counts, surplus = [largest] + [least] * (number_of - 1), total - largest - least * (number_of - 1)
    while surplus > 0:
        movable = [i for i in range(1, number_of) if counts[i] < largest] or [i for i in range(1, number_of) if counts[i] < limit]
        mass, remaining = sum([loads[i] for i in movable]), surplus
        for i in movable:
            more = min(limit - counts[i], max(1, remaining * loads[i] // mass), surplus)
            counts[i] = counts[i] + more
            surplus = surplus - more
    return np.array(counts)


def scatter_about(stream_key, dims, width, limit, pieces=(), held_as=jnp.bfloat16):
    drawn = width * jax.random.normal(stream_key, dims, jnp.float32)
    if pieces:
        drawn = drawn * levels(stream_key, dims, pieces, -0.22, 0.18)
    return jnp.clip(drawn, -limit, limit).astype(held_as)


def setup_inputs(seed: int = 0) -> dict:
    splits = jax.random.split(jax.random.key(seed), 10)
    resident_cache = draw_resident_cache(jax.random.fold_in(splits[9], 71), 0)
    lengths = jax.vmap(lambda own: uneven_parts(own, ROWS, ROWS * LRES * 5 // 8, LRES, 2))(jax.random.split(splits[1], GROUPS)).reshape((GROUPS, ROWS)).astype(jnp.int32)
    slices = draw_slices(jax.random.fold_in(splits[9], 71), 0)
    placement_keys = jax.random.split(jax.random.fold_in(splits[3], 1), SLICES // S)
    placement_turns = jax.random.permutation(jax.random.fold_in(splits[3], 3), SLICES // S)
    placement = jax.vmap(lambda own, number: deal_out(jax.random.fold_in(splits[3], 2), own, number, S, GROUPS, 1, CAP, 2))(placement_keys, placement_turns).reshape((SLICES, 1))
    queries = draw_queries(jax.random.fold_in(splits[9], 71), 0)
    latents = draw_latents(jax.random.fold_in(splits[9], 71), 0)
    w_key = scatter_about(splits[6], (H, NOPE, KV), NOPE ** -0.5, 0.5, ((0, 8),))
    w_value = scatter_about(splits[7], (H, KV, VD), (max(KV // 256, 1)) ** -0.5, 4.0, ((0, 8),))
    w_out = scatter_about(splits[8], (H * VD, D), (H * VD) ** -0.5, 0.046875, ((0, 8), (1, 16)))
    return {"resident_cache": resident_cache, "lengths": lengths, "slices": slices, "placement": placement, "queries": queries, "latents": latents, "w_key": w_key, "w_value": w_value, "w_out": w_out}


def prepare(question, w_key):
    nope_part = question[..., :NOPE].astype(jnp.float32)
    absorbed = jnp.einsum('rhd,hdc->rhc', nope_part, w_key.astype(jnp.float32)).astype(jnp.bfloat16)
    return jnp.concatenate([absorbed, question[..., NOPE:]], axis=-1)

def attend(asked, stored, stored_mask, recent):
    score_scale = 1.0 / math.sqrt(NOPE + ROPE)
    asked_wide = asked.astype(jnp.float32)
    s_stored = jnp.einsum('rhc,rlc->rhl', asked_wide, stored.astype(jnp.float32)) * score_scale
    s_stored = jnp.where(stored_mask[:, None, :], s_stored, -jnp.inf)
    s_recent = jnp.einsum('rhc,rtc->rht', asked_wide, recent.astype(jnp.float32)) * score_scale
    highest = jnp.maximum(lax.optimization_barrier(jnp.max(s_stored, axis=-1)), lax.optimization_barrier(jnp.max(s_recent, axis=-1)))
    e_stored = jnp.exp(s_stored - highest[..., None])
    e_recent = jnp.exp(s_recent - highest[..., None])
    denominator = lax.optimization_barrier(jnp.sum(e_stored, axis=-1)) + lax.optimization_barrier(jnp.sum(e_recent, axis=-1))
    p_stored = lax.optimization_barrier((e_stored / denominator[..., None]).astype(jnp.bfloat16)).astype(jnp.float32)
    p_recent = lax.optimization_barrier((e_recent / denominator[..., None]).astype(jnp.bfloat16)).astype(jnp.float32)
    latent = jnp.einsum('rhl,rlc->rhc', p_stored, stored[..., :KV].astype(jnp.float32))
    return latent + jnp.einsum('rht,rtc->rhc', p_recent, recent[..., :KV].astype(jnp.float32))

def finish(latent, w_value):
    rounded = lax.optimization_barrier(latent.astype(jnp.bfloat16)).astype(jnp.float32)
    return jnp.einsum('rhc,hcv->rhv', rounded, w_value.astype(jnp.float32)).astype(jnp.bfloat16)

def reference(resident_cache, lengths, slices, placement, queries, latents, w_key, w_value, w_out):
    arrived = slices.reshape(1, SLICES * SL, KV + ROPE)
    owners = placement[:, 0]

    def one_group(packed):
        stored, valid_len, asking, recent_all, index = packed
        stored_mask = jnp.arange(LRES, dtype=jnp.int32)[None, :] < valid_len[:, None]
        join_mask = jnp.repeat(owners == index, SL)[None, :]
        results = []
        for step_index in range(STEPS):
            question = asking[step_index].reshape(ROWS + 1, H, NOPE + ROPE)
            prepared = prepare(question, w_key)
            own_keys = jnp.swapaxes(recent_all[:step_index + 1], 0, 1)
            upper = attend(prepared[:ROWS], stored, stored_mask, own_keys[:ROWS])
            lower = attend(prepared[ROWS:], arrived, join_mask, own_keys[ROWS:])
            latent = jnp.concatenate([upper, lower], axis=0)
            heads_out = finish(latent, w_value).reshape(ROWS + 1, H * VD)
            results.append(jnp.dot(heads_out, w_out, preferred_element_type=jnp.float32).astype(jnp.bfloat16))
        return jnp.stack(results)
    mixed = lax.map(one_group, (resident_cache, lengths, jnp.swapaxes(queries, 0, 1), jnp.swapaxes(latents, 0, 1), jnp.arange(GROUPS, dtype=jnp.int32)))
    return jnp.swapaxes(mixed, 0, 1)
```

```python
import functools
import math

import jax
import jax.numpy as jnp
from jax import lax
from jax.experimental import pallas as pl
from jax.experimental.pallas import tpu as pltpu
from jax.sharding import PartitionSpec as P

KV = 512
ROPE = 64
NOPE = 128
VD = 128
ROWS = 8
LRES = 1536
SL = 64
CAP = 2
STEPS = 3

MESH = pl.DeviceIdType.MESH
SCALE = 1.0 / math.sqrt(NOPE + ROPE)
LOWEST = float(jnp.finfo(jnp.float32).min)
BF16 = jnp.bfloat16
F32 = jnp.float32
WIDE = 640
PAD = 4
HEADS = 16
ASK = HEADS * PAD
TOK = 16


def remote(src, dst, send_sem, recv_sem, dev):
    return pltpu.make_async_remote_copy(
        src_ref=src, dst_ref=dst, send_sem=send_sem, recv_sem=recv_sem, device_id=dev, device_id_type=MESH
    )


def nt(a, b):
    return lax.dot_general(a, b, (((1,), (1,)), ((), ())), preferred_element_type=F32)


def nn(a, b):
    return jnp.dot(a, b, preferred_element_type=F32)


def step_mask(rows, width):
    step = lax.broadcasted_iota(jnp.int32, (rows, width), 0) % PAD
    at = lax.broadcasted_iota(jnp.int32, (rows, width), 1)
    return (at < STEPS) & (at <= step)


def kernel(
    lengths, code, queries, latents, cache, slices, w_key, w_value, w_out,
    out,
    kt, wk, wv, wo, sl, slw, k_send, qf, lat,
    q_all, q_sib, q8, k8, o_sib, lt, o8_send, o8, st_send, st8,
    gath, p_send, p_recv, p_sum, red,
    dma, sib_s, sib_r, sl_s, sl_r, z_s, z_r, ag_s, ag_r, red_s, red_r,
):
    g = lax.axis_index("grp")
    h = lax.axis_index("head")
    y, x = g // 4, g % 4
    z, c = h // 2, h % 2
    sib = (g, h + 1 - 2 * c)

    load_wk = pltpu.make_async_copy(w_key, wk, dma.at[0])
    load_sl = pltpu.make_async_copy(slices.at[:, pl.ds(TOK * z, TOK), :], sl, dma.at[1])
    load_kt = [pltpu.make_async_copy(cache.at[4 * c + i], kt.at[i], dma.at[2 + i]) for i in range(4)]
    load_wv = pltpu.make_async_copy(w_value, wv, dma.at[6])
    load_wo = pltpu.make_async_copy(w_out, wo, dma.at[7])
    load_sl.start()
    load_wk.start()
    for cp in load_kt:
        cp.start()
    load_wv.start()
    load_wo.start()

    barrier = pltpu.get_barrier_semaphore()
    for i in range(1, 16):
        pl.semaphore_signal(barrier, inc=1, device_id=((g + i) % 16, h), device_id_type=MESH)
    for i in range(1, 8):
        pl.semaphore_signal(barrier, inc=1, device_id=(g, (h + i) % 8), device_id_type=MESH)

    qf[...] = jnp.zeros_like(qf)
    lat[...] = jnp.zeros_like(lat)
    for r in range(ROWS + 1):
        v = queries[r].astype(F32)
        qf[r, 0:STEPS, :] = v
        qf[r, PAD : PAD + STEPS, :] = v
        lat[r, 0:STEPS, :] = latents[r].astype(F32)

    load_sl.wait()
    slw[:, KV:WIDE] = jnp.ones((16 * TOK, WIDE - KV), BF16)
    slw[:, 0 : KV + ROPE] = sl[...].reshape(16 * TOK, KV + ROPE)
    at0 = lax.broadcasted_iota(jnp.int32, (16 * TOK, 16 * TOK), 0)
    at1 = lax.broadcasted_iota(jnp.int32, (16 * TOK, 16 * TOK), 1)
    chosen = (at0 % TOK == at1 % TOK) & ((at0 // TOK) * CAP + c == code[0:1, :])
    selector = jnp.where(chosen, 1.0, 0.0).astype(BF16)
    k_send[...] = nn(selector, slw[...]).astype(BF16).reshape(16, TOK, WIDE)

    pl.semaphore_wait(barrier, 22)

    slice_sends = []
    for i in range(1, 16):
        to = (g + i) % 16
        cp = remote(k_send.at[to], k8.at[c, pl.ds(TOK * g, TOK)], sl_s.at[i], sl_r.at[i], (to, h))
        cp.start()
        slice_sends.append(cp)
    k8[c, pl.ds(TOK * g, TOK), :] = k_send[g]

    load_wk.wait()
    row = lax.broadcasted_iota(jnp.int32, (72, 128), 0)
    lane = lax.broadcasted_iota(jnp.int32, (72, 128), 1)
    first = row % 8 < PAD
    low = lane < ROPE
    for quad in range(4):
        parts = []
        for p in (2 * quad, 2 * quad + 1):
            t = qf[:, :, 384 * p : 384 * p + 384].reshape(72, 384)
            t0, t1, t2 = t[:, 0:128], t[:, 128:256], t[:, 256:384]
            r1, r2 = pltpu.roll(t1, 64, 1), pltpu.roll(t2, 64, 1)
            second_nope = jnp.where(low, r1, r2)
            rope = jnp.where(low, jnp.where(first, t1, r2), 0.0)
            lhs = jnp.concatenate([jnp.where(first, t0, 0.0), jnp.where(first, 0.0, second_nope)], axis=1)
            absorbed = nn(lhs.astype(BF16), wk[2 * p : 2 * p + 2].reshape(2 * NOPE, KV))
            parts.append(jnp.concatenate([absorbed, rope], axis=1).reshape(9, 8, WIDE))
        q_all[:, 16 * quad : 16 * quad + 16, :] = jnp.concatenate(parts, axis=1).astype(BF16)

    ask_sib = remote(q_all.at[pl.ds(4 * (1 - c), 4)], q_sib, sib_s.at[0], sib_r.at[0], sib)
    ask_sib.start()
    ask_z = []
    for i in range(1, 4):
        to = (z + i) % 4
        cp = remote(q_all.at[8], q8.at[z], z_s.at[i], z_r.at[i], (g, 2 * to + c))
        cp.start()
        ask_z.append(cp)
    q8[z] = q_all[8]
    ask_sib.wait()

    recent_ok = step_mask(2 * ASK, 16)
    lat_sends = []
    for i in range(4):
        load_kt[i].wait()
        q = jnp.concatenate([q_all[4 * c + i], q_sib[i]], axis=0)[:, 0 : KV + ROPE]
        recent = lat[4 * c + i].astype(BF16)
        s = nn(q, kt[i])
        s_new = jnp.where(recent_ok, nt(q, recent), LOWEST)
        ok = lax.broadcasted_iota(jnp.int32, (1, LRES), 1) < lengths[0, 4 * c + i]
        s = jnp.where(ok, s, LOWEST)
        m = jnp.maximum(jnp.max(s, axis=1, keepdims=True), jnp.max(s_new, axis=1, keepdims=True))
        e = jnp.exp((s - m) * SCALE)
        e_new = jnp.exp((s_new - m) * SCALE)
        total = jnp.sum(e, axis=1, keepdims=True) + jnp.sum(e_new, axis=1, keepdims=True)
        o = nt(e.astype(BF16), kt[i, 0:KV, :]) + nn(e_new.astype(BF16), recent[:, 0:KV])
        o = (o / total).astype(BF16)
        lt[4 * c + i] = o[0:ASK]
        o_sib[i] = o[ASK:]
        cp = remote(o_sib.at[i], lt.at[4 * c + i], sib_s.at[1 + i], sib_r.at[1 + i], sib)
        cp.start()
        lat_sends.append(cp)

    for cp in slice_sends:
        cp.wait()
    keys_sib = remote(k8.at[c], k8.at[c], sib_s.at[5], sib_r.at[5], sib)
    keys_sib.start()
    for cp in ask_z:
        cp.wait()
    keys_sib.wait()
    keys = k8[...].reshape(2 * 16 * TOK, WIDE)
    q = q8[...].reshape(4 * ASK, WIDE)
    flag = (lax.broadcasted_iota(jnp.int32, (8, WIDE), 1) == KV + ROPE).astype(BF16)
    present = nt(flag, keys)[0:1] > 0.5
    s = jnp.where(present, nt(q, keys), LOWEST)
    m = jnp.max(s, axis=1, keepdims=True)
    e = jnp.exp((s - m) * SCALE)
    total = jnp.sum(e, axis=1, keepdims=True)
    o8_send[...] = nn(e.astype(BF16), keys[:, 0:KV]).astype(BF16).reshape(4, ASK, KV)
    left = lax.broadcasted_iota(jnp.int32, (4 * ASK, 128), 1) < 64
    st_send[...] = jnp.where(left, m, total).reshape(4, ASK, 128)
    part_z = []
    for i in range(1, 4):
        to = (z + i) % 4
        cp = remote(o8_send.at[to], o8.at[z], z_s.at[3 + i], z_r.at[3 + i], (g, 2 * to + c))
        cp.start()
        part_z.append(cp)
        cp = remote(st_send.at[to], st8.at[z], z_s.at[6 + i], z_r.at[6 + i], (g, 2 * to + c))
        cp.start()
        part_z.append(cp)
    o8[z] = o8_send[z]
    st8[z] = st_send[z]

    q = q_all[8][:, 0 : KV + ROPE]
    recent = lat[8].astype(BF16)
    s_new = jnp.where(step_mask(ASK, 16), nt(q, recent), LOWEST)
    m_new = jnp.max(s_new, axis=1, keepdims=True)
    e_new = jnp.exp((s_new - m_new) * SCALE)
    total_new = jnp.sum(e_new, axis=1, keepdims=True)
    o_new = nn(e_new.astype(BF16), recent[:, 0:KV])
    for cp in part_z:
        cp.wait()
    m_part = [st8[i][:, 0:1] for i in range(4)]
    m = m_new
    for one in m_part:
        m = jnp.maximum(m, one)
    weight = jnp.exp((m_new - m) * SCALE)
    o = o_new * weight
    total = total_new * weight
    for i in range(4):
        weight = jnp.exp((m_part[i] - m) * SCALE)
        o = o + o8[i].astype(F32) * weight
        total = total + st8[i][:, 64:65] * weight
    lt[8] = (o / total).astype(BF16)
    for cp in lat_sends:
        cp.wait()

    load_wv.wait()
    head_of_row = lax.broadcasted_iota(jnp.int32, (144, 512), 0) % 16 // PAD
    head_of_lane = lax.broadcasted_iota(jnp.int32, (144, 512), 1) // VD
    mine = head_of_row == head_of_lane
    to_row = lax.broadcasted_iota(jnp.int32, (32, 144), 0)
    from_row = lax.broadcasted_iota(jnp.int32, (32, 144), 1)
    picks = (
        (to_row < STEPS * (ROWS + 1))
        & (to_row // STEPS == from_row // 16)
        & (to_row % STEPS == from_row % PAD)
    )
    compact = jnp.where(picks, 1.0, 0.0).astype(BF16)
    for quad in range(4):
        lhs = lt[:, 16 * quad : 16 * quad + 16, :].reshape(144, KV)
        rhs = jnp.concatenate([wv[4 * quad + j] for j in range(4)], axis=1)
        heads_out = jnp.where(mine, nn(lhs, rhs), 0.0).astype(BF16)
        gath[g, :, 512 * quad : 512 * quad + 512] = nn(compact, heads_out).astype(BF16)

    ag_sends = []

    def neighbour(axis, d):
        if axis == 0:
            return (y * 4 + (x + d) % 4, h)
        return ((y + d) % 4 * 4 + x, h)

    def block(k, r1, r2):
        dx, dy = (r1, r2) if k == 0 else (r2, r1)
        return (y + dy) % 4 * 4 + (x + dx) % 4

    def view(k, r1, r2, half):
        rows = pl.ds(0, 32) if half is None else pl.ds(16 * half, 16)
        return gath.at[block(k, r1, r2), rows, pl.ds(1024 * k, 1024)]

    def arrival(k, r1, r2, half):
        return ag_r.at[((k * 4 + r1 % 4) * 4 + r2 % 4) * 2 + (half or 0)]

    def send(k, ring, d, r1, r2, half):
        axis = ring if k == 0 else 1 - ring
        q1, q2 = (r1 - d, r2) if ring == 0 else (r1, r2 - d)
        ref = view(k, r1, r2, half)
        cp = remote(ref, ref, ag_s.at[len(ag_sends)], arrival(k, q1, q2, half), neighbour(axis, d))
        cp.start()
        ag_sends.append(cp)

    def landed(k, r1, r2, half):
        ref = view(k, r1, r2, half)
        remote(ref, ref, ag_s.at[0], arrival(k, r1, r2, half), neighbour(0, 1)).wait_recv()

    for ring in (0, 1):
        for k in (0, 1):
            send(k, ring, 1, 0, 0, None)
            send(k, ring, -1, 0, 0, None)
    for d in (1, -1):
        for k in (0, 1):
            landed(k, -d, 0, None)
            send(k, 0, d, -d, 0, 0 if d == 1 else 1)
            send(k, 1, 1, -d, 0, None)
            send(k, 1, -1, -d, 0, None)
    for k in (0, 1):
        landed(k, 2, 0, 0)
        landed(k, 2, 0, 1)
        send(k, 1, 1, 2, 0, None)
        send(k, 1, -1, 2, 0, None)
    for b in (0, -1, 1, 2):
        for d in (1, -1):
            for k in (0, 1):
                landed(k, b, -d, None)
                send(k, 1, d, b, -d, 0 if d == 1 else 1)
    for b in (0, -1, 1, 2):
        for k in (0, 1):
            landed(k, b, 2, 0)
            landed(k, b, 2, 1)

    load_wo.wait()
    theirs = gath[pl.ds(8 * (1 - c), 8)].reshape(256, 2048)
    p_send[...] = nt(theirs, wo[...]).astype(BF16)
    swap = remote(p_send, p_recv, sib_s.at[6], sib_r.at[6], sib)
    swap.start()
    ours = nt(gath[pl.ds(8 * c, 8)].reshape(256, 2048), wo[...])
    swap.wait()
    p_sum[...] = (ours + p_recv[...].astype(F32)).astype(BF16).reshape(8, 32, 448)

    keeper = g // 2
    slot = (g % 2) * 4 + z
    for i in range(8):
        to = 8 * c + i

        @pl.when(jnp.logical_or(to != g, keeper != h))
        def _():
            remote(p_sum.at[i], red.at[slot], red_s.at[i], red_r.at[slot], (to, keeper)).start()

        @pl.when(jnp.logical_and(to == g, keeper == h))
        def _():
            red[slot] = p_sum[i]

    half_of = g // 8
    for j in range(2):
        for k in range(4):
            at = j * 4 + k

            @pl.when(jnp.logical_or(2 * h + j != g, 2 * k + half_of != h))
            def _():
                remote(p_sum.at[0], red.at[at], red_s.at[0], red_r.at[at], (g, h)).wait_recv()

    for j in range(2):
        acc = red[4 * j].astype(F32)
        for k in range(1, 4):
            acc = acc + red[4 * j + k].astype(F32)
        out[j] = acc.astype(BF16)

    for i in range(8):
        to = 8 * c + i

        @pl.when(jnp.logical_or(to != g, keeper != h))
        def _():
            remote(p_sum.at[i], red.at[slot], red_s.at[i], red_r.at[slot], (to, keeper)).wait_send()

    for cp in ag_sends:
        cp.wait_send()


def body(resident_cache, lengths, slices, placement, queries, latents, w_key, w_value, w_out):
    owners = placement[:, 0]
    count = owners.shape[0]
    alike = owners[:, None] == owners[None, :]
    before = jnp.arange(count)[:, None] < jnp.arange(count)[None, :]
    code = owners * CAP + jnp.sum(alike & before, axis=0).astype(jnp.int32)
    code = jnp.broadcast_to(jnp.repeat(code, TOK)[None, :], (8, count * TOK))
    vmem = pl.BlockSpec(memory_space=pltpu.VMEM)
    smem = pl.BlockSpec(memory_space=pltpu.SMEM)
    anywhere = pl.BlockSpec(memory_space=pl.ANY)
    sems = pltpu.SemaphoreType.DMA
    out = pl.pallas_call(
        kernel,
        out_shape=jax.ShapeDtypeStruct((2, 32, 448), BF16),
        in_specs=[smem, vmem, vmem, vmem] + [anywhere] * 5,
        out_specs=vmem,
        scratch_shapes=[
            pltpu.VMEM((4, KV + ROPE, LRES), BF16),
            pltpu.VMEM((HEADS, NOPE, KV), BF16),
            pltpu.VMEM((HEADS, KV, VD), BF16),
            pltpu.VMEM((448, HEADS * VD), BF16),
            pltpu.VMEM((16, TOK, KV + ROPE), BF16),
            pltpu.VMEM((16 * TOK, WIDE), BF16),
            pltpu.VMEM((16, TOK, WIDE), BF16),
            pltpu.VMEM((ROWS + 1, 8, HEADS * 192), F32),
            pltpu.VMEM((ROWS + 1, 16, KV + ROPE), F32),
            pltpu.VMEM((ROWS + 1, ASK, WIDE), BF16),
            pltpu.VMEM((4, ASK, WIDE), BF16),
            pltpu.VMEM((4, ASK, WIDE), BF16),
            pltpu.VMEM((2, 16 * TOK, WIDE), BF16),
            pltpu.VMEM((4, ASK, KV), BF16),
            pltpu.VMEM((ROWS + 1, ASK, KV), BF16),
            pltpu.VMEM((4, ASK, KV), BF16),
            pltpu.VMEM((4, ASK, KV), BF16),
            pltpu.VMEM((4, ASK, 128), F32),
            pltpu.VMEM((4, ASK, 128), F32),
            pltpu.VMEM((16, 32, 2048), BF16),
            pltpu.VMEM((256, 448), BF16),
            pltpu.VMEM((256, 448), BF16),
            pltpu.VMEM((8, 32, 448), BF16),
            pltpu.VMEM((8, 32, 448), BF16),
            sems((8,)),
            sems((7,)),
            sems((7,)),
            sems((16,)),
            sems((16,)),
            sems((10,)),
            sems((10,)),
            sems((40,)),
            sems((64,)),
            sems((8,)),
            sems((8,)),
        ],
        compiler_params=pltpu.CompilerParams(
            collective_id=0, has_side_effects=True, vmem_limit_bytes=56 * 1024 * 1024
        ),
        name="decode",
    )(
        lengths,
        code,
        jnp.swapaxes(queries[:, 0], 0, 1),
        jnp.swapaxes(latents[:, 0], 0, 1),
        jnp.swapaxes(resident_cache[0], 1, 2),
        slices,
        w_key,
        w_value,
        jnp.swapaxes(w_out, 0, 1),
    )
    mixed = jnp.swapaxes(out, 0, 1).reshape(32, 896)[: STEPS * (ROWS + 1)]
    mixed = jnp.swapaxes(mixed.reshape(ROWS + 1, STEPS, 896), 0, 1)
    return mixed[:, None]


def solution(mesh):
    placed = (
        P("grp", None, None, None),
        P("grp", None),
        P("grp", None, None),
        P("grp", None),
        P(None, "grp", None, "head"),
        P(None, "grp", None, None),
        P("head", None, None),
        P("head", None, None),
        P("head", "grp"),
    )
    return jax.shard_map(
        body, mesh=mesh, in_specs=placed, out_specs=P(None, "grp", None, "head"), check_vma=False
    )
```

```python
import math

import jax
import jax.numpy as jnp
from jax import lax
from jax.experimental import pallas as pl
from jax.experimental.pallas import tpu as pltpu
from jax.sharding import PartitionSpec as P

KV = 512
ROPE = 64
NOPE = 128
VD = 128
ROWS = 8
LRES = 1536
SL = 64
CAP = 2
STEPS = 3

MESH = pl.DeviceIdType.MESH
SCALE = 1.0 / math.sqrt(NOPE + ROPE)
LOWEST = -3.0e38
BF16 = jnp.bfloat16
F32 = jnp.float32
WIDE = 640
PAD = 4
HEADS = 16
ASK = HEADS * PAD
TOK = 16


def remote(src, dst, send_sem, recv_sem, dev):
    return pltpu.make_async_remote_copy(
        src_ref=src, dst_ref=dst, send_sem=send_sem, recv_sem=recv_sem, device_id=dev, device_id_type=MESH
    )


def nt(a, b):
    return lax.dot_general(a, b, (((1,), (1,)), ((), ())), preferred_element_type=F32)


def nn(a, b):
    return jnp.dot(a, b, preferred_element_type=F32)


def step_mask(rows, width):
    step = lax.broadcasted_iota(jnp.int32, (rows, width), 0) % PAD
    at = lax.broadcasted_iota(jnp.int32, (rows, width), 1)
    return (at < STEPS) & (at <= step)


def kernel(
    lengths, placement, queries, latents, cache, slices, w_key, w_value, w_out,
    out,
    kt, wk, wv, wo, sl, slw, k_send, qv, lv, qf, lat,
    q_all, q_sib, q8, k8, o_sib, lt, o8_send, o8,
    gath, p_all, p_send, p_recv, p_sum, red,
    dma, sib_s, sib_r, sl_s, sl_r, z_s, z_r, ag_s, ag_r, red_s, red_r,
):
    g = lax.axis_index("grp")
    h = lax.axis_index("head")
    y, x = g // 4, g % 4
    z, c = h // 2, h % 2
    sib = (g, h + 1 - 2 * c)

    load_sl = pltpu.make_async_copy(slices.at[:, pl.ds(TOK * z, TOK), :], sl, dma.at[1])
    load_qv = pltpu.make_async_copy(queries, qv, dma.at[8])
    load_lv = pltpu.make_async_copy(latents, lv, dma.at[9])
    load_wk = pltpu.make_async_copy(w_key, wk, dma.at[0])
    load_kt = [pltpu.make_async_copy(cache.at[4 * c + i], kt.at[i], dma.at[2 + i]) for i in range(4)]
    load_wv = pltpu.make_async_copy(w_value, wv, dma.at[6])
    load_wo = pltpu.make_async_copy(w_out, wo.at[0:448], dma.at[7])
    load_qv.start()
    load_sl.start()
    load_wk.start()
    load_lv.start()
    load_kt[0].start()
    load_kt[1].start()
    load_wv.start()
    load_kt[2].start()
    load_kt[3].start()
    load_wo.start()

    barrier = pltpu.get_barrier_semaphore()
    for i in range(1, 16):
        pl.semaphore_signal(barrier, inc=1, device_id=((g + i) % 16, h), device_id_type=MESH)
    for i in range(1, 8):
        pl.semaphore_signal(barrier, inc=1, device_id=(g, (h + i) % 8), device_id_type=MESH)

    qf[...] = jnp.zeros_like(qf)
    lat[...] = jnp.zeros_like(lat)
    owners = [placement[0, i] for i in range(16)]
    owner_of_lane = lax.broadcasted_iota(jnp.int32, (8, 16 * TOK), 1) // TOK
    code = jnp.zeros((8, 16 * TOK), jnp.int32)
    for i in range(16):
        rank = jnp.int32(0)
        for j in range(i):
            rank = rank + jnp.where(owners[j] == owners[i], 1, 0)
        code = jnp.where(owner_of_lane == i, owners[i] * CAP + rank, code)

    slw[:, KV:WIDE] = jnp.ones((16 * TOK, WIDE - KV), BF16)
    at0 = lax.broadcasted_iota(jnp.int32, (16 * TOK, 16 * TOK), 0)
    at1 = lax.broadcasted_iota(jnp.int32, (16 * TOK, 16 * TOK), 1)
    chosen = (at0 % TOK == at1 % TOK) & ((at0 // TOK) * CAP + c == code[0:1, :])
    selector = jnp.where(chosen, 1.0, 0.0).astype(BF16)
    load_sl.wait()
    slw[:, 0 : KV + ROPE] = sl[...].reshape(16 * TOK, KV + ROPE)
    k_send[...] = nn(selector, slw[...]).astype(BF16).reshape(16, TOK, WIDE)

    load_qv.wait()
    load_lv.wait()
    for r in range(ROWS + 1):
        v = qv[r].astype(F32)
        qf[r, 0:STEPS, :] = v
        qf[r, PAD : PAD + STEPS, :] = v
        lat[r, 0:STEPS, :] = lv[r].astype(F32)

    pl.semaphore_wait(barrier, 22)

    slice_sends = []
    for i in range(1, 16):
        to = (g + i) % 16
        cp = remote(k_send.at[to], k8.at[c, pl.ds(TOK * g, TOK)], sl_s.at[i], sl_r.at[i], (to, h))
        cp.start()
        slice_sends.append(cp)
    k8[c, pl.ds(TOK * g, TOK), :] = k_send[g]

    load_wk.wait()
    row = lax.broadcasted_iota(jnp.int32, (72, 128), 0)
    lane = lax.broadcasted_iota(jnp.int32, (72, 128), 1)
    first = row % 8 < PAD
    low = lane < ROPE
    for quad in range(4):
        parts = []
        for p in (2 * quad, 2 * quad + 1):
            t = qf[:, :, 384 * p : 384 * p + 384].reshape(72, 384)
            t0, t1, t2 = t[:, 0:128], t[:, 128:256], t[:, 256:384]
            r1, r2 = pltpu.roll(t1, 64, 1), pltpu.roll(t2, 64, 1)
            second_nope = jnp.where(low, r1, r2)
            rope = jnp.where(low, jnp.where(first, t1, r2), 0.0)
            lhs = jnp.concatenate([jnp.where(first, t0, 0.0), jnp.where(first, 0.0, second_nope)], axis=1)
            absorbed = nn(lhs.astype(BF16), wk[2 * p : 2 * p + 2].reshape(2 * NOPE, KV))
            parts.append(jnp.concatenate([absorbed, rope], axis=1).reshape(9, 8, WIDE))
        q_all[:, 16 * quad : 16 * quad + 16, :] = jnp.concatenate(parts, axis=1).astype(BF16)

    ask_sib = remote(q_all.at[pl.ds(4 * (1 - c), 4)], q_sib, sib_s.at[0], sib_r.at[0], sib)
    ask_sib.start()
    ask_z = []
    for i in range(1, 4):
        to = (z + i) % 4
        cp = remote(q_all.at[8], q8.at[z], z_s.at[i], z_r.at[i], (g, 2 * to + c))
        cp.start()
        ask_z.append(cp)
    q8[z] = q_all[8]
    ask_sib.wait()

    recent_ok = step_mask(2 * ASK, 16)

    def resident(i):
        load_kt[i].wait()
        q = jnp.concatenate([q_all[4 * c + i], q_sib[i]], axis=0)[:, 0 : KV + ROPE]
        recent = lat[4 * c + i].astype(BF16)
        s = nn(q, kt[i])
        s_new = jnp.where(recent_ok, nt(q, recent), LOWEST)
        ok = lax.broadcasted_iota(jnp.int32, (1, LRES), 1) < lengths[0, 4 * c + i]
        s = jnp.where(ok, s, LOWEST)
        m = jnp.maximum(jnp.max(s, axis=1, keepdims=True), jnp.max(s_new, axis=1, keepdims=True))
        e = jnp.exp((s - m) * SCALE)
        e_new = jnp.exp((s_new - m) * SCALE)
        total = jnp.sum(e, axis=1, keepdims=True) + jnp.sum(e_new, axis=1, keepdims=True)
        o = nt(e.astype(BF16), kt[i, 0:KV, :]) + nn(e_new.astype(BF16), recent[:, 0:KV])
        o = (o / total).astype(BF16)
        at = (i // 2) * 4 + c * 2 + i % 2
        lt[at] = o[0:ASK]
        o_sib[i] = o[ASK:]
        cp = remote(o_sib.at[i], lt.at[at], sib_s.at[1 + i], sib_r.at[1 + i], sib)
        cp.start()
        return cp

    def values(part):
        lo, count = (0, 4) if part == 0 else (4, 5)
        rows = 16 * count
        head_of_row = lax.broadcasted_iota(jnp.int32, (rows, 512), 0) % 16 // PAD
        head_of_lane = lax.broadcasted_iota(jnp.int32, (rows, 512), 1) // VD
        mine = head_of_row == head_of_lane
        to_row = lax.broadcasted_iota(jnp.int32, (16, rows), 0)
        from_row = lax.broadcasted_iota(jnp.int32, (16, rows), 1)
        picks = (
            (to_row < STEPS * count)
            & (to_row // STEPS == from_row // 16)
            & (to_row % STEPS == from_row % PAD)
        )
        compact = jnp.where(picks, 1.0, 0.0).astype(BF16)
        for quad in range(4):
            lhs = lt[lo : lo + count, 16 * quad : 16 * quad + 16, :].reshape(rows, KV)
            rhs = jnp.concatenate([wv[4 * quad + j] for j in range(4)], axis=1)
            heads_out = jnp.where(mine, nn(lhs, rhs), 0.0).astype(BF16)
            gath[part, g, :, 512 * quad : 512 * quad + 512] = nn(compact, heads_out).astype(BF16)

    ag_sends = []

    def neighbour(axis, d):
        if axis == 0:
            return (y * 4 + (x + d) % 4, h)
        return ((y + d) % 4 * 4 + x, h)

    def view(part, k, r1, r2, half):
        dx, dy = (r1, r2) if k == 0 else (r2, r1)
        columns = pl.ds(1024 * k, 1024) if half is None else pl.ds(1024 * k + 512 * half, 512)
        return gath.at[part, (y + dy) % 4 * 4 + (x + dx) % 4, :, columns]

    def arrival(part, k, r1, r2, half):
        return ag_r.at[(((part * 2 + k) * 4 + r1 % 4) * 4 + r2 % 4) * 2 + (half or 0)]

    def send(part, k, ring, d, r1, r2, half):
        axis = ring if k == 0 else 1 - ring
        q1, q2 = (r1 - d, r2) if ring == 0 else (r1, r2 - d)
        ref = view(part, k, r1, r2, half)
        cp = remote(ref, ref, ag_s.at[len(ag_sends)], arrival(part, k, q1, q2, half), neighbour(axis, d))
        cp.start()
        ag_sends.append(cp)

    def landed(part, k, r1, r2, half):
        ref = view(part, k, r1, r2, half)
        remote(ref, ref, ag_s.at[0], arrival(part, k, r1, r2, half), neighbour(0, 1)).wait_recv()

    def gather_own(part):
        for ring in (0, 1):
            for k in (0, 1):
                send(part, k, ring, 1, 0, 0, None)
                send(part, k, ring, -1, 0, 0, None)

    def gather_near(part):
        for d in (1, -1):
            for k in (0, 1):
                landed(part, k, -d, 0, None)
                send(part, k, 0, d, -d, 0, 0 if d == 1 else 1)
                send(part, k, 1, 1, -d, 0, None)
                send(part, k, 1, -1, -d, 0, None)

    def gather_far(part):
        for k in (0, 1):
            landed(part, k, 2, 0, 0)
            landed(part, k, 2, 0, 1)
            send(part, k, 1, 1, 2, 0, None)
            send(part, k, 1, -1, 2, 0, None)

    def gather_relay(part):
        for b in (0, -1, 1, 2):
            for d in (1, -1):
                for k in (0, 1):
                    landed(part, k, b, -d, None)
                    send(part, k, 1, d, b, -d, 0 if d == 1 else 1)

    def gather_end(part):
        for b in (0, -1, 1, 2):
            for k in (0, 1):
                landed(part, k, b, 2, 0)
                landed(part, k, b, 2, 1)

    def project(part):
        p_all[...] = nt(gath[part].reshape(256, 2048), wo[...]).reshape(16, 16, 512)
        p_send[part] = p_all[pl.ds(8 * (1 - c), 8)].astype(BF16)
        cp = remote(p_send.at[part], p_recv.at[part], sib_s.at[6 + part], sib_r.at[6 + part], sib)
        cp.start()
        cp.wait()
        p_sum[part] = (p_all[pl.ds(8 * c, 8)] + p_recv[part].astype(F32)).astype(BF16)

    keeper = g // 2
    slot = (g % 2) * 4 + z

    def hand(part, i):
        return remote(
            p_sum.at[part, i], red.at[part, slot], red_s.at[8 * part + i], red_r.at[8 * part + slot],
            (8 * c + i, keeper),
        )

    def hand_out(part):
        for i in range(8):
            to = 8 * c + i

            @pl.when(jnp.logical_or(to != g, keeper != h))
            def _():
                hand(part, i).start()

            @pl.when(jnp.logical_and(to == g, keeper == h))
            def _():
                red[part, slot] = p_sum[part, i]

    def take_in(part):
        half_of = g // 8
        for j in range(2):
            for k in range(4):
                at = j * 4 + k

                @pl.when(jnp.logical_or(2 * h + j != g, 2 * k + half_of != h))
                def _():
                    remote(
                        p_sum.at[part, 0], red.at[part, at], red_s.at[0], red_r.at[8 * part + at], sib
                    ).wait_recv()

        sums = []
        for j in range(2):
            acc = red[part, 4 * j].astype(F32)
            for k in range(1, 4):
                acc = acc + red[part, 4 * j + k].astype(F32)
            sums.append(acc)
        shifted = pltpu.roll(sums[1], 64, 1)
        lane = lax.broadcasted_iota(jnp.int32, (16, 128), 1)
        middle = jnp.where(lane < 64, sums[0][:, 384:512], shifted[:, 0:128])
        mixed = jnp.concatenate([sums[0][:, 0:384], middle, shifted[:, 128:512]], axis=1)
        rows = (0, 1, 4, 5) if part == 0 else (2, 3, 6, 7, 8)
        for a, r in enumerate(rows):
            out[r] = mixed[STEPS * a : STEPS * a + STEPS].astype(BF16)

    wo[448:512, :] = jnp.zeros((64, 2048), BF16)
    lat_sends = [resident(0), resident(1)]
    for cp in lat_sends:
        cp.wait()
    load_wv.wait()
    values(0)
    gather_own(0)
    lat_sends = [resident(2)]
    gather_near(0)

    for cp in slice_sends:
        cp.wait()
    keys_sib = remote(k8.at[c], k8.at[c], sib_s.at[5], sib_r.at[5], sib)
    keys_sib.start()
    lat_sends.append(resident(3))
    gather_far(0)

    for cp in ask_z:
        cp.wait()
    keys_sib.wait()
    keys = k8[...].reshape(2 * 16 * TOK, WIDE)
    q = q8[...].reshape(4 * ASK, WIDE)
    flag = (lax.broadcasted_iota(jnp.int32, (8, WIDE), 1) == KV + ROPE).astype(BF16)
    present = nt(flag, keys)[0:1] > 0.5
    s = jnp.where(present, nt(q, keys), LOWEST)
    m = jnp.max(s, axis=1, keepdims=True)
    e = jnp.exp((s - m) * SCALE)
    total = jnp.sum(e, axis=1, keepdims=True)
    o = nn(e.astype(BF16), keys[:, 0:KV])
    lane = lax.broadcasted_iota(jnp.int32, (4 * ASK, 128), 1)
    stats = jnp.zeros((4 * ASK, 128), F32)
    for n, rest in enumerate((m, total)):
        for t in range(3):
            piece = rest.astype(BF16).astype(F32)
            rest = rest - piece
            stats = jnp.where(lane == 3 * n + t, piece, stats)
    o8_send[...] = jnp.concatenate([o, stats], axis=1).astype(BF16).reshape(4, ASK, WIDE)
    part_z = []
    for i in range(1, 4):
        to = (z + i) % 4
        cp = remote(o8_send.at[to], o8.at[z], z_s.at[3 + i], z_r.at[3 + i], (g, 2 * to + c))
        cp.start()
        part_z.append(cp)
    o8[z] = o8_send[z]

    gather_relay(0)

    q = q_all[8][:, 0 : KV + ROPE]
    recent = lat[8].astype(BF16)
    s_new = jnp.where(step_mask(ASK, 16), nt(q, recent), LOWEST)
    m_new = jnp.max(s_new, axis=1, keepdims=True)
    e_new = jnp.exp((s_new - m_new) * SCALE)
    total_new = jnp.sum(e_new, axis=1, keepdims=True)
    o_new = nn(e_new.astype(BF16), recent[:, 0:KV])
    for cp in part_z:
        cp.wait()
    m_part, total_part = [], []
    for i in range(4):
        st = o8[i][:, KV:WIDE].astype(F32)
        m_part.append(st[:, 0:1] + st[:, 1:2] + st[:, 2:3])
        total_part.append(st[:, 3:4] + st[:, 4:5] + st[:, 5:6])
    m = m_new
    for one in m_part:
        m = jnp.maximum(m, one)
    weight = jnp.exp((m_new - m) * SCALE)
    o = o_new * weight
    total = total_new * weight
    for i in range(4):
        weight = jnp.exp((m_part[i] - m) * SCALE)
        o = o + o8[i][:, 0:KV].astype(F32) * weight
        total = total + total_part[i] * weight
    lt[8] = (o / total).astype(BF16)
    for cp in lat_sends:
        cp.wait()
    values(1)
    gather_own(1)

    load_wo.wait()
    gather_end(0)
    project(0)
    gather_near(1)
    hand_out(0)
    gather_far(1)
    gather_relay(1)
    take_in(0)
    gather_end(1)
    project(1)
    hand_out(1)
    take_in(1)

    for part in (0, 1):
        for i in range(8):
            pl.when(jnp.logical_or(8 * c + i != g, keeper != h))(hand(part, i).wait_send)
    for cp in ag_sends:
        cp.wait_send()


def body(resident_cache, lengths, slices, placement, queries, latents, w_key, w_value, w_out):
    vmem = pl.BlockSpec(memory_space=pltpu.VMEM)
    smem = pl.BlockSpec(memory_space=pltpu.SMEM)
    anywhere = pl.BlockSpec(memory_space=pl.ANY)
    sems = pltpu.SemaphoreType.DMA
    out = pl.pallas_call(
        kernel,
        out_shape=jax.ShapeDtypeStruct((ROWS + 1, STEPS, 896), BF16),
        in_specs=[smem, smem] + [anywhere] * 7,
        out_specs=vmem,
        scratch_shapes=[
            pltpu.VMEM((4, KV + ROPE, LRES), BF16),
            pltpu.VMEM((HEADS, NOPE, KV), BF16),
            pltpu.VMEM((HEADS, KV, VD), BF16),
            pltpu.VMEM((512, HEADS * VD), BF16),
            pltpu.VMEM((16, TOK, KV + ROPE), BF16),
            pltpu.VMEM((16 * TOK, WIDE), BF16),
            pltpu.VMEM((16, TOK, WIDE), BF16),
            pltpu.VMEM((ROWS + 1, STEPS, HEADS * 192), BF16),
            pltpu.VMEM((ROWS + 1, STEPS, KV + ROPE), BF16),
            pltpu.VMEM((ROWS + 1, 8, HEADS * 192), F32),
            pltpu.VMEM((ROWS + 1, 16, KV + ROPE), F32),
            pltpu.VMEM((ROWS + 1, ASK, WIDE), BF16),
            pltpu.VMEM((4, ASK, WIDE), BF16),
            pltpu.VMEM((4, ASK, WIDE), BF16),
            pltpu.VMEM((2, 16 * TOK, WIDE), BF16),
            pltpu.VMEM((4, ASK, KV), BF16),
            pltpu.VMEM((ROWS + 1, ASK, KV), BF16),
            pltpu.VMEM((4, ASK, WIDE), BF16),
            pltpu.VMEM((4, ASK, WIDE), BF16),
            pltpu.VMEM((2, 16, 16, 2048), BF16),
            pltpu.VMEM((16, 16, 512), F32),
            pltpu.VMEM((2, 8, 16, 512), BF16),
            pltpu.VMEM((2, 8, 16, 512), BF16),
            pltpu.VMEM((2, 8, 16, 512), BF16),
            pltpu.VMEM((2, 8, 16, 512), BF16),
            sems((10,)),
            sems((8,)),
            sems((8,)),
            sems((16,)),
            sems((16,)),
            sems((7,)),
            sems((7,)),
            sems((80,)),
            sems((128,)),
            sems((16,)),
            sems((16,)),
        ],
        compiler_params=pltpu.CompilerParams(
            collective_id=0, has_side_effects=True, vmem_limit_bytes=56 * 1024 * 1024
        ),
        name="decode",
    )(
        lengths,
        placement.reshape(1, 16),
        jnp.swapaxes(queries[:, 0], 0, 1),
        jnp.swapaxes(latents[:, 0], 0, 1),
        jnp.swapaxes(resident_cache[0], 1, 2),
        slices,
        w_key,
        w_value,
        jnp.swapaxes(w_out, 0, 1),
    )
    return jnp.swapaxes(out, 0, 1)[:, None]


def solution(mesh):
    placed = (
        P("grp", None, None, None),
        P("grp", None),
        P("grp", None, None),
        P("grp", None),
        P(None, "grp", None, "head"),
        P(None, "grp", None, None),
        P("head", None, None),
        P("head", None, None),
        P("head", "grp"),
    )
    return jax.shard_map(
        body, mesh=mesh, in_specs=placed, out_specs=P(None, "grp", None, "head"), check_vma=False
    )
```

```python
import math

import jax
import jax.numpy as jnp
from jax import lax
from jax.experimental import pallas as pl
from jax.experimental.pallas import tpu as pltpu
from jax.sharding import PartitionSpec as P

KV = 512
ROPE = 64
NOPE = 128
VD = 128
ROWS = 8
LRES = 1536
SL = 64
CAP = 2
STEPS = 3

MESH = pl.DeviceIdType.MESH
SCALE = 1.0 / math.sqrt(NOPE + ROPE)
LOWEST = -3.0e38
BF16 = jnp.bfloat16
F32 = jnp.float32
WIDE = 640
PAD = 4
HEADS = 16
ASK = HEADS * PAD
WIDTH = (768, 1024)
TOK = 16


def remote(src, dst, send_sem, recv_sem, dev):
    return pltpu.make_async_remote_copy(
        src_ref=src, dst_ref=dst, send_sem=send_sem, recv_sem=recv_sem, device_id=dev, device_id_type=MESH
    )


def nt(a, b):
    return lax.dot_general(a, b, (((1,), (1,)), ((), ())), preferred_element_type=F32)


def nn(a, b):
    return jnp.dot(a, b, preferred_element_type=F32)


def step_mask(rows, width):
    step = lax.broadcasted_iota(jnp.int32, (rows, width), 0) % PAD
    at = lax.broadcasted_iota(jnp.int32, (rows, width), 1)
    return (at < STEPS) & (at <= step)


def kernel(
    lengths, placement, queries, latents, cache, slices, w_key, w_value, w_out,
    out,
    kt, wk, wv, wo, sl, slw, k_send, qv, lv, qf, lat,
    q_all, q_sib, q8, k8, o_sib, lt, o8_send, o8,
    gath_a, gath_b, unpack, p_all, p_send, p_recv, p_sum, red,
    dma, sib_s, sib_r, sl_s, sl_r, z_s, z_r, ag_s, ag_r, red_s, red_r,
):
    g = lax.axis_index("grp")
    h = lax.axis_index("head")
    y, x = g // 4, g % 4
    z, c = h // 2, h % 2
    sib = (g, h + 1 - 2 * c)
    gath = (gath_a, gath_b)

    load_sl = pltpu.make_async_copy(slices.at[:, pl.ds(TOK * z, TOK), :], sl, dma.at[1])
    load_qv = pltpu.make_async_copy(queries, qv, dma.at[8])
    load_lv = pltpu.make_async_copy(latents, lv, dma.at[9])
    load_wk = pltpu.make_async_copy(w_key, wk, dma.at[0])
    load_kt = [pltpu.make_async_copy(cache.at[4 * c + i], kt.at[i], dma.at[2 + i]) for i in range(4)]
    load_wv = pltpu.make_async_copy(w_value, wv, dma.at[6])
    load_wo = pltpu.make_async_copy(w_out, wo.at[0:448], dma.at[7])
    load_qv.start()
    load_sl.start()
    load_wk.start()
    load_lv.start()
    load_kt[0].start()
    load_kt[1].start()
    load_wv.start()
    load_kt[2].start()
    load_kt[3].start()
    load_wo.start()

    barrier = pltpu.get_barrier_semaphore()
    for i in range(1, 16):
        pl.semaphore_signal(barrier, inc=1, device_id=((g + i) % 16, h), device_id_type=MESH)
    for i in range(1, 8):
        pl.semaphore_signal(barrier, inc=1, device_id=(g, (h + i) % 8), device_id_type=MESH)

    qf[...] = jnp.zeros_like(qf)
    lat[...] = jnp.zeros_like(lat)
    owners = [placement[0, i] for i in range(16)]
    owner_of_lane = lax.broadcasted_iota(jnp.int32, (8, 16 * TOK), 1) // TOK
    code = jnp.zeros((8, 16 * TOK), jnp.int32)
    for i in range(16):
        rank = jnp.int32(0)
        for j in range(i):
            rank = rank + jnp.where(owners[j] == owners[i], 1, 0)
        code = jnp.where(owner_of_lane == i, owners[i] * CAP + rank, code)

    wo[448:512, :] = jnp.zeros((64, 2048), BF16)
    to_row = lax.broadcasted_iota(jnp.int32, (256, 256), 0)
    from_row = lax.broadcasted_iota(jnp.int32, (256, 256), 1)
    for b in range(3):
        back = (to_row // 16 == from_row // 16) & (to_row % 16 == from_row % 16 - 12 + 4 * b) & (from_row % 16 >= 12)
        unpack[:, 256 * b : 256 * b + 256] = jnp.where(back, 1.0, 0.0).astype(BF16)

    slw[:, KV:WIDE] = jnp.ones((16 * TOK, WIDE - KV), BF16)
    at0 = lax.broadcasted_iota(jnp.int32, (16 * TOK, 16 * TOK), 0)
    at1 = lax.broadcasted_iota(jnp.int32, (16 * TOK, 16 * TOK), 1)
    chosen = (at0 % TOK == at1 % TOK) & ((at0 // TOK) * CAP + c == code[0:1, :])
    selector = jnp.where(chosen, 1.0, 0.0).astype(BF16)
    load_sl.wait()
    slw[:, 0 : KV + ROPE] = sl[...].reshape(16 * TOK, KV + ROPE)
    k_send[...] = nn(selector, slw[...]).astype(BF16).reshape(16, TOK, WIDE)

    load_qv.wait()
    load_lv.wait()
    for r in range(ROWS + 1):
        v = qv[r].astype(F32)
        qf[r, 0:STEPS, :] = v
        qf[r, PAD : PAD + STEPS, :] = v
        lat[r, 0:STEPS, :] = lv[r].astype(F32)

    pl.semaphore_wait(barrier, 22)

    slice_sends = []
    for i in range(1, 16):
        to = (g + i) % 16
        cp = remote(k_send.at[to], k8.at[c, pl.ds(TOK * g, TOK)], sl_s.at[i], sl_r.at[i], (to, h))
        cp.start()
        slice_sends.append(cp)
    k8[c, pl.ds(TOK * g, TOK), :] = k_send[g]

    load_wk.wait()
    row = lax.broadcasted_iota(jnp.int32, (72, 128), 0)
    lane = lax.broadcasted_iota(jnp.int32, (72, 128), 1)
    first = row % 8 < PAD
    low = lane < ROPE
    for quad in range(4):
        parts = []
        for p in (2 * quad, 2 * quad + 1):
            t = qf[:, :, 384 * p : 384 * p + 384].reshape(72, 384)
            t0, t1, t2 = t[:, 0:128], t[:, 128:256], t[:, 256:384]
            r1, r2 = pltpu.roll(t1, 64, 1), pltpu.roll(t2, 64, 1)
            second_nope = jnp.where(low, r1, r2)
            rope = jnp.where(low, jnp.where(first, t1, r2), 0.0)
            lhs = jnp.concatenate([jnp.where(first, t0, 0.0), jnp.where(first, 0.0, second_nope)], axis=1)
            absorbed = nn(lhs.astype(BF16), wk[2 * p : 2 * p + 2].reshape(2 * NOPE, KV))
            parts.append(jnp.concatenate([absorbed, rope], axis=1).reshape(9, 8, WIDE))
        q_all[:, 16 * quad : 16 * quad + 16, :] = jnp.concatenate(parts, axis=1).astype(BF16)

    ask_sib = remote(q_all.at[pl.ds(4 * (1 - c), 4)], q_sib, sib_s.at[0], sib_r.at[0], sib)
    ask_sib.start()
    ask_z = []
    for i in range(1, 4):
        to = (z + i) % 4
        cp = remote(q_all.at[8], q8.at[z], z_s.at[i], z_r.at[i], (g, 2 * to + c))
        cp.start()
        ask_z.append(cp)
    q8[z] = q_all[8]
    ask_sib.wait()

    recent_ok = step_mask(2 * ASK, 16)

    def resident(i):
        load_kt[i].wait()
        q = jnp.concatenate([q_all[4 * c + i], q_sib[i]], axis=0)[:, 0 : KV + ROPE]
        recent = lat[4 * c + i].astype(BF16)
        s = nn(q, kt[i])
        s_new = jnp.where(recent_ok, nt(q, recent), LOWEST)
        ok = lax.broadcasted_iota(jnp.int32, (1, LRES), 1) < lengths[0, 4 * c + i]
        s = jnp.where(ok, s, LOWEST)
        m = jnp.maximum(jnp.max(s, axis=1, keepdims=True), jnp.max(s_new, axis=1, keepdims=True))
        e = jnp.exp((s - m) * SCALE)
        e_new = jnp.exp((s_new - m) * SCALE)
        total = jnp.sum(e, axis=1, keepdims=True) + jnp.sum(e_new, axis=1, keepdims=True)
        o = nt(e.astype(BF16), kt[i, 0:KV, :]) + nn(e_new.astype(BF16), recent[:, 0:KV])
        o = (o / total).astype(BF16)
        at = (i // 2) * 4 + c * 2 + i % 2
        lt[at] = o[0:ASK]
        o_sib[i] = o[ASK:]
        cp = remote(o_sib.at[i], lt.at[at], sib_s.at[1 + i], sib_r.at[1 + i], sib)
        cp.start()
        return cp

    def values(part):
        lo, count = (0, 4) if part == 0 else (4, 5)
        rows = 16 * count
        head_of_row = lax.broadcasted_iota(jnp.int32, (rows, 512), 0) % 16 // PAD
        head_of_lane = lax.broadcasted_iota(jnp.int32, (rows, 512), 1) // VD
        mine = head_of_row == head_of_lane
        heads_out = []
        for quad in range(4):
            lhs = lt[lo : lo + count, 16 * quad : 16 * quad + 16, :].reshape(rows, KV)
            rhs = jnp.concatenate([wv[4 * quad + j] for j in range(4)], axis=1)
            heads_out.append(jnp.where(mine, nn(lhs, rhs), 0.0).astype(BF16))
        to_row = lax.broadcasted_iota(jnp.int32, (16, rows), 0)
        from_row = lax.broadcasted_iota(jnp.int32, (16, rows), 1)

        def picks(at):
            return (at // STEPS == from_row // 16) & (at % STEPS == from_row % PAD)

        blocks = []
        if part == 0:
            direct = jnp.where((to_row < 12) & picks(to_row), 1.0, 0.0).astype(BF16)
            for b in range(3):
                under = jnp.where((to_row >= 12) & picks(4 * b + to_row - 12), 1.0, 0.0).astype(BF16)
                blocks.append(nn(direct, heads_out[b]) + nn(under, heads_out[3]))
        else:
            direct = jnp.where((to_row < 15) & picks(to_row), 1.0, 0.0).astype(BF16)
            for b in range(4):
                blocks.append(nn(direct, heads_out[b]))
        block = jnp.concatenate(blocks, axis=1).astype(BF16)
        half = WIDTH[part]
        gath[part][0, 4 * y + x] = block[:, 0:half]
        gath[part][1, 4 * x + y] = block[:, half:]

    ag_sends = []

    def along(axis, d):
        if axis == 0:
            return (4 * y + (x + d) % 4, h)
        return ((y + d) % 4 * 4 + x, h)

    def blocks_of(part, k, ring, d):
        one, two = (x, y) if k == 0 else (y, x)
        if ring == 0:
            return gath[part].at[k, pl.ds(4 * two + (one - d) % 4, 1)]
        return gath[part].at[k, pl.ds(4 * ((two - d) % 4), 4)]

    def gather_send(part, ring):
        for k in (0, 1):
            ref = blocks_of(part, k, ring, 0)
            for d in (2, 1, 3):
                n = ((part * 2 + k) * 2 + ring) * 4 + d
                cp = remote(ref, ref, ag_s.at[n], ag_r.at[n], along(ring if k == 0 else 1 - ring, d))
                cp.start()
                ag_sends.append(cp)

    def gather_wait(part, ring):
        for k in (0, 1):
            for d in (1, 3, 2):
                n = ((part * 2 + k) * 2 + ring) * 4 + d
                ref = blocks_of(part, k, ring, d)
                remote(ref, ref, ag_s.at[n], ag_r.at[n], along(ring if k == 0 else 1 - ring, d)).wait_recv()

    def project(part):
        half = WIDTH[part]
        first_half = gath[part][0].reshape(256, half)
        second_half = jnp.concatenate([gath[part][1, 4 * (i % 4) + i // 4] for i in range(16)], axis=0)
        lhs = jnp.concatenate([first_half, second_half], axis=1)
        if part == 0:
            tall = jnp.concatenate([lhs[:, 512 * b : 512 * b + 512] for b in range(3)], axis=0)
            lhs = jnp.concatenate([lhs, nn(unpack[...], tall).astype(BF16)], axis=1)
        p_all[part] = nt(lhs, wo[...]).reshape(16, 16, 512)
        p_send[part] = p_all[part, pl.ds(8 * (1 - c), 8)].astype(BF16)
        cp = remote(p_send.at[part], p_recv.at[part], sib_s.at[6 + part], sib_r.at[6 + part], sib)
        cp.start()
        return cp

    def add_cores(part, cp):
        cp.wait()
        p_sum[part] = (p_all[part, pl.ds(8 * c, 8)] + p_recv[part].astype(F32)).astype(BF16)

    keeper = g // 2
    slot = (g % 2) * 4 + z

    def hand(part, i):
        return remote(
            p_sum.at[part, i], red.at[part, slot], red_s.at[8 * part + i], red_r.at[8 * part + slot],
            (8 * c + i, keeper),
        )

    def hand_out(part):
        for i in range(8):
            to = 8 * c + i

            @pl.when(jnp.logical_or(to != g, keeper != h))
            def _():
                hand(part, i).start()

            @pl.when(jnp.logical_and(to == g, keeper == h))
            def _():
                red[part, slot] = p_sum[part, i]

    def take_in(part):
        half_of = g // 8
        for j in range(2):
            for k in range(4):
                at = j * 4 + k

                @pl.when(jnp.logical_or(2 * h + j != g, 2 * k + half_of != h))
                def _():
                    remote(
                        p_sum.at[part, 0], red.at[part, at], red_s.at[0], red_r.at[8 * part + at], sib
                    ).wait_recv()

        sums = []
        for j in range(2):
            acc = red[part, 4 * j].astype(F32)
            for k in range(1, 4):
                acc = acc + red[part, 4 * j + k].astype(F32)
            sums.append(acc)
        shifted = pltpu.roll(sums[1], 64, 1)
        lane = lax.broadcasted_iota(jnp.int32, (16, 128), 1)
        middle = jnp.where(lane < 64, sums[0][:, 384:512], shifted[:, 0:128])
        mixed = jnp.concatenate([sums[0][:, 0:384], middle, shifted[:, 128:512]], axis=1)
        rows = (0, 1, 4, 5) if part == 0 else (2, 3, 6, 7, 8)
        for a, r in enumerate(rows):
            out[r] = mixed[STEPS * a : STEPS * a + STEPS].astype(BF16)

    lat_sends = [resident(0), resident(1)]
    for cp in lat_sends:
        cp.wait()
    load_wv.wait()
    values(0)
    gather_send(0, 0)

    for cp in slice_sends:
        cp.wait()
    keys_sib = remote(k8.at[c], k8.at[c], sib_s.at[5], sib_r.at[5], sib)
    keys_sib.start()
    lat_sends = [resident(2)]
    gather_wait(0, 0)
    gather_send(0, 1)

    for cp in ask_z:
        cp.wait()
    keys_sib.wait()
    keys = k8[...].reshape(2 * 16 * TOK, WIDE)
    q = q8[...].reshape(4 * ASK, WIDE)
    flag = (lax.broadcasted_iota(jnp.int32, (8, WIDE), 1) == KV + ROPE).astype(BF16)
    present = nt(flag, keys)[0:1] > 0.5
    s = jnp.where(present, nt(q, keys), LOWEST)
    m = jnp.max(s, axis=1, keepdims=True)
    e = jnp.exp((s - m) * SCALE)
    total = jnp.sum(e, axis=1, keepdims=True)
    o = nn(e.astype(BF16), keys[:, 0:KV])
    lane = lax.broadcasted_iota(jnp.int32, (4 * ASK, 128), 1)
    stats = jnp.zeros((4 * ASK, 128), F32)
    for n, rest in enumerate((m, total)):
        for t in range(3):
            piece = rest.astype(BF16).astype(F32)
            rest = rest - piece
            stats = jnp.where(lane == 3 * n + t, piece, stats)
    o8_send[...] = jnp.concatenate([o, stats], axis=1).astype(BF16).reshape(4, ASK, WIDE)
    part_z = []
    for i in range(1, 4):
        to = (z + i) % 4
        cp = remote(o8_send.at[to], o8.at[z], z_s.at[3 + i], z_r.at[3 + i], (g, 2 * to + c))
        cp.start()
        part_z.append(cp)
    o8[z] = o8_send[z]

    lat_sends.append(resident(3))

    q = q_all[8][:, 0 : KV + ROPE]
    recent = lat[8].astype(BF16)
    s_new = jnp.where(step_mask(ASK, 16), nt(q, recent), LOWEST)
    m_new = jnp.max(s_new, axis=1, keepdims=True)
    e_new = jnp.exp((s_new - m_new) * SCALE)
    total_new = jnp.sum(e_new, axis=1, keepdims=True)
    o_new = nn(e_new.astype(BF16), recent[:, 0:KV])
    for cp in part_z:
        cp.wait()
    m_part, total_part = [], []
    for i in range(4):
        st = o8[i][:, KV:WIDE].astype(F32)
        m_part.append(st[:, 0:1] + st[:, 1:2] + st[:, 2:3])
        total_part.append(st[:, 3:4] + st[:, 4:5] + st[:, 5:6])
    m = m_new
    for one in m_part:
        m = jnp.maximum(m, one)
    weight = jnp.exp((m_new - m) * SCALE)
    o = o_new * weight
    total = total_new * weight
    for i in range(4):
        weight = jnp.exp((m_part[i] - m) * SCALE)
        o = o + o8[i][:, 0:KV].astype(F32) * weight
        total = total + total_part[i] * weight
    lt[8] = (o / total).astype(BF16)
    for cp in lat_sends:
        cp.wait()
    values(1)
    gather_send(1, 0)

    load_wo.wait()
    gather_wait(0, 1)
    swap = project(0)
    gather_wait(1, 0)
    gather_send(1, 1)
    add_cores(0, swap)
    hand_out(0)
    take_in(0)
    gather_wait(1, 1)
    swap = project(1)
    add_cores(1, swap)
    hand_out(1)
    take_in(1)

    for part in (0, 1):
        for i in range(8):
            pl.when(jnp.logical_or(8 * c + i != g, keeper != h))(hand(part, i).wait_send)
    for cp in ag_sends:
        cp.wait_send()


def body(resident_cache, lengths, slices, placement, queries, latents, w_key, w_value, w_out):
    vmem = pl.BlockSpec(memory_space=pltpu.VMEM)
    smem = pl.BlockSpec(memory_space=pltpu.SMEM)
    anywhere = pl.BlockSpec(memory_space=pl.ANY)
    sems = pltpu.SemaphoreType.DMA
    out = pl.pallas_call(
        kernel,
        out_shape=jax.ShapeDtypeStruct((ROWS + 1, STEPS, 896), BF16),
        in_specs=[smem, smem] + [anywhere] * 7,
        out_specs=vmem,
        scratch_shapes=[
            pltpu.VMEM((4, KV + ROPE, LRES), BF16),
            pltpu.VMEM((HEADS, NOPE, KV), BF16),
            pltpu.VMEM((HEADS, KV, VD), BF16),
            pltpu.VMEM((512, HEADS * VD), BF16),
            pltpu.VMEM((16, TOK, KV + ROPE), BF16),
            pltpu.VMEM((16 * TOK, WIDE), BF16),
            pltpu.VMEM((16, TOK, WIDE), BF16),
            pltpu.VMEM((ROWS + 1, STEPS, HEADS * 192), BF16),
            pltpu.VMEM((ROWS + 1, STEPS, KV + ROPE), BF16),
            pltpu.VMEM((ROWS + 1, 8, HEADS * 192), F32),
            pltpu.VMEM((ROWS + 1, 16, KV + ROPE), F32),
            pltpu.VMEM((ROWS + 1, ASK, WIDE), BF16),
            pltpu.VMEM((4, ASK, WIDE), BF16),
            pltpu.VMEM((4, ASK, WIDE), BF16),
            pltpu.VMEM((2, 16 * TOK, WIDE), BF16),
            pltpu.VMEM((4, ASK, KV), BF16),
            pltpu.VMEM((ROWS + 1, ASK, KV), BF16),
            pltpu.VMEM((4, ASK, WIDE), BF16),
            pltpu.VMEM((4, ASK, WIDE), BF16),
            pltpu.VMEM((2, 16, 16, WIDTH[0]), BF16),
            pltpu.VMEM((2, 16, 16, WIDTH[1]), BF16),
            pltpu.VMEM((256, 768), BF16),
            pltpu.VMEM((2, 16, 16, 512), F32),
            pltpu.VMEM((2, 8, 16, 512), BF16),
            pltpu.VMEM((2, 8, 16, 512), BF16),
            pltpu.VMEM((2, 8, 16, 512), BF16),
            pltpu.VMEM((2, 8, 16, 512), BF16),
            sems((10,)),
            sems((8,)),
            sems((8,)),
            sems((16,)),
            sems((16,)),
            sems((7,)),
            sems((7,)),
            sems((32,)),
            sems((32,)),
            sems((16,)),
            sems((16,)),
        ],
        compiler_params=pltpu.CompilerParams(
            collective_id=0, has_side_effects=True, vmem_limit_bytes=56 * 1024 * 1024
        ),
        name="decode",
    )(
        lengths,
        placement.reshape(1, 16),
        jnp.swapaxes(queries[:, 0], 0, 1),
        jnp.swapaxes(latents[:, 0], 0, 1),
        jnp.swapaxes(resident_cache[0], 1, 2),
        slices,
        w_key,
        w_value,
        jnp.swapaxes(w_out, 0, 1),
    )
    return jnp.swapaxes(out, 0, 1)[:, None]


def solution(mesh):
    placed = (
        P("grp", None, None, None),
        P("grp", None),
        P("grp", None, None),
        P("grp", None),
        P(None, "grp", None, "head"),
        P(None, "grp", None, None),
        P("head", None, None),
        P("head", None, None),
        P("head", "grp"),
    )
    return jax.shard_map(
        body, mesh=mesh, in_specs=placed, out_specs=P(None, "grp", None, "head"), check_vma=False
    )
```

```python
import math

import jax
import jax.numpy as jnp
from jax import lax
from jax.experimental import pallas as pl
from jax.experimental.pallas import tpu as pltpu
from jax.sharding import PartitionSpec as P

KV = 512
ROPE = 64
NOPE = 128
VD = 128
ROWS = 8
LRES = 1536
SL = 64
CAP = 2
STEPS = 3

MESH = pl.DeviceIdType.MESH
SCALE = 1.0 / math.sqrt(NOPE + ROPE)
LOWEST = -3.0e38
BF16 = jnp.bfloat16
F32 = jnp.float32
WIDE = 640
PAD = 4
HEADS = 16
ASK = HEADS * PAD
WIDTH = (768, 1024)
TOK = 16


def remote(src, dst, send_sem, recv_sem, dev):
    return pltpu.make_async_remote_copy(
        src_ref=src, dst_ref=dst, send_sem=send_sem, recv_sem=recv_sem, device_id=dev, device_id_type=MESH
    )


def nt(a, b):
    return lax.dot_general(a, b, (((1,), (1,)), ((), ())), preferred_element_type=F32)


def nn(a, b):
    return jnp.dot(a, b, preferred_element_type=F32)


def step_mask(rows, width):
    step = lax.broadcasted_iota(jnp.int32, (rows, width), 0) % PAD
    at = lax.broadcasted_iota(jnp.int32, (rows, width), 1)
    return (at < STEPS) & (at <= step)


def kernel(
    lengths, placement, queries, latents, cache, slices, w_key, w_value, w_out,
    out,
    kt, wk, wv, wo, sl, slw, k_send, qv, lv, qf, lat,
    q_all, q_sib, q8, k8, o_sib, lt, o8_send, o8,
    gath_a, gath_b, unpack, p_all, p_send, p_recv, p_sum, red,
    dma, sib_s, sib_r, sl_s, sl_r, z_s, z_r, ag_s, ag_r, red_s, red_r,
):
    g = lax.axis_index("grp")
    h = lax.axis_index("head")
    y, x = g // 4, g % 4
    z, c = h // 2, h % 2
    sib = (g, h + 1 - 2 * c)
    gath = (gath_a, gath_b)

    load_sl = pltpu.make_async_copy(slices.at[:, pl.ds(TOK * z, TOK), :], sl, dma.at[1])
    load_qv = pltpu.make_async_copy(queries, qv, dma.at[8])
    load_lv = pltpu.make_async_copy(latents, lv, dma.at[9])
    load_wk = pltpu.make_async_copy(w_key, wk, dma.at[0])
    load_kt = [pltpu.make_async_copy(cache.at[4 * c + i], kt.at[i], dma.at[2 + i]) for i in range(4)]
    load_wv = pltpu.make_async_copy(w_value, wv, dma.at[6])
    load_wo = pltpu.make_async_copy(w_out, wo.at[0:448], dma.at[7])
    load_qv.start()
    load_wk.start()
    load_lv.start()
    load_kt[0].start()
    load_sl.start()

    barrier = pltpu.get_barrier_semaphore()
    for i in range(1, 16):
        pl.semaphore_signal(barrier, inc=1, device_id=((g + i) % 16, h), device_id_type=MESH)
    for i in range(1, 8):
        pl.semaphore_signal(barrier, inc=1, device_id=(g, (h + i) % 8), device_id_type=MESH)

    qf[...] = jnp.zeros_like(qf)
    lat[...] = jnp.zeros_like(lat)
    load_qv.wait()
    load_lv.wait()
    for r in range(ROWS + 1):
        v = qv[r].astype(F32)
        qf[r, 0:STEPS, :] = v
        qf[r, PAD : PAD + STEPS, :] = v
        lat[r, 0:STEPS, :] = lv[r].astype(F32)

    load_wk.wait()
    load_kt[1].start()
    load_wv.start()
    row = lax.broadcasted_iota(jnp.int32, (72, 128), 0)
    lane = lax.broadcasted_iota(jnp.int32, (72, 128), 1)
    first = row % 8 < PAD
    low = lane < ROPE
    for quad in range(4):
        parts = []
        for p in (2 * quad, 2 * quad + 1):
            t = qf[:, :, 384 * p : 384 * p + 384].reshape(72, 384)
            t0, t1, t2 = t[:, 0:128], t[:, 128:256], t[:, 256:384]
            r1, r2 = pltpu.roll(t1, 64, 1), pltpu.roll(t2, 64, 1)
            second_nope = jnp.where(low, r1, r2)
            rope = jnp.where(low, jnp.where(first, t1, r2), 0.0)
            lhs = jnp.concatenate([jnp.where(first, t0, 0.0), jnp.where(first, 0.0, second_nope)], axis=1)
            absorbed = nn(lhs.astype(BF16), wk[2 * p : 2 * p + 2].reshape(2 * NOPE, KV))
            parts.append(jnp.concatenate([absorbed, rope], axis=1).reshape(9, 8, WIDE))
        q_all[:, 16 * quad : 16 * quad + 16, :] = jnp.concatenate(parts, axis=1).astype(BF16)

    pl.semaphore_wait(barrier, 22)

    ask_sib = remote(q_all.at[pl.ds(4 * (1 - c), 4)], q_sib, sib_s.at[0], sib_r.at[0], sib)
    ask_sib.start()
    ask_z = []
    for i in range(1, 4):
        to = (z + i) % 4
        cp = remote(q_all.at[8], q8.at[z], z_s.at[i], z_r.at[i], (g, 2 * to + c))
        cp.start()
        ask_z.append(cp)
    q8[z] = q_all[8]

    owners = [placement[0, i] for i in range(16)]
    owner_of_lane = lax.broadcasted_iota(jnp.int32, (8, 16 * TOK), 1) // TOK
    code = jnp.zeros((8, 16 * TOK), jnp.int32)
    for i in range(16):
        rank = jnp.int32(0)
        for j in range(i):
            rank = rank + jnp.where(owners[j] == owners[i], 1, 0)
        code = jnp.where(owner_of_lane == i, owners[i] * CAP + rank, code)

    wo[448:512, :] = jnp.zeros((64, 2048), BF16)
    to_row = lax.broadcasted_iota(jnp.int32, (256, 256), 0)
    from_row = lax.broadcasted_iota(jnp.int32, (256, 256), 1)
    for b in range(3):
        back = (to_row // 16 == from_row // 16) & (to_row % 16 == from_row % 16 - 12 + 4 * b) & (from_row % 16 >= 12)
        unpack[:, 256 * b : 256 * b + 256] = jnp.where(back, 1.0, 0.0).astype(BF16)

    slw[:, KV:WIDE] = jnp.ones((16 * TOK, WIDE - KV), BF16)
    at0 = lax.broadcasted_iota(jnp.int32, (16 * TOK, 16 * TOK), 0)
    at1 = lax.broadcasted_iota(jnp.int32, (16 * TOK, 16 * TOK), 1)
    chosen = (at0 % TOK == at1 % TOK) & ((at0 // TOK) * CAP + c == code[0:1, :])
    selector = jnp.where(chosen, 1.0, 0.0).astype(BF16)
    load_sl.wait()
    slw[:, 0 : KV + ROPE] = sl[...].reshape(16 * TOK, KV + ROPE)
    k_send[...] = nn(selector, slw[...]).astype(BF16).reshape(16, TOK, WIDE)

    slice_sends = []
    for i in range(1, 16):
        to = (g + i) % 16
        cp = remote(k_send.at[to], k8.at[c, pl.ds(TOK * g, TOK)], sl_s.at[i], sl_r.at[i], (to, h))
        cp.start()
        slice_sends.append(cp)
    k8[c, pl.ds(TOK * g, TOK), :] = k_send[g]

    ask_sib.wait()

    recent_ok = step_mask(2 * ASK, 16)

    def resident(i):
        load_kt[i].wait()
        if i == 0:
            load_kt[2].start()
        if i == 1:
            load_kt[3].start()
            load_wo.start()
        q = jnp.concatenate([q_all[4 * c + i], q_sib[i]], axis=0)[:, 0 : KV + ROPE]
        recent = lat[4 * c + i].astype(BF16)
        s = nn(q, kt[i])
        s_new = jnp.where(recent_ok, nt(q, recent), LOWEST)
        ok = lax.broadcasted_iota(jnp.int32, (1, LRES), 1) < lengths[0, 4 * c + i]
        s = jnp.where(ok, s, LOWEST)
        m = jnp.maximum(jnp.max(s, axis=1, keepdims=True), jnp.max(s_new, axis=1, keepdims=True))
        e = jnp.exp((s - m) * SCALE)
        e_new = jnp.exp((s_new - m) * SCALE)
        total = jnp.sum(e, axis=1, keepdims=True) + jnp.sum(e_new, axis=1, keepdims=True)
        o = nt(e.astype(BF16), kt[i, 0:KV, :]) + nn(e_new.astype(BF16), recent[:, 0:KV])
        o = (o / total).astype(BF16)
        at = (i // 2) * 4 + c * 2 + i % 2
        lt[at] = o[0:ASK]
        o_sib[i] = o[ASK:]
        cp = remote(o_sib.at[i], lt.at[at], sib_s.at[1 + i], sib_r.at[1 + i], sib)
        cp.start()
        return cp

    def values(part):
        lo, count = (0, 4) if part == 0 else (4, 5)
        rows = 16 * count
        head_of_row = lax.broadcasted_iota(jnp.int32, (rows, 512), 0) % 16 // PAD
        head_of_lane = lax.broadcasted_iota(jnp.int32, (rows, 512), 1) // VD
        mine = head_of_row == head_of_lane
        heads_out = []
        for quad in range(4):
            lhs = lt[lo : lo + count, 16 * quad : 16 * quad + 16, :].reshape(rows, KV)
            rhs = jnp.concatenate([wv[4 * quad + j] for j in range(4)], axis=1)
            heads_out.append(jnp.where(mine, nn(lhs, rhs), 0.0).astype(BF16))
        to_row = lax.broadcasted_iota(jnp.int32, (16, rows), 0)
        from_row = lax.broadcasted_iota(jnp.int32, (16, rows), 1)

        def picks(at):
            return (at // STEPS == from_row // 16) & (at % STEPS == from_row % PAD)

        blocks = []
        if part == 0:
            direct = jnp.where((to_row < 12) & picks(to_row), 1.0, 0.0).astype(BF16)
            for b in range(3):
                under = jnp.where((to_row >= 12) & picks(4 * b + to_row - 12), 1.0, 0.0).astype(BF16)
                blocks.append(nn(direct, heads_out[b]) + nn(under, heads_out[3]))
        else:
            direct = jnp.where((to_row < 15) & picks(to_row), 1.0, 0.0).astype(BF16)
            for b in range(4):
                blocks.append(nn(direct, heads_out[b]))
        block = jnp.concatenate(blocks, axis=1).astype(BF16)
        half = WIDTH[part]
        gath[part][0, 4 * y + x] = block[:, 0:half]
        gath[part][1, 4 * x + y] = block[:, half:]

    ag_sends = []

    def along(axis, d):
        if axis == 0:
            return (4 * y + (x + d) % 4, h)
        return ((y + d) % 4 * 4 + x, h)

    def blocks_of(part, k, ring, d):
        one, two = (x, y) if k == 0 else (y, x)
        if ring == 0:
            return gath[part].at[k, pl.ds(4 * two + (one - d) % 4, 1)]
        return gath[part].at[k, pl.ds(4 * ((two - d) % 4), 4)]

    def gather_send(part, ring):
        for k in (0, 1):
            ref = blocks_of(part, k, ring, 0)
            for d in (2, 1, 3):
                n = ((part * 2 + k) * 2 + ring) * 4 + d
                cp = remote(ref, ref, ag_s.at[n], ag_r.at[n], along(ring if k == 0 else 1 - ring, d))
                cp.start()
                ag_sends.append(cp)

    def gather_wait(part, ring):
        for k in (0, 1):
            for d in (1, 3, 2):
                n = ((part * 2 + k) * 2 + ring) * 4 + d
                ref = blocks_of(part, k, ring, d)
                remote(ref, ref, ag_s.at[n], ag_r.at[n], along(ring if k == 0 else 1 - ring, d)).wait_recv()

    def project(part):
        half = WIDTH[part]
        first_half = gath[part][0].reshape(256, half)
        second_half = jnp.concatenate([gath[part][1, 4 * (i % 4) + i // 4] for i in range(16)], axis=0)
        lhs = jnp.concatenate([first_half, second_half], axis=1)
        if part == 0:
            tall = jnp.concatenate([lhs[:, 512 * b : 512 * b + 512] for b in range(3)], axis=0)
            lhs = jnp.concatenate([lhs, nn(unpack[...], tall).astype(BF16)], axis=1)
        p_all[part] = nt(lhs, wo[...]).reshape(16, 16, 512)
        p_send[part] = p_all[part, pl.ds(8 * (1 - c), 8)].astype(BF16)
        cp = remote(p_send.at[part], p_recv.at[part], sib_s.at[6 + part], sib_r.at[6 + part], sib)
        cp.start()
        return cp

    def add_cores(part, cp):
        cp.wait()
        p_sum[part] = (p_all[part, pl.ds(8 * c, 8)] + p_recv[part].astype(F32)).astype(BF16)

    keeper = g // 2
    slot = (g % 2) * 4 + z

    def hand(part, i):
        return remote(
            p_sum.at[part, i], red.at[part, slot], red_s.at[8 * part + i], red_r.at[8 * part + slot],
            (8 * c + i, keeper),
        )

    def hand_out(part):
        for i in range(8):
            to = 8 * c + i

            @pl.when(jnp.logical_or(to != g, keeper != h))
            def _():
                hand(part, i).start()

            @pl.when(jnp.logical_and(to == g, keeper == h))
            def _():
                red[part, slot] = p_sum[part, i]

    def take_in(part):
        half_of = g // 8
        for j in range(2):
            for k in range(4):
                at = j * 4 + k

                @pl.when(jnp.logical_or(2 * h + j != g, 2 * k + half_of != h))
                def _():
                    remote(
                        p_sum.at[part, 0], red.at[part, at], red_s.at[0], red_r.at[8 * part + at], sib
                    ).wait_recv()

        sums = []
        for j in range(2):
            acc = red[part, 4 * j].astype(F32)
            for k in range(1, 4):
                acc = acc + red[part, 4 * j + k].astype(F32)
            sums.append(acc)
        shifted = pltpu.roll(sums[1], 64, 1)
        lane = lax.broadcasted_iota(jnp.int32, (16, 128), 1)
        middle = jnp.where(lane < 64, sums[0][:, 384:512], shifted[:, 0:128])
        mixed = jnp.concatenate([sums[0][:, 0:384], middle, shifted[:, 128:512]], axis=1)
        return mixed.astype(BF16)

    lat_sends = [resident(0), resident(1)]
    for cp in lat_sends:
        cp.wait()
    load_wv.wait()
    values(0)
    gather_send(0, 0)

    for cp in slice_sends:
        cp.wait()
    keys_sib = remote(k8.at[c], k8.at[c], sib_s.at[5], sib_r.at[5], sib)
    keys_sib.start()
    lat_sends = [resident(2)]
    gather_wait(0, 0)
    gather_send(0, 1)

    for cp in ask_z:
        cp.wait()
    keys_sib.wait()
    keys = k8[...].reshape(2 * 16 * TOK, WIDE)
    q = q8[...].reshape(4 * ASK, WIDE)
    flag = (lax.broadcasted_iota(jnp.int32, (8, WIDE), 1) == KV + ROPE).astype(BF16)
    present = nt(flag, keys)[0:1] > 0.5
    s = jnp.where(present, nt(q, keys), LOWEST)
    m = jnp.max(s, axis=1, keepdims=True)
    e = jnp.exp((s - m) * SCALE)
    total = jnp.sum(e, axis=1, keepdims=True)
    o = nn(e.astype(BF16), keys[:, 0:KV])
    lane = lax.broadcasted_iota(jnp.int32, (4 * ASK, 128), 1)
    stats = jnp.zeros((4 * ASK, 128), F32)
    for n, rest in enumerate((m, total)):
        for t in range(3):
            piece = rest.astype(BF16).astype(F32)
            rest = rest - piece
            stats = jnp.where(lane == 3 * n + t, piece, stats)
    o8_send[...] = jnp.concatenate([o, stats], axis=1).astype(BF16).reshape(4, ASK, WIDE)
    part_z = []
    for i in range(1, 4):
        to = (z + i) % 4
        cp = remote(o8_send.at[to], o8.at[z], z_s.at[3 + i], z_r.at[3 + i], (g, 2 * to + c))
        cp.start()
        part_z.append(cp)
    o8[z] = o8_send[z]

    lat_sends.append(resident(3))

    q = q_all[8][:, 0 : KV + ROPE]
    recent = lat[8].astype(BF16)
    s_new = jnp.where(step_mask(ASK, 16), nt(q, recent), LOWEST)
    m_new = jnp.max(s_new, axis=1, keepdims=True)
    e_new = jnp.exp((s_new - m_new) * SCALE)
    total_new = jnp.sum(e_new, axis=1, keepdims=True)
    o_new = nn(e_new.astype(BF16), recent[:, 0:KV])
    for cp in part_z:
        cp.wait()
    m_part, total_part = [], []
    for i in range(4):
        st = o8[i][:, KV:WIDE].astype(F32)
        m_part.append(st[:, 0:1] + st[:, 1:2] + st[:, 2:3])
        total_part.append(st[:, 3:4] + st[:, 4:5] + st[:, 5:6])
    m = m_new
    for one in m_part:
        m = jnp.maximum(m, one)
    weight = jnp.exp((m_new - m) * SCALE)
    o = o_new * weight
    total = total_new * weight
    for i in range(4):
        weight = jnp.exp((m_part[i] - m) * SCALE)
        o = o + o8[i][:, 0:KV].astype(F32) * weight
        total = total + total_part[i] * weight
    lt[8] = (o / total).astype(BF16)
    for cp in lat_sends:
        cp.wait()
    values(1)
    gather_send(1, 0)
    gather_wait(1, 0)
    gather_send(1, 1)

    load_wo.wait()
    gather_wait(0, 1)
    swap = project(0)
    add_cores(0, swap)
    hand_out(0)
    gather_wait(1, 1)
    swap = project(1)
    sums_a = take_in(0)
    add_cores(1, swap)
    hand_out(1)
    sums_b = take_in(1)

    to_row = lax.broadcasted_iota(jnp.int32, (32, 32), 0)
    from_row = lax.broadcasted_iota(jnp.int32, (32, 32), 1)
    r = to_row // STEPS
    source = jnp.where(r >= ROWS, 16 + 4 * STEPS, r // 2 % 2 * 16 + (r // 4 * 2 + r % 2) * STEPS) + to_row % STEPS
    order = jnp.where(source == from_row, 1.0, 0.0).astype(BF16)
    out[...] = nn(order, jnp.concatenate([sums_a, sums_b], axis=0)).astype(BF16)

    for part in (0, 1):
        for i in range(8):
            pl.when(jnp.logical_or(8 * c + i != g, keeper != h))(hand(part, i).wait_send)
    for cp in ag_sends:
        cp.wait_send()


def body(resident_cache, lengths, slices, placement, queries, latents, w_key, w_value, w_out):
    vmem = pl.BlockSpec(memory_space=pltpu.VMEM)
    smem = pl.BlockSpec(memory_space=pltpu.SMEM)
    anywhere = pl.BlockSpec(memory_space=pl.ANY)
    sems = pltpu.SemaphoreType.DMA
    out = pl.pallas_call(
        kernel,
        out_shape=jax.ShapeDtypeStruct((32, 896), BF16),
        in_specs=[smem, smem] + [anywhere] * 7,
        out_specs=vmem,
        scratch_shapes=[
            pltpu.VMEM((4, KV + ROPE, LRES), BF16),
            pltpu.VMEM((HEADS, NOPE, KV), BF16),
            pltpu.VMEM((HEADS, KV, VD), BF16),
            pltpu.VMEM((512, HEADS * VD), BF16),
            pltpu.VMEM((16, TOK, KV + ROPE), BF16),
            pltpu.VMEM((16 * TOK, WIDE), BF16),
            pltpu.VMEM((16, TOK, WIDE), BF16),
            pltpu.VMEM((ROWS + 1, STEPS, HEADS * 192), BF16),
            pltpu.VMEM((ROWS + 1, STEPS, KV + ROPE), BF16),
            pltpu.VMEM((ROWS + 1, 8, HEADS * 192), F32),
            pltpu.VMEM((ROWS + 1, 16, KV + ROPE), F32),
            pltpu.VMEM((ROWS + 1, ASK, WIDE), BF16),
            pltpu.VMEM((4, ASK, WIDE), BF16),
            pltpu.VMEM((4, ASK, WIDE), BF16),
            pltpu.VMEM((2, 16 * TOK, WIDE), BF16),
            pltpu.VMEM((4, ASK, KV), BF16),
            pltpu.VMEM((ROWS + 1, ASK, KV), BF16),
            pltpu.VMEM((4, ASK, WIDE), BF16),
            pltpu.VMEM((4, ASK, WIDE), BF16),
            pltpu.VMEM((2, 16, 16, WIDTH[0]), BF16),
            pltpu.VMEM((2, 16, 16, WIDTH[1]), BF16),
            pltpu.VMEM((256, 768), BF16),
            pltpu.VMEM((2, 16, 16, 512), F32),
            pltpu.VMEM((2, 8, 16, 512), BF16),
            pltpu.VMEM((2, 8, 16, 512), BF16),
            pltpu.VMEM((2, 8, 16, 512), BF16),
            pltpu.VMEM((2, 8, 16, 512), BF16),
            sems((10,)),
            sems((8,)),
            sems((8,)),
            sems((16,)),
            sems((16,)),
            sems((7,)),
            sems((7,)),
            sems((32,)),
            sems((32,)),
            sems((16,)),
            sems((16,)),
        ],
        compiler_params=pltpu.CompilerParams(
            collective_id=0, has_side_effects=True, vmem_limit_bytes=56 * 1024 * 1024
        ),
        name="decode",
    )(
        lengths,
        placement.reshape(1, 16),
        jnp.swapaxes(queries[:, 0], 0, 1),
        jnp.swapaxes(latents[:, 0], 0, 1),
        jnp.swapaxes(resident_cache[0], 1, 2),
        slices,
        w_key,
        w_value,
        jnp.swapaxes(w_out, 0, 1),
    )
    mixed = out[: STEPS * (ROWS + 1)].reshape(ROWS + 1, STEPS, 896)
    return jnp.swapaxes(mixed, 0, 1)[:, None]


def solution(mesh):
    placed = (
        P("grp", None, None, None),
        P("grp", None),
        P("grp", None, None),
        P("grp", None),
        P(None, "grp", None, "head"),
        P(None, "grp", None, None),
        P("head", None, None),
        P("head", None, None),
        P("head", "grp"),
    )
    return jax.shard_map(
        body, mesh=mesh, in_specs=placed, out_specs=P(None, "grp", None, "head"), check_vma=False
    )
```

```python
import math

import jax
import jax.numpy as jnp
from jax import lax
from jax.experimental import pallas as pl
from jax.experimental.pallas import tpu as pltpu
from jax.sharding import PartitionSpec as P

KV = 512
ROPE = 64
NOPE = 128
VD = 128
ROWS = 8
LRES = 1536
SL = 64
CAP = 2
STEPS = 3

MESH = pl.DeviceIdType.MESH
SCALE = 1.0 / math.sqrt(NOPE + ROPE)
LOWEST = -3.0e38
BF16 = jnp.bfloat16
F32 = jnp.float32
WIDE = 640
PAD = 4
HEADS = 16
ASK = HEADS * PAD
WIDTH = (768, 1024)
TOK = 16


def remote(src, dst, send_sem, recv_sem, dev):
    return pltpu.make_async_remote_copy(
        src_ref=src, dst_ref=dst, send_sem=send_sem, recv_sem=recv_sem, device_id=dev, device_id_type=MESH
    )


def nt(a, b):
    return lax.dot_general(a, b, (((1,), (1,)), ((), ())), preferred_element_type=F32)


def nn(a, b):
    return jnp.dot(a, b, preferred_element_type=F32)


def step_mask(rows, width):
    step = lax.broadcasted_iota(jnp.int32, (rows, width), 0) % PAD
    at = lax.broadcasted_iota(jnp.int32, (rows, width), 1)
    return (at < STEPS) & (at <= step)


def kernel(
    lengths, placement, queries, latents, cache, slices, w_key, w_value, w_out,
    out,
    kt, wk, wv, wo, sl, slw, k_send, qv, lv, qf, lat,
    q_all, q_sib, q8, k8, o_sib, lt, o8_send, o8,
    gath_a, gath_b, unpack, p_all, p_send, p_recv, p_sum, red,
    dma, sib_s, sib_r, sl_s, sl_r, z_s, z_r, ag_s, ag_r, red_s, red_r,
):
    g = lax.axis_index("grp")
    h = lax.axis_index("head")
    y, x = g // 4, g % 4
    z, c = h // 2, h % 2
    sib = (g, h + 1 - 2 * c)
    gath = (gath_a, gath_b)

    load_sl = pltpu.make_async_copy(slices.at[:, pl.ds(TOK * z, TOK), :], sl, dma.at[1])
    load_qv = pltpu.make_async_copy(queries, qv, dma.at[8])
    load_lv = pltpu.make_async_copy(latents, lv, dma.at[9])
    load_wk = pltpu.make_async_copy(w_key, wk, dma.at[0])
    load_kt = [pltpu.make_async_copy(cache.at[4 * c + i], kt.at[i], dma.at[2 + i]) for i in range(4)]
    load_wv = pltpu.make_async_copy(w_value, wv, dma.at[6])
    load_wo = pltpu.make_async_copy(w_out, wo.at[0:448], dma.at[7])
    load_sl.start()
    load_qv.start()
    load_lv.start()
    load_wk.start()
    load_kt[0].start()

    barrier = pltpu.get_barrier_semaphore()
    for i in range(1, 16):
        pl.semaphore_signal(barrier, inc=1, device_id=((g + i) % 16, h), device_id_type=MESH)
    for i in range(1, 8):
        pl.semaphore_signal(barrier, inc=1, device_id=(g, (h + i) % 8), device_id_type=MESH)

    owners = [placement[0, i] for i in range(16)]
    owner_of_lane = lax.broadcasted_iota(jnp.int32, (8, 16 * TOK), 1) // TOK
    code = jnp.zeros((8, 16 * TOK), jnp.int32)
    for i in range(16):
        rank = jnp.int32(0)
        for j in range(i):
            rank = rank + jnp.where(owners[j] == owners[i], 1, 0)
        code = jnp.where(owner_of_lane == i, owners[i] * CAP + rank, code)

    slw[:, KV:WIDE] = jnp.ones((16 * TOK, WIDE - KV), BF16)
    at0 = lax.broadcasted_iota(jnp.int32, (16 * TOK, 16 * TOK), 0)
    at1 = lax.broadcasted_iota(jnp.int32, (16 * TOK, 16 * TOK), 1)
    chosen = (at0 % TOK == at1 % TOK) & ((at0 // TOK) * CAP + c == code[0:1, :])
    selector = jnp.where(chosen, 1.0, 0.0).astype(BF16)
    load_sl.wait()
    slw[:, 0 : KV + ROPE] = sl[...].reshape(16 * TOK, KV + ROPE)
    k_send[...] = nn(selector, slw[...]).astype(BF16).reshape(16, TOK, WIDE)

    pl.semaphore_wait(barrier, 22)

    slice_sends = []
    for i in range(1, 16):
        to = (g + i) % 16
        cp = remote(k_send.at[to], k8.at[c, pl.ds(TOK * g, TOK)], sl_s.at[i], sl_r.at[i], (to, h))
        cp.start()
        slice_sends.append(cp)
    k8[c, pl.ds(TOK * g, TOK), :] = k_send[g]

    qf[...] = jnp.zeros_like(qf)
    lat[...] = jnp.zeros_like(lat)
    load_qv.wait()
    load_lv.wait()
    for r in range(ROWS + 1):
        v = qv[r].astype(F32)
        qf[r, 0:STEPS, :] = v
        qf[r, PAD : PAD + STEPS, :] = v
        lat[r, 0:STEPS, :] = lv[r].astype(F32)

    load_wk.wait()
    load_kt[1].start()
    load_wv.start()
    row = lax.broadcasted_iota(jnp.int32, (72, 128), 0)
    lane = lax.broadcasted_iota(jnp.int32, (72, 128), 1)
    first = row % 8 < PAD
    low = lane < ROPE
    for quad in range(4):
        parts = []
        for p in (2 * quad, 2 * quad + 1):
            t = qf[:, :, 384 * p : 384 * p + 384].reshape(72, 384)
            t0, t1, t2 = t[:, 0:128], t[:, 128:256], t[:, 256:384]
            r1, r2 = pltpu.roll(t1, 64, 1), pltpu.roll(t2, 64, 1)
            second_nope = jnp.where(low, r1, r2)
            rope = jnp.where(low, jnp.where(first, t1, r2), 0.0)
            lhs = jnp.concatenate([jnp.where(first, t0, 0.0), jnp.where(first, 0.0, second_nope)], axis=1)
            absorbed = nn(lhs.astype(BF16), wk[2 * p : 2 * p + 2].reshape(2 * NOPE, KV))
            parts.append(jnp.concatenate([absorbed, rope], axis=1).reshape(9, 8, WIDE))
        q_all[:, 16 * quad : 16 * quad + 16, :] = jnp.concatenate(parts, axis=1).astype(BF16)

    ask_sib = remote(q_all.at[pl.ds(4 * (1 - c), 4)], q_sib, sib_s.at[0], sib_r.at[0], sib)
    ask_sib.start()
    ask_z = []
    for i in range(1, 4):
        to = (z + i) % 4
        cp = remote(q_all.at[8], q8.at[z], z_s.at[i], z_r.at[i], (g, 2 * to + c))
        cp.start()
        ask_z.append(cp)
    q8[z] = q_all[8]

    wo[448:512, :] = jnp.zeros((64, 2048), BF16)
    to_row = lax.broadcasted_iota(jnp.int32, (256, 256), 0)
    from_row = lax.broadcasted_iota(jnp.int32, (256, 256), 1)
    for b in range(3):
        back = (to_row // 16 == from_row // 16) & (to_row % 16 == from_row % 16 - 12 + 4 * b) & (from_row % 16 >= 12)
        unpack[:, 256 * b : 256 * b + 256] = jnp.where(back, 1.0, 0.0).astype(BF16)

    ask_sib.wait()

    recent_ok = step_mask(2 * ASK, 16)

    def resident(i):
        load_kt[i].wait()
        if i == 0:
            load_kt[2].start()
        if i == 1:
            load_kt[3].start()
            load_wo.start()
        q = jnp.concatenate([q_all[4 * c + i], q_sib[i]], axis=0)[:, 0 : KV + ROPE]
        recent = lat[4 * c + i].astype(BF16)
        s = nn(q, kt[i])
        s_new = jnp.where(recent_ok, nt(q, recent), LOWEST)
        ok = lax.broadcasted_iota(jnp.int32, (1, LRES), 1) < lengths[0, 4 * c + i]
        s = jnp.where(ok, s, LOWEST)
        m = jnp.maximum(jnp.max(s, axis=1, keepdims=True), jnp.max(s_new, axis=1, keepdims=True))
        e = jnp.exp((s - m) * SCALE)
        e_new = jnp.exp((s_new - m) * SCALE)
        total = jnp.sum(e, axis=1, keepdims=True) + jnp.sum(e_new, axis=1, keepdims=True)
        o = nt(e.astype(BF16), kt[i, 0:KV, :]) + nn(e_new.astype(BF16), recent[:, 0:KV])
        o = (o / total).astype(BF16)
        at = (i // 2) * 4 + c * 2 + i % 2
        lt[at] = o[0:ASK]
        o_sib[i] = o[ASK:]
        cp = remote(o_sib.at[i], lt.at[at], sib_s.at[1 + i], sib_r.at[1 + i], sib)
        cp.start()
        return cp

    def values(part):
        lo, count = (0, 4) if part == 0 else (4, 5)
        rows = 16 * count
        head_of_row = lax.broadcasted_iota(jnp.int32, (rows, 512), 0) % 16 // PAD
        head_of_lane = lax.broadcasted_iota(jnp.int32, (rows, 512), 1) // VD
        mine = head_of_row == head_of_lane
        heads_out = []
        for quad in range(4):
            lhs = lt[lo : lo + count, 16 * quad : 16 * quad + 16, :].reshape(rows, KV)
            rhs = jnp.concatenate([wv[4 * quad + j] for j in range(4)], axis=1)
            heads_out.append(jnp.where(mine, nn(lhs, rhs), 0.0).astype(BF16))
        to_row = lax.broadcasted_iota(jnp.int32, (16, rows), 0)
        from_row = lax.broadcasted_iota(jnp.int32, (16, rows), 1)

        def picks(at):
            return (at // STEPS == from_row // 16) & (at % STEPS == from_row % PAD)

        blocks = []
        if part == 0:
            direct = jnp.where((to_row < 12) & picks(to_row), 1.0, 0.0).astype(BF16)
            for b in range(3):
                under = jnp.where((to_row >= 12) & picks(4 * b + to_row - 12), 1.0, 0.0).astype(BF16)
                blocks.append(nn(direct, heads_out[b]) + nn(under, heads_out[3]))
        else:
            direct = jnp.where((to_row < 15) & picks(to_row), 1.0, 0.0).astype(BF16)
            for b in range(4):
                blocks.append(nn(direct, heads_out[b]))
        block = jnp.concatenate(blocks, axis=1).astype(BF16)
        half = WIDTH[part]
        gath[part][0, 4 * y + x] = block[:, 0:half]
        gath[part][1, 4 * x + y] = block[:, half:]

    ag_sends = []

    def along(axis, d):
        if axis == 0:
            return (4 * y + (x + d) % 4, h)
        return ((y + d) % 4 * 4 + x, h)

    def blocks_of(part, k, ring, d):
        one, two = (x, y) if k == 0 else (y, x)
        if ring == 0:
            return gath[part].at[k, pl.ds(4 * two + (one - d) % 4, 1)]
        return gath[part].at[k, pl.ds(4 * ((two - d) % 4), 4)]

    def gather_send(part, ring):
        for k in (0, 1):
            ref = blocks_of(part, k, ring, 0)
            for d in (2, 1, 3):
                n = ((part * 2 + k) * 2 + ring) * 4 + d
                cp = remote(ref, ref, ag_s.at[n], ag_r.at[n], along(ring if k == 0 else 1 - ring, d))
                cp.start()
                ag_sends.append(cp)

    def gather_wait(part, ring):
        for k in (0, 1):
            for d in (1, 3, 2):
                n = ((part * 2 + k) * 2 + ring) * 4 + d
                ref = blocks_of(part, k, ring, d)
                remote(ref, ref, ag_s.at[n], ag_r.at[n], along(ring if k == 0 else 1 - ring, d)).wait_recv()

    def one_block(part, k, d1, d2):
        one, two = (x, y) if k == 0 else (y, x)
        return gath[part].at[k, pl.ds(4 * ((two - d2) % 4) + (one - d1) % 4, 1)]

    def pass_on(part, k, d1):
        ref = one_block(part, k, d1, 0)
        for d in (2, 1, 3):
            n = 32 + (k * 4 + d1) * 4 + d
            cp = remote(ref, ref, ag_s.at[n], ag_r.at[n], along(1 - k, d))
            cp.start()
            ag_sends.append(cp)

    def gather_blocks(part):
        for d in (1, 3, 2):
            for k in (0, 1):
                n = ((part * 2 + k) * 2) * 4 + d
                ref = blocks_of(part, k, 0, d)
                remote(ref, ref, ag_s.at[n], ag_r.at[n], along(k, d)).wait_recv()
                pass_on(part, k, d)

    def gather_last(part):
        for k in (0, 1):
            for d1 in (0, 1, 3, 2):
                for d2 in (1, 3, 2):
                    n = 32 + (k * 4 + d1) * 4 + d2
                    ref = one_block(part, k, d1, d2)
                    remote(ref, ref, ag_s.at[n], ag_r.at[n], along(1 - k, d2)).wait_recv()

    def project(part):
        half = WIDTH[part]
        first_half = gath[part][0].reshape(256, half)
        second_half = jnp.concatenate([gath[part][1, 4 * (i % 4) + i // 4] for i in range(16)], axis=0)
        lhs = jnp.concatenate([first_half, second_half], axis=1)
        if part == 0:
            tall = jnp.concatenate([lhs[:, 512 * b : 512 * b + 512] for b in range(3)], axis=0)
            lhs = jnp.concatenate([lhs, nn(unpack[...], tall).astype(BF16)], axis=1)
        p_all[part] = nt(lhs, wo[...]).reshape(16, 16, 512)
        p_send[part] = p_all[part, pl.ds(8 * (1 - c), 8)].astype(BF16)
        cp = remote(p_send.at[part], p_recv.at[part], sib_s.at[6 + part], sib_r.at[6 + part], sib)
        cp.start()
        return cp

    def add_cores(part, cp):
        cp.wait()
        p_sum[part] = (p_all[part, pl.ds(8 * c, 8)] + p_recv[part].astype(F32)).astype(BF16)

    keeper = g // 2
    slot = (g % 2) * 4 + z

    def hand(part, i):
        return remote(
            p_sum.at[part, i], red.at[part, slot], red_s.at[8 * part + i], red_r.at[8 * part + slot],
            (8 * c + i, keeper),
        )

    def hand_out(part):
        for i in range(8):
            to = 8 * c + i

            @pl.when(jnp.logical_or(to != g, keeper != h))
            def _():
                hand(part, i).start()

            @pl.when(jnp.logical_and(to == g, keeper == h))
            def _():
                red[part, slot] = p_sum[part, i]

    def take_in(part):
        half_of = g // 8
        for j in range(2):
            for k in range(4):
                at = j * 4 + k

                @pl.when(jnp.logical_or(2 * h + j != g, 2 * k + half_of != h))
                def _():
                    remote(
                        p_sum.at[part, 0], red.at[part, at], red_s.at[0], red_r.at[8 * part + at], sib
                    ).wait_recv()

        sums = []
        for j in range(2):
            acc = red[part, 4 * j].astype(F32)
            for k in range(1, 4):
                acc = acc + red[part, 4 * j + k].astype(F32)
            sums.append(acc)
        shifted = pltpu.roll(sums[1], 64, 1)
        lane = lax.broadcasted_iota(jnp.int32, (16, 128), 1)
        middle = jnp.where(lane < 64, sums[0][:, 384:512], shifted[:, 0:128])
        mixed = jnp.concatenate([sums[0][:, 0:384], middle, shifted[:, 128:512]], axis=1)
        return mixed.astype(BF16)

    lat_sends = [resident(0), resident(1)]

    for cp in slice_sends:
        cp.wait()
    keys_sib = remote(k8.at[c], k8.at[c], sib_s.at[5], sib_r.at[5], sib)
    keys_sib.start()
    for cp in lat_sends:
        cp.wait()
    load_wv.wait()
    values(0)
    gather_send(0, 0)

    for cp in ask_z:
        cp.wait()
    keys_sib.wait()
    keys = k8[...].reshape(2 * 16 * TOK, WIDE)
    q = q8[...].reshape(4 * ASK, WIDE)
    flag = (lax.broadcasted_iota(jnp.int32, (8, WIDE), 1) == KV + ROPE).astype(BF16)
    present = nt(flag, keys)[0:1] > 0.5
    s = jnp.where(present, nt(q, keys), LOWEST)
    m = jnp.max(s, axis=1, keepdims=True)
    e = jnp.exp((s - m) * SCALE)
    total = jnp.sum(e, axis=1, keepdims=True)
    o = nn(e.astype(BF16), keys[:, 0:KV])
    lane = lax.broadcasted_iota(jnp.int32, (4 * ASK, 128), 1)
    stats = jnp.zeros((4 * ASK, 128), F32)
    for n, rest in enumerate((m, total)):
        for t in range(3):
            piece = rest.astype(BF16).astype(F32)
            rest = rest - piece
            stats = jnp.where(lane == 3 * n + t, piece, stats)
    o8_send[...] = jnp.concatenate([o, stats], axis=1).astype(BF16).reshape(4, ASK, WIDE)
    part_z = []
    for i in range(1, 4):
        to = (z + i) % 4
        cp = remote(o8_send.at[to], o8.at[z], z_s.at[3 + i], z_r.at[3 + i], (g, 2 * to + c))
        cp.start()
        part_z.append(cp)
    o8[z] = o8_send[z]

    lat_sends = [resident(2)]
    gather_wait(0, 0)
    gather_send(0, 1)
    lat_sends.append(resident(3))

    q = q_all[8][:, 0 : KV + ROPE]
    recent = lat[8].astype(BF16)
    s_new = jnp.where(step_mask(ASK, 16), nt(q, recent), LOWEST)
    m_new = jnp.max(s_new, axis=1, keepdims=True)
    e_new = jnp.exp((s_new - m_new) * SCALE)
    total_new = jnp.sum(e_new, axis=1, keepdims=True)
    o_new = nn(e_new.astype(BF16), recent[:, 0:KV])
    for cp in part_z:
        cp.wait()
    m_part, total_part = [], []
    for i in range(4):
        st = o8[i][:, KV:WIDE].astype(F32)
        m_part.append(st[:, 0:1] + st[:, 1:2] + st[:, 2:3])
        total_part.append(st[:, 3:4] + st[:, 4:5] + st[:, 5:6])
    m = m_new
    for one in m_part:
        m = jnp.maximum(m, one)
    weight = jnp.exp((m_new - m) * SCALE)
    o = o_new * weight
    total = total_new * weight
    for i in range(4):
        weight = jnp.exp((m_part[i] - m) * SCALE)
        o = o + o8[i][:, 0:KV].astype(F32) * weight
        total = total + total_part[i] * weight
    lt[8] = (o / total).astype(BF16)
    for cp in lat_sends:
        cp.wait()
    values(1)
    gather_send(1, 0)
    for k in (0, 1):
        pass_on(1, k, 0)
    gather_blocks(1)

    load_wo.wait()
    gather_wait(0, 1)
    swap = project(0)
    add_cores(0, swap)
    hand_out(0)
    gather_last(1)
    swap = project(1)
    sums_a = take_in(0)
    add_cores(1, swap)
    hand_out(1)
    sums_b = take_in(1)

    to_row = lax.broadcasted_iota(jnp.int32, (32, 32), 0)
    from_row = lax.broadcasted_iota(jnp.int32, (32, 32), 1)
    r = to_row // STEPS
    source = jnp.where(r >= ROWS, 16 + 4 * STEPS, r // 2 % 2 * 16 + (r // 4 * 2 + r % 2) * STEPS) + to_row % STEPS
    order = jnp.where(source == from_row, 1.0, 0.0).astype(BF16)
    out[...] = nn(order, jnp.concatenate([sums_a, sums_b], axis=0)).astype(BF16)

    for part in (0, 1):
        for i in range(8):
            pl.when(jnp.logical_or(8 * c + i != g, keeper != h))(hand(part, i).wait_send)
    for cp in ag_sends:
        cp.wait_send()


def body(resident_cache, lengths, slices, placement, queries, latents, w_key, w_value, w_out):
    vmem = pl.BlockSpec(memory_space=pltpu.VMEM)
    smem = pl.BlockSpec(memory_space=pltpu.SMEM)
    anywhere = pl.BlockSpec(memory_space=pl.ANY)
    sems = pltpu.SemaphoreType.DMA
    out = pl.pallas_call(
        kernel,
        out_shape=jax.ShapeDtypeStruct((32, 896), BF16),
        in_specs=[smem, smem] + [anywhere] * 7,
        out_specs=vmem,
        scratch_shapes=[
            pltpu.VMEM((4, KV + ROPE, LRES), BF16),
            pltpu.VMEM((HEADS, NOPE, KV), BF16),
            pltpu.VMEM((HEADS, KV, VD), BF16),
            pltpu.VMEM((512, HEADS * VD), BF16),
            pltpu.VMEM((16, TOK, KV + ROPE), BF16),
            pltpu.VMEM((16 * TOK, WIDE), BF16),
            pltpu.VMEM((16, TOK, WIDE), BF16),
            pltpu.VMEM((ROWS + 1, STEPS, HEADS * 192), BF16),
            pltpu.VMEM((ROWS + 1, STEPS, KV + ROPE), BF16),
            pltpu.VMEM((ROWS + 1, 8, HEADS * 192), F32),
            pltpu.VMEM((ROWS + 1, 16, KV + ROPE), F32),
            pltpu.VMEM((ROWS + 1, ASK, WIDE), BF16),
            pltpu.VMEM((4, ASK, WIDE), BF16),
            pltpu.VMEM((4, ASK, WIDE), BF16),
            pltpu.VMEM((2, 16 * TOK, WIDE), BF16),
            pltpu.VMEM((4, ASK, KV), BF16),
            pltpu.VMEM((ROWS + 1, ASK, KV), BF16),
            pltpu.VMEM((4, ASK, WIDE), BF16),
            pltpu.VMEM((4, ASK, WIDE), BF16),
            pltpu.VMEM((2, 16, 16, WIDTH[0]), BF16),
            pltpu.VMEM((2, 16, 16, WIDTH[1]), BF16),
            pltpu.VMEM((256, 768), BF16),
            pltpu.VMEM((2, 16, 16, 512), F32),
            pltpu.VMEM((2, 8, 16, 512), BF16),
            pltpu.VMEM((2, 8, 16, 512), BF16),
            pltpu.VMEM((2, 8, 16, 512), BF16),
            pltpu.VMEM((2, 8, 16, 512), BF16),
            sems((10,)),
            sems((8,)),
            sems((8,)),
            sems((16,)),
            sems((16,)),
            sems((7,)),
            sems((7,)),
            sems((64,)),
            sems((64,)),
            sems((16,)),
            sems((16,)),
        ],
        compiler_params=pltpu.CompilerParams(
            collective_id=0, has_side_effects=True, vmem_limit_bytes=56 * 1024 * 1024
        ),
        name="decode",
    )(
        lengths,
        placement.reshape(1, 16),
        jnp.swapaxes(queries[:, 0], 0, 1),
        jnp.swapaxes(latents[:, 0], 0, 1),
        jnp.swapaxes(resident_cache[0], 1, 2),
        slices,
        w_key,
        w_value,
        jnp.swapaxes(w_out, 0, 1),
    )
    mixed = out[: STEPS * (ROWS + 1)].reshape(ROWS + 1, STEPS, 896)
    return jnp.swapaxes(mixed, 0, 1)[:, None]


def solution(mesh):
    placed = (
        P("grp", None, None, None),
        P("grp", None),
        P("grp", None, None),
        P("grp", None),
        P(None, "grp", None, "head"),
        P(None, "grp", None, None),
        P("head", None, None),
        P("head", None, None),
        P("head", "grp"),
    )
    return jax.shard_map(
        body, mesh=mesh, in_specs=placed, out_specs=P(None, "grp", None, "head"), check_vma=False
    )
```

```python
import math

import jax
import jax.numpy as jnp
from jax import lax
from jax.experimental import pallas as pl
from jax.experimental.pallas import tpu as pltpu
from jax.sharding import PartitionSpec as P

KV = 512
ROPE = 64
NOPE = 128
VD = 128
ROWS = 8
LRES = 1536
SL = 64
CAP = 2
STEPS = 3

MESH = pl.DeviceIdType.MESH
SCALE = 1.0 / math.sqrt(NOPE + ROPE)
LOWEST = -3.0e38
BF16 = jnp.bfloat16
F32 = jnp.float32
WIDE = 640
PAD = 4
HEADS = 16
ASK = HEADS * PAD
WIDTH = (768, 1024)
TIGHT = HEADS * STEPS
TOK = 16


def remote(src, dst, send_sem, recv_sem, dev):
    return pltpu.make_async_remote_copy(
        src_ref=src, dst_ref=dst, send_sem=send_sem, recv_sem=recv_sem, device_id=dev, device_id_type=MESH
    )


def nt(a, b):
    return lax.dot_general(a, b, (((1,), (1,)), ((), ())), preferred_element_type=F32)


def nn(a, b):
    return jnp.dot(a, b, preferred_element_type=F32)


def step_mask(rows, width, steps=PAD):
    step = lax.broadcasted_iota(jnp.int32, (rows, width), 0) % steps
    at = lax.broadcasted_iota(jnp.int32, (rows, width), 1)
    return (at < STEPS) & (at <= step)


def kernel(
    lengths, placement, queries, latents, cache, slices, w_key, w_value, w_out,
    out,
    kt, wk, wv, wo, sl, slw, k_send, qv, lv, qf, lat,
    q_all, q_sib, q8_mine, q8, k8, o_sib, lt, o8_send, o8,
    gath_a, gath_b, unpack, p_all, p_send, p_recv, p_sum, red,
    dma, sib_s, sib_r, sl_s, sl_r, z_s, z_r, ag_s, ag_r, red_s, red_r,
):
    g = lax.axis_index("grp")
    h = lax.axis_index("head")
    y, x = g // 4, g % 4
    z, c = h // 2, h % 2
    sib = (g, h + 1 - 2 * c)
    gath = (gath_a, gath_b)

    load_sl = pltpu.make_async_copy(slices.at[:, pl.ds(TOK * z, TOK), :], sl, dma.at[1])
    load_qv = pltpu.make_async_copy(queries, qv, dma.at[8])
    load_lv = pltpu.make_async_copy(latents, lv, dma.at[9])
    load_wk = pltpu.make_async_copy(w_key, wk, dma.at[0])
    load_kt = [pltpu.make_async_copy(cache.at[4 * c + i], kt.at[i], dma.at[2 + i]) for i in range(4)]
    load_wv = pltpu.make_async_copy(w_value, wv, dma.at[6])
    load_wo = pltpu.make_async_copy(w_out, wo.at[0:448], dma.at[7])
    load_qv.start()
    load_lv.start()
    load_wk.start()
    load_sl.start()
    load_kt[0].start()

    barrier = pltpu.get_barrier_semaphore()
    for i in range(1, 16):
        pl.semaphore_signal(barrier, inc=1, device_id=((g + i) % 16, h), device_id_type=MESH)
    for i in range(1, 8):
        pl.semaphore_signal(barrier, inc=1, device_id=(g, (h + i) % 8), device_id_type=MESH)

    qf[...] = jnp.zeros_like(qf)
    lat[...] = jnp.zeros_like(lat)
    load_qv.wait()
    load_lv.wait()
    for r in range(ROWS + 1):
        v = qv[r].astype(F32)
        qf[r, 0:STEPS, :] = v
        qf[r, PAD : PAD + STEPS, :] = v
        lat[r, 0:STEPS, :] = lv[r].astype(F32)

    load_wk.wait()
    load_kt[1].start()
    load_wv.start()
    row = lax.broadcasted_iota(jnp.int32, (72, 128), 0)
    lane = lax.broadcasted_iota(jnp.int32, (72, 128), 1)
    first = row % 8 < PAD
    low = lane < ROPE
    for quad in range(4):
        parts = []
        for p in (2 * quad, 2 * quad + 1):
            t = qf[:, :, 384 * p : 384 * p + 384].reshape(72, 384)
            t0, t1, t2 = t[:, 0:128], t[:, 128:256], t[:, 256:384]
            r1, r2 = pltpu.roll(t1, 64, 1), pltpu.roll(t2, 64, 1)
            second_nope = jnp.where(low, r1, r2)
            rope = jnp.where(low, jnp.where(first, t1, r2), 0.0)
            lhs = jnp.concatenate([jnp.where(first, t0, 0.0), jnp.where(first, 0.0, second_nope)], axis=1)
            absorbed = nn(lhs.astype(BF16), wk[2 * p : 2 * p + 2].reshape(2 * NOPE, KV))
            parts.append(jnp.concatenate([absorbed, rope], axis=1).reshape(9, 8, WIDE))
        q_all[:, 16 * quad : 16 * quad + 16, :] = jnp.concatenate(parts, axis=1).astype(BF16)

    owners = [placement[0, i] for i in range(16)]
    owner_of_lane = lax.broadcasted_iota(jnp.int32, (8, 16 * TOK), 1) // TOK
    code = jnp.zeros((8, 16 * TOK), jnp.int32)
    for i in range(16):
        rank = jnp.int32(0)
        for j in range(i):
            rank = rank + jnp.where(owners[j] == owners[i], 1, 0)
        code = jnp.where(owner_of_lane == i, owners[i] * CAP + rank, code)

    slw[:, KV:WIDE] = jnp.ones((16 * TOK, WIDE - KV), BF16)
    at0 = lax.broadcasted_iota(jnp.int32, (16 * TOK, 16 * TOK), 0)
    at1 = lax.broadcasted_iota(jnp.int32, (16 * TOK, 16 * TOK), 1)
    chosen = (at0 % TOK == at1 % TOK) & ((at0 // TOK) * CAP + c == code[0:1, :])
    selector = jnp.where(chosen, 1.0, 0.0).astype(BF16)
    load_sl.wait()
    slw[:, 0 : KV + ROPE] = sl[...].reshape(16 * TOK, KV + ROPE)
    k_send[...] = nn(selector, slw[...]).astype(BF16).reshape(16, TOK, WIDE)

    wo[448:512, :] = jnp.zeros((64, 2048), BF16)
    to_row = lax.broadcasted_iota(jnp.int32, (256, 256), 0)
    from_row = lax.broadcasted_iota(jnp.int32, (256, 256), 1)
    for b in range(3):
        back = (to_row // 16 == from_row // 16) & (to_row % 16 == from_row % 16 - 12 + 4 * b) & (from_row % 16 >= 12)
        unpack[:, 256 * b : 256 * b + 256] = jnp.where(back, 1.0, 0.0).astype(BF16)

    tight = (lax.broadcasted_iota(jnp.int32, (TIGHT, ASK), 0), lax.broadcasted_iota(jnp.int32, (TIGHT, ASK), 1))
    tight = jnp.where((tight[0] // STEPS == tight[1] // PAD) & (tight[0] % STEPS == tight[1] % PAD), 1.0, 0.0)
    q8_mine[...] = nn(tight.astype(BF16), q_all[8]).astype(BF16)

    pl.semaphore_wait(barrier, 22)

    ask_sib = remote(q_all.at[pl.ds(4 * (1 - c), 4)], q_sib, sib_s.at[0], sib_r.at[0], sib)
    ask_sib.start()
    ask_z = []
    for i in range(1, 4):
        to = (z + i) % 4
        cp = remote(q8_mine, q8.at[z], z_s.at[i], z_r.at[i], (g, 2 * to + c))
        cp.start()
        ask_z.append(cp)
    q8[z] = q8_mine[...]

    slice_sends = []
    for i in range(1, 16):
        to = (g + i) % 16
        cp = remote(k_send.at[to], k8.at[c, pl.ds(TOK * g, TOK)], sl_s.at[i], sl_r.at[i], (to, h))
        cp.start()
        slice_sends.append(cp)
    k8[c, pl.ds(TOK * g, TOK), :] = k_send[g]

    ask_sib.wait()

    recent_ok = step_mask(2 * ASK, 16)

    def resident(i):
        load_kt[i].wait()
        if i == 0:
            load_kt[2].start()
        if i == 1:
            load_kt[3].start()
            load_wo.start()
        q = jnp.concatenate([q_all[4 * c + i], q_sib[i]], axis=0)[:, 0 : KV + ROPE]
        recent = lat[4 * c + i].astype(BF16)
        s = nn(q, kt[i])
        s_new = jnp.where(recent_ok, nt(q, recent), LOWEST)
        ok = lax.broadcasted_iota(jnp.int32, (1, LRES), 1) < lengths[0, 4 * c + i]
        s = jnp.where(ok, s, LOWEST)
        m = jnp.maximum(jnp.max(s, axis=1, keepdims=True), jnp.max(s_new, axis=1, keepdims=True))
        e = jnp.exp((s - m) * SCALE)
        e_new = jnp.exp((s_new - m) * SCALE)
        total = jnp.sum(e, axis=1, keepdims=True) + jnp.sum(e_new, axis=1, keepdims=True)
        o = nt(e.astype(BF16), kt[i, 0:KV, :]) + nn(e_new.astype(BF16), recent[:, 0:KV])
        o = (o / total).astype(BF16)
        at = (i // 2) * 4 + c * 2 + i % 2
        lt[at] = o[0:ASK]
        o_sib[i] = o[ASK:]
        cp = remote(o_sib.at[i], lt.at[at], sib_s.at[1 + i], sib_r.at[1 + i], sib)
        cp.start()
        return cp

    def values(part):
        lo, count = (0, 4) if part == 0 else (4, 5)
        rows = 16 * count
        head_of_row = lax.broadcasted_iota(jnp.int32, (rows, 512), 0) % 16 // PAD
        head_of_lane = lax.broadcasted_iota(jnp.int32, (rows, 512), 1) // VD
        mine = head_of_row == head_of_lane
        heads_out = []
        for quad in range(4):
            lhs = lt[lo : lo + count, 16 * quad : 16 * quad + 16, :].reshape(rows, KV)
            rhs = jnp.concatenate([wv[4 * quad + j] for j in range(4)], axis=1)
            heads_out.append(jnp.where(mine, nn(lhs, rhs), 0.0).astype(BF16))
        to_row = lax.broadcasted_iota(jnp.int32, (16, rows), 0)
        from_row = lax.broadcasted_iota(jnp.int32, (16, rows), 1)

        def picks(at):
            return (at // STEPS == from_row // 16) & (at % STEPS == from_row % PAD)

        blocks = []
        if part == 0:
            direct = jnp.where((to_row < 12) & picks(to_row), 1.0, 0.0).astype(BF16)
            for b in range(3):
                under = jnp.where((to_row >= 12) & picks(4 * b + to_row - 12), 1.0, 0.0).astype(BF16)
                blocks.append(nn(direct, heads_out[b]) + nn(under, heads_out[3]))
        else:
            direct = jnp.where((to_row < 15) & picks(to_row), 1.0, 0.0).astype(BF16)
            for b in range(4):
                blocks.append(nn(direct, heads_out[b]))
        block = jnp.concatenate(blocks, axis=1).astype(BF16)
        half = WIDTH[part]
        gath[part][0, 4 * y + x] = block[:, 0:half]
        gath[part][1, 4 * x + y] = block[:, half:]

    ag_sends = []

    def along(axis, d):
        if axis == 0:
            return (4 * y + (x + d) % 4, h)
        return ((y + d) % 4 * 4 + x, h)

    def blocks_of(part, k, ring, d):
        one, two = (x, y) if k == 0 else (y, x)
        if ring == 0:
            return gath[part].at[k, pl.ds(4 * two + (one - d) % 4, 1)]
        return gath[part].at[k, pl.ds(4 * ((two - d) % 4), 4)]

    def gather_send(part, ring):
        for k in (0, 1):
            ref = blocks_of(part, k, ring, 0)
            for d in (2, 1, 3):
                n = ((part * 2 + k) * 2 + ring) * 4 + d
                cp = remote(ref, ref, ag_s.at[n], ag_r.at[n], along(ring if k == 0 else 1 - ring, d))
                cp.start()
                ag_sends.append(cp)

    def gather_wait(part, ring):
        for k in (0, 1):
            for d in (1, 3, 2):
                n = ((part * 2 + k) * 2 + ring) * 4 + d
                ref = blocks_of(part, k, ring, d)
                remote(ref, ref, ag_s.at[n], ag_r.at[n], along(ring if k == 0 else 1 - ring, d)).wait_recv()

    def one_block(part, k, d1, d2):
        one, two = (x, y) if k == 0 else (y, x)
        return gath[part].at[k, pl.ds(4 * ((two - d2) % 4) + (one - d1) % 4, 1)]

    def pass_on(part, k, d1):
        ref = one_block(part, k, d1, 0)
        for d in (2, 1, 3):
            n = 32 + (k * 4 + d1) * 4 + d
            cp = remote(ref, ref, ag_s.at[n], ag_r.at[n], along(1 - k, d))
            cp.start()
            ag_sends.append(cp)

    def gather_blocks(part):
        for d in (1, 3, 2):
            for k in (0, 1):
                n = ((part * 2 + k) * 2) * 4 + d
                ref = blocks_of(part, k, 0, d)
                remote(ref, ref, ag_s.at[n], ag_r.at[n], along(k, d)).wait_recv()
                pass_on(part, k, d)

    def gather_last(part):
        for k in (0, 1):
            for d1 in (0, 1, 3, 2):
                for d2 in (1, 3, 2):
                    n = 32 + (k * 4 + d1) * 4 + d2
                    ref = one_block(part, k, d1, d2)
                    remote(ref, ref, ag_s.at[n], ag_r.at[n], along(1 - k, d2)).wait_recv()

    def project(part):
        half = WIDTH[part]
        first_half = gath[part][0].reshape(256, half)
        second_half = jnp.concatenate([gath[part][1, 4 * (i % 4) + i // 4] for i in range(16)], axis=0)
        lhs = jnp.concatenate([first_half, second_half], axis=1)
        if part == 0:
            tall = jnp.concatenate([lhs[:, 512 * b : 512 * b + 512] for b in range(3)], axis=0)
            lhs = jnp.concatenate([lhs, nn(unpack[...], tall).astype(BF16)], axis=1)
        p_all[part] = nt(lhs, wo[...]).reshape(16, 16, 512)
        p_send[part] = p_all[part, pl.ds(8 * (1 - c), 8)].astype(BF16)
        cp = remote(p_send.at[part], p_recv.at[part], sib_s.at[6 + part], sib_r.at[6 + part], sib)
        cp.start()
        return cp

    def add_cores(part, cp):
        cp.wait()
        p_sum[part] = (p_all[part, pl.ds(8 * c, 8)] + p_recv[part].astype(F32)).astype(BF16)

    keeper = g // 2
    slot = (g % 2) * 4 + z

    def hand(part, i):
        return remote(
            p_sum.at[part, i], red.at[part, slot], red_s.at[8 * part + i], red_r.at[8 * part + slot],
            (8 * c + i, keeper),
        )

    def hand_out(part):
        for i in range(8):
            to = 8 * c + i

            @pl.when(jnp.logical_or(to != g, keeper != h))
            def _():
                hand(part, i).start()

            @pl.when(jnp.logical_and(to == g, keeper == h))
            def _():
                red[part, slot] = p_sum[part, i]

    def take_in(part):
        half_of = g // 8
        for j in range(2):
            for k in range(4):
                at = j * 4 + k

                @pl.when(jnp.logical_or(2 * h + j != g, 2 * k + half_of != h))
                def _():
                    remote(
                        p_sum.at[part, 0], red.at[part, at], red_s.at[0], red_r.at[8 * part + at], sib
                    ).wait_recv()

        sums = []
        for j in range(2):
            acc = red[part, 4 * j].astype(F32)
            for k in range(1, 4):
                acc = acc + red[part, 4 * j + k].astype(F32)
            sums.append(acc)
        shifted = pltpu.roll(sums[1], 64, 1)
        lane = lax.broadcasted_iota(jnp.int32, (16, 128), 1)
        middle = jnp.where(lane < 64, sums[0][:, 384:512], shifted[:, 0:128])
        mixed = jnp.concatenate([sums[0][:, 0:384], middle, shifted[:, 128:512]], axis=1)
        return mixed.astype(BF16)

    lat_sends = [resident(0), resident(1)]

    for cp in slice_sends:
        cp.wait()
    keys_sib = remote(k8.at[c], k8.at[c], sib_s.at[5], sib_r.at[5], sib)
    keys_sib.start()
    for cp in lat_sends:
        cp.wait()
    load_wv.wait()
    values(0)
    gather_send(0, 0)

    for cp in ask_z:
        cp.wait()
    keys_sib.wait()
    keys = k8[...].reshape(2 * 16 * TOK, WIDE)
    q = q8[...].reshape(4 * TIGHT, WIDE)
    flag = (lax.broadcasted_iota(jnp.int32, (8, WIDE), 1) == KV + ROPE).astype(BF16)
    present = nt(flag, keys)[0:1] > 0.5
    s = jnp.where(present, nt(q, keys), LOWEST)
    m = jnp.max(s, axis=1, keepdims=True)
    e = jnp.exp((s - m) * SCALE)
    total = jnp.sum(e, axis=1, keepdims=True)
    o = nn(e.astype(BF16), keys[:, 0:KV])
    lane = lax.broadcasted_iota(jnp.int32, (4 * TIGHT, 128), 1)
    stats = jnp.zeros((4 * TIGHT, 128), F32)
    for n, rest in enumerate((m, total)):
        for t in range(3):
            piece = rest.astype(BF16).astype(F32)
            rest = rest - piece
            stats = jnp.where(lane == 3 * n + t, piece, stats)
    o8_send[...] = jnp.concatenate([o, stats], axis=1).astype(BF16).reshape(4, TIGHT, WIDE)
    part_z = []
    for i in range(1, 4):
        to = (z + i) % 4
        cp = remote(o8_send.at[to], o8.at[z], z_s.at[3 + i], z_r.at[3 + i], (g, 2 * to + c))
        cp.start()
        part_z.append(cp)
    o8[z] = o8_send[z]

    lat_sends = [resident(2)]
    gather_wait(0, 0)
    gather_send(0, 1)
    lat_sends.append(resident(3))

    q = q8_mine[:, 0 : KV + ROPE]
    recent = lat[8].astype(BF16)
    s_new = jnp.where(step_mask(TIGHT, 16, STEPS), nt(q, recent), LOWEST)
    m_new = jnp.max(s_new, axis=1, keepdims=True)
    e_new = jnp.exp((s_new - m_new) * SCALE)
    total_new = jnp.sum(e_new, axis=1, keepdims=True)
    o_new = nn(e_new.astype(BF16), recent[:, 0:KV])
    for cp in part_z:
        cp.wait()
    m_part, total_part = [], []
    for i in range(4):
        st = o8[i][:, KV:WIDE].astype(F32)
        m_part.append(st[:, 0:1] + st[:, 1:2] + st[:, 2:3])
        total_part.append(st[:, 3:4] + st[:, 4:5] + st[:, 5:6])
    m = m_new
    for one in m_part:
        m = jnp.maximum(m, one)
    weight = jnp.exp((m_new - m) * SCALE)
    o = o_new * weight
    total = total_new * weight
    for i in range(4):
        weight = jnp.exp((m_part[i] - m) * SCALE)
        o = o + o8[i][:, 0:KV].astype(F32) * weight
        total = total + total_part[i] * weight
    loose = (lax.broadcasted_iota(jnp.int32, (ASK, TIGHT), 0), lax.broadcasted_iota(jnp.int32, (ASK, TIGHT), 1))
    loose = jnp.where((loose[0] // PAD == loose[1] // STEPS) & (loose[0] % PAD == loose[1] % STEPS), 1.0, 0.0)
    lt[8] = nn(loose.astype(BF16), (o / total).astype(BF16)).astype(BF16)
    for cp in lat_sends:
        cp.wait()
    values(1)
    gather_send(1, 0)
    for k in (0, 1):
        pass_on(1, k, 0)
    gather_blocks(1)

    load_wo.wait()
    gather_wait(0, 1)
    swap = project(0)
    add_cores(0, swap)
    hand_out(0)
    gather_last(1)
    swap = project(1)
    sums_a = take_in(0)
    add_cores(1, swap)
    hand_out(1)
    sums_b = take_in(1)

    to_row = lax.broadcasted_iota(jnp.int32, (16 * STEPS, 32), 0)
    from_row = lax.broadcasted_iota(jnp.int32, (16 * STEPS, 32), 1)
    r = to_row % 16
    source = jnp.where(r >= ROWS, 16 + 4 * STEPS, r // 2 % 2 * 16 + (r // 4 * 2 + r % 2) * STEPS) + to_row // 16
    order = jnp.where(source == from_row, 1.0, 0.0).astype(BF16)
    mixed = nn(order, jnp.concatenate([sums_a, sums_b], axis=0)).astype(BF16)
    for t in range(STEPS):
        out[t] = mixed[16 * t : 16 * t + ROWS + 1]

    for part in (0, 1):
        for i in range(8):
            pl.when(jnp.logical_or(8 * c + i != g, keeper != h))(hand(part, i).wait_send)
    for cp in ag_sends:
        cp.wait_send()


def body(resident_cache, lengths, slices, placement, queries, latents, w_key, w_value, w_out):
    vmem = pl.BlockSpec(memory_space=pltpu.VMEM)
    smem = pl.BlockSpec(memory_space=pltpu.SMEM)
    anywhere = pl.BlockSpec(memory_space=pl.ANY)
    sems = pltpu.SemaphoreType.DMA
    out = pl.pallas_call(
        kernel,
        out_shape=jax.ShapeDtypeStruct((STEPS, ROWS + 1, 896), BF16),
        in_specs=[smem, smem] + [anywhere] * 7,
        out_specs=vmem,
        scratch_shapes=[
            pltpu.VMEM((4, KV + ROPE, LRES), BF16),
            pltpu.VMEM((HEADS, NOPE, KV), BF16),
            pltpu.VMEM((HEADS, KV, VD), BF16),
            pltpu.VMEM((512, HEADS * VD), BF16),
            pltpu.VMEM((16, TOK, KV + ROPE), BF16),
            pltpu.VMEM((16 * TOK, WIDE), BF16),
            pltpu.VMEM((16, TOK, WIDE), BF16),
            pltpu.VMEM((ROWS + 1, STEPS, HEADS * 192), BF16),
            pltpu.VMEM((ROWS + 1, STEPS, KV + ROPE), BF16),
            pltpu.VMEM((ROWS + 1, 8, HEADS * 192), F32),
            pltpu.VMEM((ROWS + 1, 16, KV + ROPE), F32),
            pltpu.VMEM((ROWS + 1, ASK, WIDE), BF16),
            pltpu.VMEM((4, ASK, WIDE), BF16),
            pltpu.VMEM((TIGHT, WIDE), BF16),
            pltpu.VMEM((4, TIGHT, WIDE), BF16),
            pltpu.VMEM((2, 16 * TOK, WIDE), BF16),
            pltpu.VMEM((4, ASK, KV), BF16),
            pltpu.VMEM((ROWS + 1, ASK, KV), BF16),
            pltpu.VMEM((4, TIGHT, WIDE), BF16),
            pltpu.VMEM((4, TIGHT, WIDE), BF16),
            pltpu.VMEM((2, 16, 16, WIDTH[0]), BF16),
            pltpu.VMEM((2, 16, 16, WIDTH[1]), BF16),
            pltpu.VMEM((256, 768), BF16),
            pltpu.VMEM((2, 16, 16, 512), F32),
            pltpu.VMEM((2, 8, 16, 512), BF16),
            pltpu.VMEM((2, 8, 16, 512), BF16),
            pltpu.VMEM((2, 8, 16, 512), BF16),
            pltpu.VMEM((2, 8, 16, 512), BF16),
            sems((10,)),
            sems((8,)),
            sems((8,)),
            sems((16,)),
            sems((16,)),
            sems((7,)),
            sems((7,)),
            sems((64,)),
            sems((64,)),
            sems((16,)),
            sems((16,)),
        ],
        compiler_params=pltpu.CompilerParams(
            collective_id=0, has_side_effects=True, vmem_limit_bytes=56 * 1024 * 1024
        ),
        name="decode",
    )(
        lengths,
        placement.reshape(1, 16),
        jnp.swapaxes(queries[:, 0], 0, 1),
        jnp.swapaxes(latents[:, 0], 0, 1),
        jnp.swapaxes(resident_cache[0], 1, 2),
        slices,
        w_key,
        w_value,
        jnp.swapaxes(w_out, 0, 1),
    )
    return out[:, None]


def solution(mesh):
    placed = (
        P("grp", None, None, None),
        P("grp", None),
        P("grp", None, None),
        P("grp", None),
        P(None, "grp", None, "head"),
        P(None, "grp", None, None),
        P("head", None, None),
        P("head", None, None),
        P("head", "grp"),
    )
    return jax.shard_map(
        body, mesh=mesh, in_specs=placed, out_specs=P(None, "grp", None, "head"), check_vma=False
    )
```

```python
import math

import jax
import jax.numpy as jnp
from jax import lax
from jax.experimental import pallas as pl
from jax.experimental.pallas import tpu as pltpu
from jax.sharding import PartitionSpec as P

KV = 512
ROPE = 64
NOPE = 128
VD = 128
ROWS = 8
LRES = 1536
SL = 64
CAP = 2
STEPS = 3

MESH = pl.DeviceIdType.MESH
SCALE = 1.0 / math.sqrt(NOPE + ROPE)
LOWEST = -3.0e38
BF16 = jnp.bfloat16
F32 = jnp.float32
WIDE = 640
PAD = 4
HEADS = 16
ASK = HEADS * PAD
WIDTH = (768, 768, 256)
TIGHT = HEADS * STEPS
FAR = (2, 1, 3, 0)
TOK = 16


def remote(src, dst, send_sem, recv_sem, dev):
    return pltpu.make_async_remote_copy(
        src_ref=src, dst_ref=dst, send_sem=send_sem, recv_sem=recv_sem, device_id=dev, device_id_type=MESH
    )


def nt(a, b):
    return lax.dot_general(a, b, (((1,), (1,)), ((), ())), preferred_element_type=F32)


def nn(a, b):
    return jnp.dot(a, b, preferred_element_type=F32)


def step_mask(rows, width, steps=PAD):
    step = lax.broadcasted_iota(jnp.int32, (rows, width), 0) % steps
    at = lax.broadcasted_iota(jnp.int32, (rows, width), 1)
    return (at < STEPS) & (at <= step)


def kernel(
    lengths, placement, queries, latents, cache, slices, w_key, w_value, w_out,
    out,
    kt, wk, wv, wo, sl, slw, k_send, qv, lv, qf, lat,
    q_all, q_sib, q8_mine, q8, k8, o_sib, lt, o8_send, o8,
    gath_a, gath_b, gath_c, unpack, unpack_new, p_all, p_send, p_recv, p_sum, red,
    dma, sib_s, sib_r, sl_s, sl_r, z_s, z_r, ag_s, ag_r, red_s, red_r,
):
    g = lax.axis_index("grp")
    h = lax.axis_index("head")
    y, x = g // 4, g % 4
    z, c = h // 2, h % 2
    sib = (g, h + 1 - 2 * c)
    gath = (gath_a, gath_b, gath_c)

    load_sl = pltpu.make_async_copy(slices.at[:, pl.ds(TOK * z, TOK), :], sl, dma.at[1])
    load_qv = pltpu.make_async_copy(queries, qv, dma.at[8])
    load_lv = pltpu.make_async_copy(latents, lv, dma.at[9])
    load_wk = pltpu.make_async_copy(w_key, wk, dma.at[0])
    load_kt = [pltpu.make_async_copy(cache.at[4 * c + i], kt.at[i], dma.at[2 + i]) for i in range(4)]
    load_wv = pltpu.make_async_copy(w_value, wv, dma.at[6])
    load_wo = pltpu.make_async_copy(w_out, wo.at[0:448], dma.at[7])
    load_qv.start()
    load_lv.start()
    load_wk.start()
    load_sl.start()
    load_kt[0].start()

    barrier = pltpu.get_barrier_semaphore()
    offsets = sorted(
        ((dy, dx) for dy in range(4) for dx in range(4) if dy or dx),
        key=lambda o: -min(o[0], 4 - o[0]) - min(o[1], 4 - o[1]),
    )

    def group_at(dy, dx):
        return (y + dy) % 4 * 4 + (x + dx) % 4

    for dy, dx in offsets:
        pl.semaphore_signal(barrier, inc=1, device_id=(group_at(dy, dx), h), device_id_type=MESH)
    for i in (2, 1, 3):
        pl.semaphore_signal(barrier, inc=1, device_id=(g, 2 * ((z + i) % 4) + c), device_id_type=MESH)
    pl.semaphore_signal(barrier, inc=1, device_id=sib, device_id_type=MESH)

    qf[...] = jnp.zeros_like(qf)
    lat[...] = jnp.zeros_like(lat)
    load_qv.wait()
    load_lv.wait()
    for r in range(ROWS + 1):
        v = qv[r].astype(F32)
        qf[r, 0:STEPS, :] = v
        qf[r, PAD : PAD + STEPS, :] = v
        lat[r, 0:STEPS, :] = lv[r].astype(F32)

    load_wk.wait()
    load_kt[1].start()
    load_wv.start()
    row = lax.broadcasted_iota(jnp.int32, (72, 128), 0)
    lane = lax.broadcasted_iota(jnp.int32, (72, 128), 1)
    first = row % 8 < PAD
    low = lane < ROPE
    for quad in range(4):
        parts = []
        for p in (2 * quad, 2 * quad + 1):
            t = qf[:, :, 384 * p : 384 * p + 384].reshape(72, 384)
            t0, t1, t2 = t[:, 0:128], t[:, 128:256], t[:, 256:384]
            r1, r2 = pltpu.roll(t1, 64, 1), pltpu.roll(t2, 64, 1)
            second_nope = jnp.where(low, r1, r2)
            rope = jnp.where(low, jnp.where(first, t1, r2), 0.0)
            lhs = jnp.concatenate([jnp.where(first, t0, 0.0), jnp.where(first, 0.0, second_nope)], axis=1)
            absorbed = nn(lhs.astype(BF16), wk[2 * p : 2 * p + 2].reshape(2 * NOPE, KV))
            parts.append(jnp.concatenate([absorbed, rope], axis=1).reshape(9, 8, WIDE))
        q_all[:, 16 * quad : 16 * quad + 16, :] = jnp.concatenate(parts, axis=1).astype(BF16)

    owners = [placement[0, i] for i in range(16)]
    owner_of_lane = lax.broadcasted_iota(jnp.int32, (8, 16 * TOK), 1) // TOK
    code = jnp.zeros((8, 16 * TOK), jnp.int32)
    for i in range(16):
        rank = jnp.int32(0)
        for j in range(i):
            rank = rank + jnp.where(owners[j] == owners[i], 1, 0)
        code = jnp.where(owner_of_lane == i, owners[i] * CAP + rank, code)

    slw[:, KV:WIDE] = jnp.ones((16 * TOK, WIDE - KV), BF16)
    at0 = lax.broadcasted_iota(jnp.int32, (16 * TOK, 16 * TOK), 0)
    at1 = lax.broadcasted_iota(jnp.int32, (16 * TOK, 16 * TOK), 1)
    chosen = (at0 % TOK == at1 % TOK) & ((at0 // TOK) * CAP + c == code[0:1, :])
    selector = jnp.where(chosen, 1.0, 0.0).astype(BF16)
    load_sl.wait()
    slw[:, 0 : KV + ROPE] = sl[...].reshape(16 * TOK, KV + ROPE)
    k_send[...] = nn(selector, slw[...]).astype(BF16).reshape(16, TOK, WIDE)

    wo[448:512, :] = jnp.zeros((64, 2048), BF16)
    to_row = lax.broadcasted_iota(jnp.int32, (256, 256), 0)
    from_row = lax.broadcasted_iota(jnp.int32, (256, 256), 1)
    for b in range(3):
        back = (to_row // 16 == from_row // 16) & (to_row % 16 == from_row % 16 - 12 + 4 * b) & (from_row % 16 >= 12)
        unpack[:, 256 * b : 256 * b + 256] = jnp.where(back, 1.0, 0.0).astype(BF16)

    tight = (lax.broadcasted_iota(jnp.int32, (TIGHT, ASK), 0), lax.broadcasted_iota(jnp.int32, (TIGHT, ASK), 1))
    tight = jnp.where((tight[0] // STEPS == tight[1] // PAD) & (tight[0] % STEPS == tight[1] % PAD), 1.0, 0.0)
    q8_mine[...] = nn(tight.astype(BF16), q_all[8]).astype(BF16)

    pl.semaphore_wait(barrier, 19)

    ask_sib = remote(q_all.at[pl.ds(4 * (1 - c), 4)], q_sib, sib_s.at[0], sib_r.at[0], sib)
    ask_sib.start()

    slice_sends = []
    for i, (dy, dx) in enumerate(offsets):
        to = group_at(dy, dx)
        cp = remote(k_send.at[to], k8.at[c, pl.ds(TOK * g, TOK)], sl_s.at[i], sl_r.at[i], (to, h))
        cp.start()
        slice_sends.append(cp)
    k8[c, pl.ds(TOK * g, TOK), :] = k_send[g]

    ask_z = []
    for i in (2, 1, 3):
        to = (z + i) % 4
        cp = remote(q8_mine, q8.at[z], z_s.at[i], z_r.at[i], (g, 2 * to + c))
        cp.start()
        ask_z.append(cp)
    q8[z] = q8_mine[...]

    ask_sib.wait()

    recent_ok = step_mask(2 * ASK, 16)

    def resident(i):
        load_kt[i].wait()
        if i == 0:
            load_kt[2].start()
        if i == 1:
            load_kt[3].start()
            load_wo.start()
        q = jnp.concatenate([q_all[4 * c + i], q_sib[i]], axis=0)[:, 0 : KV + ROPE]
        recent = lat[4 * c + i].astype(BF16)
        s = nn(q, kt[i])
        s_new = jnp.where(recent_ok, nt(q, recent), LOWEST)
        ok = lax.broadcasted_iota(jnp.int32, (1, LRES), 1) < lengths[0, 4 * c + i]
        s = jnp.where(ok, s, LOWEST)
        m = jnp.maximum(jnp.max(s, axis=1, keepdims=True), jnp.max(s_new, axis=1, keepdims=True))
        e = jnp.exp((s - m) * SCALE)
        e_new = jnp.exp((s_new - m) * SCALE)
        total = jnp.sum(e, axis=1, keepdims=True) + jnp.sum(e_new, axis=1, keepdims=True)
        o = nt(e.astype(BF16), kt[i, 0:KV, :]) + nn(e_new.astype(BF16), recent[:, 0:KV])
        o = (o / total).astype(BF16)
        at = (i // 2) * 4 + c * 2 + i % 2
        lt[at] = o[0:ASK]
        o_sib[i] = o[ASK:]
        cp = remote(o_sib.at[i], lt.at[at], sib_s.at[1 + i], sib_r.at[1 + i], sib)
        cp.start()
        return cp

    def values(part):
        count = 1 if part == 2 else 4
        rows = 16 * count
        head_of_row = lax.broadcasted_iota(jnp.int32, (rows, 512), 0) % 16 // PAD
        head_of_lane = lax.broadcasted_iota(jnp.int32, (rows, 512), 1) // VD
        mine = head_of_row == head_of_lane
        heads_out = []
        for quad in range(4):
            lhs = lt[4 * part : 4 * part + count, 16 * quad : 16 * quad + 16, :].reshape(rows, KV)
            rhs = jnp.concatenate([wv[4 * quad + j] for j in range(4)], axis=1)
            heads_out.append(jnp.where(mine, nn(lhs, rhs), 0.0).astype(BF16))
        if part == 2:
            to_row = lax.broadcasted_iota(jnp.int32, (16, 64), 0)
            from_row = lax.broadcasted_iota(jnp.int32, (16, 64), 1)
            spread = (to_row // 4 == from_row // 16) & (to_row % 4 == from_row % PAD) & (to_row % 4 < STEPS)
            spread = jnp.where(spread, 1.0, 0.0).astype(BF16)
            block = nn(spread, jnp.concatenate(heads_out, axis=0)).astype(BF16)
        else:
            to_row = lax.broadcasted_iota(jnp.int32, (16, rows), 0)
            from_row = lax.broadcasted_iota(jnp.int32, (16, rows), 1)

            def picks(at):
                return (at // STEPS == from_row // 16) & (at % STEPS == from_row % PAD)

            blocks = []
            direct = jnp.where((to_row < 12) & picks(to_row), 1.0, 0.0).astype(BF16)
            for b in range(3):
                under = jnp.where((to_row >= 12) & picks(4 * b + to_row - 12), 1.0, 0.0).astype(BF16)
                blocks.append(nn(direct, heads_out[b]) + nn(under, heads_out[3]))
            block = jnp.concatenate(blocks, axis=1).astype(BF16)
        half = WIDTH[part]
        gath[part][0, 4 * y + x] = block[:, 0:half]
        gath[part][1, 4 * x + y] = block[:, half:]

    ag_sends = []

    def along(axis, d):
        if axis == 0:
            return (4 * y + (x + d) % 4, h)
        return ((y + d) % 4 * 4 + x, h)

    def blocks_of(part, k, ring, d):
        one, two = (x, y) if k == 0 else (y, x)
        if ring == 0:
            return gath[part].at[k, pl.ds(4 * two + (one - d) % 4, 1)]
        return gath[part].at[k, pl.ds(4 * ((two - d) % 4), 4)]

    def gather_send(part, ring):
        for k in (0, 1):
            ref = blocks_of(part, k, ring, 0)
            for d in (2, 1, 3):
                n = ((part * 2 + k) * 2 + ring) * 4 + d
                cp = remote(ref, ref, ag_s.at[n], ag_r.at[n], along(ring if k == 0 else 1 - ring, d))
                cp.start()
                ag_sends.append(cp)

    def gather_wait(part, ring):
        for k in (0, 1):
            for d in (1, 3, 2):
                n = ((part * 2 + k) * 2 + ring) * 4 + d
                ref = blocks_of(part, k, ring, d)
                remote(ref, ref, ag_s.at[n], ag_r.at[n], along(ring if k == 0 else 1 - ring, d)).wait_recv()

    def project(part):
        half = WIDTH[part]
        first_half = gath[part][0].reshape(256, half)
        second_half = jnp.concatenate([gath[part][1, 4 * (i % 4) + i // 4] for i in range(16)], axis=0)
        lhs = jnp.concatenate([first_half, second_half], axis=1)
        if part == 2:
            lhs = jnp.concatenate([nn(unpack_new[b], lhs).astype(BF16) for b in range(4)], axis=1)
        else:
            tall = jnp.concatenate([lhs[:, 512 * b : 512 * b + 512] for b in range(3)], axis=0)
            lhs = jnp.concatenate([lhs, nn(unpack[...], tall).astype(BF16)], axis=1)
        p_all[part] = nt(lhs, wo[...]).reshape(16, 16, 512)
        p_send[part] = p_all[part, pl.ds(8 * (1 - c), 8)].astype(BF16)
        cp = remote(p_send.at[part], p_recv.at[part], sib_s.at[6 + part], sib_r.at[6 + part], sib)
        cp.start()
        return cp

    def add_cores(part, cp):
        cp.wait()
        p_sum[part] = (p_all[part, pl.ds(8 * c, 8)] + p_recv[part].astype(F32)).astype(BF16)

    keeper = g // 2
    slot = (g % 2) * 4 + z

    def hand(part, i):
        return remote(
            p_sum.at[part, i // 4 * 4 + (x + FAR[i % 4]) % 4], red.at[part, slot], red_s.at[8 * part + i], red_r.at[8 * part + slot],
            (8 * c + i // 4 * 4 + (x + FAR[i % 4]) % 4, keeper),
        )

    def hand_out(part):
        for i in range(8):
            to = 8 * c + i // 4 * 4 + (x + FAR[i % 4]) % 4

            @pl.when(jnp.logical_or(to != g, keeper != h))
            def _():
                hand(part, i).start()

            @pl.when(jnp.logical_and(to == g, keeper == h))
            def _():
                red[part, slot] = p_sum[part, i // 4 * 4 + (x + FAR[i % 4]) % 4]

    def take_in(part):
        half_of = g // 8
        for j in range(2):
            for k in range(4):
                at = j * 4 + k

                @pl.when(jnp.logical_or(2 * h + j != g, 2 * k + half_of != h))
                def _():
                    remote(
                        p_sum.at[part, 0], red.at[part, at], red_s.at[0], red_r.at[8 * part + at], sib
                    ).wait_recv()

        sums = []
        for j in range(2):
            acc = red[part, 4 * j].astype(F32)
            for k in range(1, 4):
                acc = acc + red[part, 4 * j + k].astype(F32)
            sums.append(acc)
        shifted = pltpu.roll(sums[1], 64, 1)
        lane = lax.broadcasted_iota(jnp.int32, (16, 128), 1)
        middle = jnp.where(lane < 64, sums[0][:, 384:512], shifted[:, 0:128])
        mixed = jnp.concatenate([sums[0][:, 0:384], middle, shifted[:, 128:512]], axis=1)
        return mixed.astype(BF16)

    lat_sends = [resident(0), resident(1), resident(2)]
    lat_sends[0].wait()
    lat_sends[1].wait()
    load_wv.wait()
    values(0)
    gather_send(0, 0)

    for cp in slice_sends:
        cp.wait()
    keys_sib = remote(k8.at[c], k8.at[c], sib_s.at[5], sib_r.at[5], sib)
    keys_sib.start()
    lat_sends.append(resident(3))
    gather_wait(0, 0)
    gather_send(0, 1)

    for cp in ask_z:
        cp.wait()
    keys_sib.wait()
    keys = k8[...].reshape(2 * 16 * TOK, WIDE)
    q = q8[...].reshape(4 * TIGHT, WIDE)
    flag = (lax.broadcasted_iota(jnp.int32, (8, WIDE), 1) == KV + ROPE).astype(BF16)
    present = nt(flag, keys)[0:1] > 0.5
    s = jnp.where(present, nt(q, keys), LOWEST)
    m = jnp.max(s, axis=1, keepdims=True)
    e = jnp.exp((s - m) * SCALE)
    total = jnp.sum(e, axis=1, keepdims=True)
    o = nn(e.astype(BF16), keys[:, 0:KV])
    lane = lax.broadcasted_iota(jnp.int32, (4 * TIGHT, 128), 1)
    stats = jnp.zeros((4 * TIGHT, 128), F32)
    for n, rest in enumerate((m, total)):
        for t in range(3):
            piece = rest.astype(BF16).astype(F32)
            rest = rest - piece
            stats = jnp.where(lane == 3 * n + t, piece, stats)
    o8_send[...] = jnp.concatenate([o, stats], axis=1).astype(BF16).reshape(4, TIGHT, WIDE)
    part_z = []
    for i in (2, 1, 3):
        to = (z + i) % 4
        cp = remote(o8_send.at[to], o8.at[z], z_s.at[3 + i], z_r.at[3 + i], (g, 2 * to + c))
        cp.start()
        part_z.append(cp)
    o8[z] = o8_send[z]

    lat_sends[2].wait()
    lat_sends[3].wait()
    values(1)
    gather_send(1, 0)

    q = q8_mine[:, 0 : KV + ROPE]
    recent = lat[8].astype(BF16)
    s_new = jnp.where(step_mask(TIGHT, 16, STEPS), nt(q, recent), LOWEST)
    m_new = jnp.max(s_new, axis=1, keepdims=True)
    e_new = jnp.exp((s_new - m_new) * SCALE)
    total_new = jnp.sum(e_new, axis=1, keepdims=True)
    o_new = nn(e_new.astype(BF16), recent[:, 0:KV])
    gather_wait(1, 0)
    gather_send(1, 1)
    for cp in part_z:
        cp.wait()
    m_part, total_part = [], []
    for i in range(4):
        st = o8[i][:, KV:WIDE].astype(F32)
        m_part.append(st[:, 0:1] + st[:, 1:2] + st[:, 2:3])
        total_part.append(st[:, 3:4] + st[:, 4:5] + st[:, 5:6])
    m = m_new
    for one in m_part:
        m = jnp.maximum(m, one)
    weight = jnp.exp((m_new - m) * SCALE)
    o = o_new * weight
    total = total_new * weight
    for i in range(4):
        weight = jnp.exp((m_part[i] - m) * SCALE)
        o = o + o8[i][:, 0:KV].astype(F32) * weight
        total = total + total_part[i] * weight
    loose = (lax.broadcasted_iota(jnp.int32, (ASK, TIGHT), 0), lax.broadcasted_iota(jnp.int32, (ASK, TIGHT), 1))
    loose = jnp.where((loose[0] // PAD == loose[1] // STEPS) & (loose[0] % PAD == loose[1] % STEPS), 1.0, 0.0)
    lt[8] = nn(loose.astype(BF16), (o / total).astype(BF16)).astype(BF16)
    values(2)
    gather_send(2, 0)

    to_row = lax.broadcasted_iota(jnp.int32, (256, 256), 0)
    from_row = lax.broadcasted_iota(jnp.int32, (256, 256), 1)
    for b in range(4):
        back = (to_row // 16 == from_row // 16) & (from_row % 16 == to_row % 16 + 4 * b) & (to_row % 16 < 4)
        unpack_new[b] = jnp.where(back, 1.0, 0.0).astype(BF16)

    load_wo.wait()
    gather_wait(0, 1)
    swap = project(0)
    gather_wait(2, 0)
    gather_send(2, 1)
    add_cores(0, swap)
    hand_out(0)
    gather_wait(1, 1)
    add_cores(1, project(1))
    hand_out(1)
    gather_wait(2, 1)
    add_cores(2, project(2))
    hand_out(2)
    sums = [take_in(0), take_in(1), take_in(2)]

    to_row = lax.broadcasted_iota(jnp.int32, (16 * STEPS, 48), 0)
    from_row = lax.broadcasted_iota(jnp.int32, (16 * STEPS, 48), 1)
    r = to_row % 16
    source = jnp.where(r >= ROWS, 32, r // 2 % 2 * 16 + (r // 4 * 2 + r % 2) * STEPS) + to_row // 16
    order = jnp.where(source == from_row, 1.0, 0.0).astype(BF16)
    mixed = nn(order, jnp.concatenate(sums, axis=0)).astype(BF16)
    for t in range(STEPS):
        out[t] = mixed[16 * t : 16 * t + ROWS + 1]

    for part in (0, 1, 2):
        for i in range(8):
            pl.when(jnp.logical_or(8 * c + i // 4 * 4 + (x + FAR[i % 4]) % 4 != g, keeper != h))(hand(part, i).wait_send)
    for cp in ag_sends:
        cp.wait_send()


def body(resident_cache, lengths, slices, placement, queries, latents, w_key, w_value, w_out):
    vmem = pl.BlockSpec(memory_space=pltpu.VMEM)
    smem = pl.BlockSpec(memory_space=pltpu.SMEM)
    anywhere = pl.BlockSpec(memory_space=pl.ANY)
    sems = pltpu.SemaphoreType.DMA
    out = pl.pallas_call(
        kernel,
        out_shape=jax.ShapeDtypeStruct((STEPS, ROWS + 1, 896), BF16),
        in_specs=[smem, smem] + [anywhere] * 7,
        out_specs=vmem,
        scratch_shapes=[
            pltpu.VMEM((4, KV + ROPE, LRES), BF16),
            pltpu.VMEM((HEADS, NOPE, KV), BF16),
            pltpu.VMEM((HEADS, KV, VD), BF16),
            pltpu.VMEM((512, HEADS * VD), BF16),
            pltpu.VMEM((16, TOK, KV + ROPE), BF16),
            pltpu.VMEM((16 * TOK, WIDE), BF16),
            pltpu.VMEM((16, TOK, WIDE), BF16),
            pltpu.VMEM((ROWS + 1, STEPS, HEADS * 192), BF16),
            pltpu.VMEM((ROWS + 1, STEPS, KV + ROPE), BF16),
            pltpu.VMEM((ROWS + 1, 8, HEADS * 192), F32),
            pltpu.VMEM((ROWS + 1, 16, KV + ROPE), F32),
            pltpu.VMEM((ROWS + 1, ASK, WIDE), BF16),
            pltpu.VMEM((4, ASK, WIDE), BF16),
            pltpu.VMEM((TIGHT, WIDE), BF16),
            pltpu.VMEM((4, TIGHT, WIDE), BF16),
            pltpu.VMEM((2, 16 * TOK, WIDE), BF16),
            pltpu.VMEM((4, ASK, KV), BF16),
            pltpu.VMEM((ROWS + 1, ASK, KV), BF16),
            pltpu.VMEM((4, TIGHT, WIDE), BF16),
            pltpu.VMEM((4, TIGHT, WIDE), BF16),
            pltpu.VMEM((2, 16, 16, WIDTH[0]), BF16),
            pltpu.VMEM((2, 16, 16, WIDTH[1]), BF16),
            pltpu.VMEM((2, 16, 16, WIDTH[2]), BF16),
            pltpu.VMEM((256, 768), BF16),
            pltpu.VMEM((4, 256, 256), BF16),
            pltpu.VMEM((3, 16, 16, 512), F32),
            pltpu.VMEM((3, 8, 16, 512), BF16),
            pltpu.VMEM((3, 8, 16, 512), BF16),
            pltpu.VMEM((3, 8, 16, 512), BF16),
            pltpu.VMEM((3, 8, 16, 512), BF16),
            sems((10,)),
            sems((9,)),
            sems((9,)),
            sems((16,)),
            sems((16,)),
            sems((7,)),
            sems((7,)),
            sems((48,)),
            sems((48,)),
            sems((24,)),
            sems((24,)),
        ],
        compiler_params=pltpu.CompilerParams(
            collective_id=0, has_side_effects=True, vmem_limit_bytes=56 * 1024 * 1024
        ),
        name="decode",
    )(
        lengths,
        placement.reshape(1, 16),
        jnp.swapaxes(queries[:, 0], 0, 1),
        jnp.swapaxes(latents[:, 0], 0, 1),
        jnp.swapaxes(resident_cache[0], 1, 2),
        slices,
        w_key,
        w_value,
        jnp.swapaxes(w_out, 0, 1),
    )
    return out[:, None]


def solution(mesh):
    placed = (
        P("grp", None, None, None),
        P("grp", None),
        P("grp", None, None),
        P("grp", None),
        P(None, "grp", None, "head"),
        P(None, "grp", None, None),
        P("head", None, None),
        P("head", None, None),
        P("head", "grp"),
    )
    return jax.shard_map(
        body, mesh=mesh, in_specs=placed, out_specs=P(None, "grp", None, "head"), check_vma=False
    )
```

```python
import math

import jax
import jax.numpy as jnp
from jax import lax
from jax.experimental import pallas as pl
from jax.experimental.pallas import tpu as pltpu
from jax.sharding import PartitionSpec as P

KV = 512
ROPE = 64
NOPE = 128
VD = 128
ROWS = 8
LRES = 1536
SL = 64
CAP = 2
STEPS = 3

MESH = pl.DeviceIdType.MESH
SCALE = 1.0 / math.sqrt(NOPE + ROPE)
LOWEST = -3.0e38
BF16 = jnp.bfloat16
F32 = jnp.float32
WIDE = 640
PAD = 4
HEADS = 16
ASK = HEADS * PAD
WIDTH = (768, 1024)
TIGHT = HEADS * STEPS
FAR = (2, 1, 3, 0)
TOK = 16


def remote(src, dst, send_sem, recv_sem, dev):
    return pltpu.make_async_remote_copy(
        src_ref=src, dst_ref=dst, send_sem=send_sem, recv_sem=recv_sem, device_id=dev, device_id_type=MESH
    )


def nt(a, b):
    return lax.dot_general(a, b, (((1,), (1,)), ((), ())), preferred_element_type=F32)


def nn(a, b):
    return jnp.dot(a, b, preferred_element_type=F32)


def step_mask(rows, width, steps=PAD):
    step = lax.broadcasted_iota(jnp.int32, (rows, width), 0) % steps
    at = lax.broadcasted_iota(jnp.int32, (rows, width), 1)
    return (at < STEPS) & (at <= step)


def kernel(
    lengths, placement, queries, latents, cache, slices, w_key, w_value, w_out,
    out,
    kt, wk, wv, wo, sl, slw, k_send, qv, lv, qf, lat,
    q_all, q_sib, q8_mine, q8, k8, o_sib, lt, o8_send, o8,
    gath_a, gath_b, unpack, p_all, p_send, p_recv, p_sum, red,
    dma, sib_s, sib_r, sl_s, sl_r, z_s, z_r, ag_s, ag_r, red_s, red_r,
):
    g = lax.axis_index("grp")
    h = lax.axis_index("head")
    y, x = g // 4, g % 4
    z, c = h // 2, h % 2
    sib = (g, h + 1 - 2 * c)
    gath = (gath_a, gath_b)

    load_sl = pltpu.make_async_copy(slices.at[:, pl.ds(TOK * z, TOK), :], sl, dma.at[1])
    load_qv = pltpu.make_async_copy(queries, qv, dma.at[8])
    load_lv = pltpu.make_async_copy(latents, lv, dma.at[9])
    load_wk = pltpu.make_async_copy(w_key, wk, dma.at[0])
    load_kt = [pltpu.make_async_copy(cache.at[4 * c + i], kt.at[i], dma.at[2 + i]) for i in range(4)]
    load_wv = pltpu.make_async_copy(w_value, wv, dma.at[6])
    load_wo = pltpu.make_async_copy(w_out, wo.at[0:448], dma.at[7])
    load_qv.start()
    load_lv.start()
    load_wk.start()
    load_sl.start()
    load_kt[0].start()

    barrier = pltpu.get_barrier_semaphore()
    offsets = sorted(
        ((dy, dx) for dy in range(4) for dx in range(4) if dy or dx),
        key=lambda o: -min(o[0], 4 - o[0]) - min(o[1], 4 - o[1]),
    )

    def group_at(dy, dx):
        return (y + dy) % 4 * 4 + (x + dx) % 4

    for dy, dx in offsets:
        pl.semaphore_signal(barrier, inc=1, device_id=(group_at(dy, dx), h), device_id_type=MESH)
    for i in (2, 1, 3):
        pl.semaphore_signal(barrier, inc=1, device_id=(g, 2 * ((z + i) % 4) + c), device_id_type=MESH)
    pl.semaphore_signal(barrier, inc=1, device_id=sib, device_id_type=MESH)

    qf[...] = jnp.zeros_like(qf)
    lat[...] = jnp.zeros_like(lat)
    load_qv.wait()
    load_lv.wait()
    for r in range(ROWS + 1):
        v = qv[r].astype(F32)
        qf[r, 0:STEPS, :] = v
        qf[r, PAD : PAD + STEPS, :] = v
        lat[r, 0:STEPS, :] = lv[r].astype(F32)

    load_wk.wait()
    load_kt[1].start()
    load_wv.start()
    row = lax.broadcasted_iota(jnp.int32, (72, 128), 0)
    lane = lax.broadcasted_iota(jnp.int32, (72, 128), 1)
    first = row % 8 < PAD
    low = lane < ROPE
    for quad in range(4):
        parts = []
        for p in (2 * quad, 2 * quad + 1):
            t = qf[:, :, 384 * p : 384 * p + 384].reshape(72, 384)
            t0, t1, t2 = t[:, 0:128], t[:, 128:256], t[:, 256:384]
            r1, r2 = pltpu.roll(t1, 64, 1), pltpu.roll(t2, 64, 1)
            second_nope = jnp.where(low, r1, r2)
            rope = jnp.where(low, jnp.where(first, t1, r2), 0.0)
            lhs = jnp.concatenate([jnp.where(first, t0, 0.0), jnp.where(first, 0.0, second_nope)], axis=1)
            absorbed = nn(lhs.astype(BF16), wk[2 * p : 2 * p + 2].reshape(2 * NOPE, KV))
            parts.append(jnp.concatenate([absorbed, rope], axis=1).reshape(9, 8, WIDE))
        q_all[:, 16 * quad : 16 * quad + 16, :] = jnp.concatenate(parts, axis=1).astype(BF16)

    owners = [placement[0, i] for i in range(16)]
    owner_of_lane = lax.broadcasted_iota(jnp.int32, (8, 16 * TOK), 1) // TOK
    code = jnp.zeros((8, 16 * TOK), jnp.int32)
    for i in range(16):
        rank = jnp.int32(0)
        for j in range(i):
            rank = rank + jnp.where(owners[j] == owners[i], 1, 0)
        code = jnp.where(owner_of_lane == i, owners[i] * CAP + rank, code)

    slw[:, KV:WIDE] = jnp.ones((16 * TOK, WIDE - KV), BF16)
    at0 = lax.broadcasted_iota(jnp.int32, (16 * TOK, 16 * TOK), 0)
    at1 = lax.broadcasted_iota(jnp.int32, (16 * TOK, 16 * TOK), 1)
    chosen = (at0 % TOK == at1 % TOK) & ((at0 // TOK) * CAP + c == code[0:1, :])
    selector = jnp.where(chosen, 1.0, 0.0).astype(BF16)
    load_sl.wait()
    slw[:, 0 : KV + ROPE] = sl[...].reshape(16 * TOK, KV + ROPE)
    k_send[...] = nn(selector, slw[...]).astype(BF16).reshape(16, TOK, WIDE)

    wo[448:512, :] = jnp.zeros((64, 2048), BF16)
    to_row = lax.broadcasted_iota(jnp.int32, (256, 256), 0)
    from_row = lax.broadcasted_iota(jnp.int32, (256, 256), 1)
    for b in range(3):
        back = (to_row // 16 == from_row // 16) & (to_row % 16 == from_row % 16 - 12 + 4 * b) & (from_row % 16 >= 12)
        unpack[:, 256 * b : 256 * b + 256] = jnp.where(back, 1.0, 0.0).astype(BF16)

    tight = (lax.broadcasted_iota(jnp.int32, (TIGHT, ASK), 0), lax.broadcasted_iota(jnp.int32, (TIGHT, ASK), 1))
    tight = jnp.where((tight[0] // STEPS == tight[1] // PAD) & (tight[0] % STEPS == tight[1] % PAD), 1.0, 0.0)
    q8_mine[...] = nn(tight.astype(BF16), q_all[8]).astype(BF16)

    pl.semaphore_wait(barrier, 19)

    ask_sib = remote(q_all.at[pl.ds(4 * (1 - c), 4)], q_sib, sib_s.at[0], sib_r.at[0], sib)
    ask_sib.start()

    slice_sends = []
    for i, (dy, dx) in enumerate(offsets):
        to = group_at(dy, dx)
        cp = remote(k_send.at[to], k8.at[c, pl.ds(TOK * g, TOK)], sl_s.at[i], sl_r.at[i], (to, h))
        cp.start()
        slice_sends.append(cp)
    k8[c, pl.ds(TOK * g, TOK), :] = k_send[g]

    ask_z = []
    for i in (2, 1, 3):
        to = (z + i) % 4
        cp = remote(q8_mine, q8.at[z], z_s.at[i], z_r.at[i], (g, 2 * to + c))
        cp.start()
        ask_z.append(cp)
    q8[z] = q8_mine[...]

    ask_sib.wait()

    recent_ok = step_mask(2 * ASK, 16)

    def resident(i):
        load_kt[i].wait()
        if i == 0:
            load_kt[2].start()
        if i == 1:
            load_kt[3].start()
            load_wo.start()
        q = jnp.concatenate([q_all[4 * c + i], q_sib[i]], axis=0)[:, 0 : KV + ROPE]
        recent = lat[4 * c + i].astype(BF16)
        s = nn(q, kt[i])
        s_new = jnp.where(recent_ok, nt(q, recent), LOWEST)
        ok = lax.broadcasted_iota(jnp.int32, (1, LRES), 1) < lengths[0, 4 * c + i]
        s = jnp.where(ok, s, LOWEST)
        m = jnp.maximum(jnp.max(s, axis=1, keepdims=True), jnp.max(s_new, axis=1, keepdims=True))
        e = jnp.exp((s - m) * SCALE)
        e_new = jnp.exp((s_new - m) * SCALE)
        total = jnp.sum(e, axis=1, keepdims=True) + jnp.sum(e_new, axis=1, keepdims=True)
        o = nt(e.astype(BF16), kt[i, 0:KV, :]) + nn(e_new.astype(BF16), recent[:, 0:KV])
        o = (o / total).astype(BF16)
        at = (i // 2) * 4 + c * 2 + i % 2
        lt[at] = o[0:ASK]
        o_sib[i] = o[ASK:]
        cp = remote(o_sib.at[i], lt.at[at], sib_s.at[1 + i], sib_r.at[1 + i], sib)
        cp.start()
        return cp

    def values(part):
        lo, count = (0, 4) if part == 0 else (4, 5)
        rows = 16 * count
        head_of_row = lax.broadcasted_iota(jnp.int32, (rows, 512), 0) % 16 // PAD
        head_of_lane = lax.broadcasted_iota(jnp.int32, (rows, 512), 1) // VD
        mine = head_of_row == head_of_lane
        heads_out = []
        for quad in range(4):
            lhs = lt[lo : lo + count, 16 * quad : 16 * quad + 16, :].reshape(rows, KV)
            rhs = jnp.concatenate([wv[4 * quad + j] for j in range(4)], axis=1)
            heads_out.append(jnp.where(mine, nn(lhs, rhs), 0.0).astype(BF16))
        to_row = lax.broadcasted_iota(jnp.int32, (16, rows), 0)
        from_row = lax.broadcasted_iota(jnp.int32, (16, rows), 1)

        def picks(at):
            return (at // STEPS == from_row // 16) & (at % STEPS == from_row % PAD)

        blocks = []
        if part == 0:
            direct = jnp.where((to_row < 12) & picks(to_row), 1.0, 0.0).astype(BF16)
            for b in range(3):
                under = jnp.where((to_row >= 12) & picks(4 * b + to_row - 12), 1.0, 0.0).astype(BF16)
                blocks.append(nn(direct, heads_out[b]) + nn(under, heads_out[3]))
        else:
            direct = jnp.where((to_row < 15) & picks(to_row), 1.0, 0.0).astype(BF16)
            for b in range(4):
                blocks.append(nn(direct, heads_out[b]))
        block = jnp.concatenate(blocks, axis=1).astype(BF16)
        half = WIDTH[part]
        gath[part][0, 4 * y + x] = block[:, 0:half]
        gath[part][1, 4 * x + y] = block[:, half:]

    ag_sends = []

    def along(axis, d):
        if axis == 0:
            return (4 * y + (x + d) % 4, h)
        return ((y + d) % 4 * 4 + x, h)

    def blocks_of(part, k, ring, d):
        one, two = (x, y) if k == 0 else (y, x)
        if ring == 0:
            return gath[part].at[k, pl.ds(4 * two + (one - d) % 4, 1)]
        return gath[part].at[k, pl.ds(4 * ((two - d) % 4), 4)]

    def gather_send(part, ring):
        for k in (0, 1):
            ref = blocks_of(part, k, ring, 0)
            for d in (2, 1, 3):
                n = ((part * 2 + k) * 2 + ring) * 4 + d
                cp = remote(ref, ref, ag_s.at[n], ag_r.at[n], along(ring if k == 0 else 1 - ring, d))
                cp.start()
                ag_sends.append(cp)

    def gather_wait(part, ring):
        for k in (0, 1):
            for d in (1, 3, 2):
                n = ((part * 2 + k) * 2 + ring) * 4 + d
                ref = blocks_of(part, k, ring, d)
                remote(ref, ref, ag_s.at[n], ag_r.at[n], along(ring if k == 0 else 1 - ring, d)).wait_recv()

    def one_block(part, k, d1, d2):
        one, two = (x, y) if k == 0 else (y, x)
        return gath[part].at[k, pl.ds(4 * ((two - d2) % 4) + (one - d1) % 4, 1)]

    def pass_on(part, k, d1):
        ref = one_block(part, k, d1, 0)
        for d in (2, 1, 3):
            n = 32 + (k * 4 + d1) * 4 + d
            cp = remote(ref, ref, ag_s.at[n], ag_r.at[n], along(1 - k, d))
            cp.start()
            ag_sends.append(cp)

    def gather_blocks(part):
        for d in (1, 3, 2):
            for k in (0, 1):
                n = ((part * 2 + k) * 2) * 4 + d
                ref = blocks_of(part, k, 0, d)
                remote(ref, ref, ag_s.at[n], ag_r.at[n], along(k, d)).wait_recv()
                pass_on(part, k, d)

    def gather_last(part):
        for k in (0, 1):
            for d1 in (0, 1, 3, 2):
                for d2 in (1, 3, 2):
                    n = 32 + (k * 4 + d1) * 4 + d2
                    ref = one_block(part, k, d1, d2)
                    remote(ref, ref, ag_s.at[n], ag_r.at[n], along(1 - k, d2)).wait_recv()

    def project(part):
        half = WIDTH[part]
        first_half = gath[part][0].reshape(256, half)
        second_half = jnp.concatenate([gath[part][1, 4 * (i % 4) + i // 4] for i in range(16)], axis=0)
        lhs = jnp.concatenate([first_half, second_half], axis=1)
        if part == 0:
            tall = jnp.concatenate([lhs[:, 512 * b : 512 * b + 512] for b in range(3)], axis=0)
            lhs = jnp.concatenate([lhs, nn(unpack[...], tall).astype(BF16)], axis=1)
        p_all[part] = nt(lhs, wo[...]).reshape(16, 16, 512)
        p_send[part] = p_all[part, pl.ds(8 * (1 - c), 8)].astype(BF16)
        cp = remote(p_send.at[part], p_recv.at[part], sib_s.at[6 + part], sib_r.at[6 + part], sib)
        cp.start()
        return cp

    def add_cores(part, cp):
        cp.wait()
        p_sum[part] = (p_all[part, pl.ds(8 * c, 8)] + p_recv[part].astype(F32)).astype(BF16)

    keeper = g // 2
    slot = (g % 2) * 4 + z

    def hand(part, i):
        return remote(
            p_sum.at[part, i // 4 * 4 + (x + FAR[i % 4]) % 4], red.at[part, slot], red_s.at[8 * part + i], red_r.at[8 * part + slot],
            (8 * c + i // 4 * 4 + (x + FAR[i % 4]) % 4, keeper),
        )

    def hand_out(part):
        for i in range(8):
            to = 8 * c + i // 4 * 4 + (x + FAR[i % 4]) % 4

            @pl.when(jnp.logical_or(to != g, keeper != h))
            def _():
                hand(part, i).start()

            @pl.when(jnp.logical_and(to == g, keeper == h))
            def _():
                red[part, slot] = p_sum[part, i // 4 * 4 + (x + FAR[i % 4]) % 4]

    def take_in(part):
        half_of = g // 8
        for j in range(2):
            for k in range(4):
                at = j * 4 + k

                @pl.when(jnp.logical_or(2 * h + j != g, 2 * k + half_of != h))
                def _():
                    remote(
                        p_sum.at[part, 0], red.at[part, at], red_s.at[0], red_r.at[8 * part + at], sib
                    ).wait_recv()

        sums = []
        for j in range(2):
            acc = red[part, 4 * j].astype(F32)
            for k in range(1, 4):
                acc = acc + red[part, 4 * j + k].astype(F32)
            sums.append(acc)
        shifted = pltpu.roll(sums[1], 64, 1)
        lane = lax.broadcasted_iota(jnp.int32, (16, 128), 1)
        middle = jnp.where(lane < 64, sums[0][:, 384:512], shifted[:, 0:128])
        mixed = jnp.concatenate([sums[0][:, 0:384], middle, shifted[:, 128:512]], axis=1)
        return mixed.astype(BF16)

    lat_sends = [resident(0), resident(1)]

    for cp in slice_sends:
        cp.wait()
    keys_sib = remote(k8.at[c], k8.at[c], sib_s.at[5], sib_r.at[5], sib)
    keys_sib.start()
    for cp in lat_sends:
        cp.wait()
    load_wv.wait()
    values(0)
    gather_send(0, 0)

    for cp in ask_z:
        cp.wait()
    keys_sib.wait()
    keys = k8[...].reshape(2 * 16 * TOK, WIDE)
    q = q8[...].reshape(4 * TIGHT, WIDE)
    flag = (lax.broadcasted_iota(jnp.int32, (8, WIDE), 1) == KV + ROPE).astype(BF16)
    present = nt(flag, keys)[0:1] > 0.5
    s = jnp.where(present, nt(q, keys), LOWEST)
    m = jnp.max(s, axis=1, keepdims=True)
    e = jnp.exp((s - m) * SCALE)
    total = jnp.sum(e, axis=1, keepdims=True)
    o = nn(e.astype(BF16), keys[:, 0:KV])
    lane = lax.broadcasted_iota(jnp.int32, (4 * TIGHT, 128), 1)
    stats = jnp.zeros((4 * TIGHT, 128), F32)
    for n, rest in enumerate((m, total)):
        for t in range(3):
            piece = rest.astype(BF16).astype(F32)
            rest = rest - piece
            stats = jnp.where(lane == 3 * n + t, piece, stats)
    o8_send[...] = jnp.concatenate([o, stats], axis=1).astype(BF16).reshape(4, TIGHT, WIDE)
    part_z = []
    for i in (2, 1, 3):
        to = (z + i) % 4
        cp = remote(o8_send.at[to], o8.at[z], z_s.at[3 + i], z_r.at[3 + i], (g, 2 * to + c))
        cp.start()
        part_z.append(cp)
    o8[z] = o8_send[z]

    lat_sends = [resident(2)]
    gather_wait(0, 0)
    gather_send(0, 1)
    lat_sends.append(resident(3))

    q = q8_mine[:, 0 : KV + ROPE]
    recent = lat[8].astype(BF16)
    s_new = jnp.where(step_mask(TIGHT, 16, STEPS), nt(q, recent), LOWEST)
    m_new = jnp.max(s_new, axis=1, keepdims=True)
    e_new = jnp.exp((s_new - m_new) * SCALE)
    total_new = jnp.sum(e_new, axis=1, keepdims=True)
    o_new = nn(e_new.astype(BF16), recent[:, 0:KV])
    for cp in part_z:
        cp.wait()
    m_part, total_part = [], []
    for i in range(4):
        st = o8[i][:, KV:WIDE].astype(F32)
        m_part.append(st[:, 0:1] + st[:, 1:2] + st[:, 2:3])
        total_part.append(st[:, 3:4] + st[:, 4:5] + st[:, 5:6])
    m = m_new
    for one in m_part:
        m = jnp.maximum(m, one)
    weight = jnp.exp((m_new - m) * SCALE)
    o = o_new * weight
    total = total_new * weight
    for i in range(4):
        weight = jnp.exp((m_part[i] - m) * SCALE)
        o = o + o8[i][:, 0:KV].astype(F32) * weight
        total = total + total_part[i] * weight
    loose = (lax.broadcasted_iota(jnp.int32, (ASK, TIGHT), 0), lax.broadcasted_iota(jnp.int32, (ASK, TIGHT), 1))
    loose = jnp.where((loose[0] // PAD == loose[1] // STEPS) & (loose[0] % PAD == loose[1] % STEPS), 1.0, 0.0)
    lt[8] = nn(loose.astype(BF16), (o / total).astype(BF16)).astype(BF16)
    for cp in lat_sends:
        cp.wait()
    values(1)
    gather_send(1, 0)
    for k in (0, 1):
        pass_on(1, k, 0)
    gather_blocks(1)

    load_wo.wait()
    gather_wait(0, 1)
    swap = project(0)
    add_cores(0, swap)
    hand_out(0)
    gather_last(1)
    swap = project(1)
    add_cores(1, swap)
    hand_out(1)
    sums_a = take_in(0)
    sums_b = take_in(1)

    to_row = lax.broadcasted_iota(jnp.int32, (16 * STEPS, 32), 0)
    from_row = lax.broadcasted_iota(jnp.int32, (16 * STEPS, 32), 1)
    r = to_row % 16
    source = jnp.where(r >= ROWS, 16 + 4 * STEPS, r // 2 % 2 * 16 + (r // 4 * 2 + r % 2) * STEPS) + to_row // 16
    order = jnp.where(source == from_row, 1.0, 0.0).astype(BF16)
    mixed = nn(order, jnp.concatenate([sums_a, sums_b], axis=0)).astype(BF16)
    for t in range(STEPS):
        out[t] = mixed[16 * t : 16 * t + ROWS + 1]

    for part in (0, 1):
        for i in range(8):
            pl.when(jnp.logical_or(8 * c + i // 4 * 4 + (x + FAR[i % 4]) % 4 != g, keeper != h))(hand(part, i).wait_send)
    for cp in ag_sends:
        cp.wait_send()


def body(resident_cache, lengths, slices, placement, queries, latents, w_key, w_value, w_out):
    vmem = pl.BlockSpec(memory_space=pltpu.VMEM)
    smem = pl.BlockSpec(memory_space=pltpu.SMEM)
    anywhere = pl.BlockSpec(memory_space=pl.ANY)
    sems = pltpu.SemaphoreType.DMA
    out = pl.pallas_call(
        kernel,
        out_shape=jax.ShapeDtypeStruct((STEPS, ROWS + 1, 896), BF16),
        in_specs=[smem, smem] + [anywhere] * 7,
        out_specs=vmem,
        scratch_shapes=[
            pltpu.VMEM((4, KV + ROPE, LRES), BF16),
            pltpu.VMEM((HEADS, NOPE, KV), BF16),
            pltpu.VMEM((HEADS, KV, VD), BF16),
            pltpu.VMEM((512, HEADS * VD), BF16),
            pltpu.VMEM((16, TOK, KV + ROPE), BF16),
            pltpu.VMEM((16 * TOK, WIDE), BF16),
            pltpu.VMEM((16, TOK, WIDE), BF16),
            pltpu.VMEM((ROWS + 1, STEPS, HEADS * 192), BF16),
            pltpu.VMEM((ROWS + 1, STEPS, KV + ROPE), BF16),
            pltpu.VMEM((ROWS + 1, 8, HEADS * 192), F32),
            pltpu.VMEM((ROWS + 1, 16, KV + ROPE), F32),
            pltpu.VMEM((ROWS + 1, ASK, WIDE), BF16),
            pltpu.VMEM((4, ASK, WIDE), BF16),
            pltpu.VMEM((TIGHT, WIDE), BF16),
            pltpu.VMEM((4, TIGHT, WIDE), BF16),
            pltpu.VMEM((2, 16 * TOK, WIDE), BF16),
            pltpu.VMEM((4, ASK, KV), BF16),
            pltpu.VMEM((ROWS + 1, ASK, KV), BF16),
            pltpu.VMEM((4, TIGHT, WIDE), BF16),
            pltpu.VMEM((4, TIGHT, WIDE), BF16),
            pltpu.VMEM((2, 16, 16, WIDTH[0]), BF16),
            pltpu.VMEM((2, 16, 16, WIDTH[1]), BF16),
            pltpu.VMEM((256, 768), BF16),
            pltpu.VMEM((2, 16, 16, 512), F32),
            pltpu.VMEM((2, 8, 16, 512), BF16),
            pltpu.VMEM((2, 8, 16, 512), BF16),
            pltpu.VMEM((2, 8, 16, 512), BF16),
            pltpu.VMEM((2, 8, 16, 512), BF16),
            sems((10,)),
            sems((8,)),
            sems((8,)),
            sems((16,)),
            sems((16,)),
            sems((7,)),
            sems((7,)),
            sems((64,)),
            sems((64,)),
            sems((16,)),
            sems((16,)),
        ],
        compiler_params=pltpu.CompilerParams(
            collective_id=0, has_side_effects=True, vmem_limit_bytes=56 * 1024 * 1024
        ),
        name="decode",
    )(
        lengths,
        placement.reshape(1, 16),
        jnp.swapaxes(queries[:, 0], 0, 1),
        jnp.swapaxes(latents[:, 0], 0, 1),
        jnp.swapaxes(resident_cache[0], 1, 2),
        slices,
        w_key,
        w_value,
        jnp.swapaxes(w_out, 0, 1),
    )
    return out[:, None]


def solution(mesh):
    placed = (
        P("grp", None, None, None),
        P("grp", None),
        P("grp", None, None),
        P("grp", None),
        P(None, "grp", None, "head"),
        P(None, "grp", None, None),
        P("head", None, None),
        P("head", None, None),
        P("head", "grp"),
    )
    return jax.shard_map(
        body, mesh=mesh, in_specs=placed, out_specs=P(None, "grp", None, "head"), check_vma=False
    )
```

```python
import math

import jax
import jax.numpy as jnp
from jax import lax
from jax.experimental import pallas as pl
from jax.experimental.pallas import tpu as pltpu
from jax.sharding import PartitionSpec as P

KV = 512
ROPE = 64
NOPE = 128
VD = 128
ROWS = 8
LRES = 1536
SL = 64
CAP = 2
STEPS = 3

MESH = pl.DeviceIdType.MESH
SCALE = 1.0 / math.sqrt(NOPE + ROPE)
LOWEST = -3.0e38
BF16 = jnp.bfloat16
F32 = jnp.float32
WIDE = 640
PAD = 4
HEADS = 16
ASK = HEADS * PAD
WIDTH = (768, 1024)
TIGHT = HEADS * STEPS
FAR = (2, 1, 3, 0)
TOK = 16


def remote(src, dst, send_sem, recv_sem, dev):
    return pltpu.make_async_remote_copy(
        src_ref=src, dst_ref=dst, send_sem=send_sem, recv_sem=recv_sem, device_id=dev, device_id_type=MESH
    )


def nt(a, b):
    return lax.dot_general(a, b, (((1,), (1,)), ((), ())), preferred_element_type=F32)


def nn(a, b):
    return jnp.dot(a, b, preferred_element_type=F32)


def step_mask(rows, width, steps=PAD):
    step = lax.broadcasted_iota(jnp.int32, (rows, width), 0) % steps
    at = lax.broadcasted_iota(jnp.int32, (rows, width), 1)
    return (at < STEPS) & (at <= step)


def kernel(
    lengths, placement, queries, latents, cache, slices, w_key, w_value, w_out,
    out,
    kt, wk, wv, wo, sl, slw, k_send, qv, lv, qf, lat,
    q_all, q_sib, q8_mine, q8, k8, o_sib, lt, o8_send, o8,
    gath_a, gath_b, unpack, p_all, p_send, p_recv, p_sum, red,
    dma, sib_s, sib_r, sl_s, sl_r, z_s, z_r, ag_s, ag_r, red_s, red_r,
):
    g = lax.axis_index("grp")
    h = lax.axis_index("head")
    y, x = g // 4, g % 4
    z, c = h // 2, h % 2
    sib = (g, h + 1 - 2 * c)
    gath = (gath_a, gath_b)

    load_sl = pltpu.make_async_copy(slices.at[:, pl.ds(TOK * z, TOK), :], sl, dma.at[1])
    load_qv = pltpu.make_async_copy(queries, qv, dma.at[8])
    load_lv = pltpu.make_async_copy(latents, lv, dma.at[9])
    load_wk = pltpu.make_async_copy(w_key, wk, dma.at[0])
    load_kt = [pltpu.make_async_copy(cache.at[4 * c + i], kt.at[i], dma.at[2 + i]) for i in range(4)]
    load_wv = pltpu.make_async_copy(w_value, wv, dma.at[6])
    load_wo = pltpu.make_async_copy(w_out, wo.at[0:448], dma.at[7])
    load_qv.start()
    load_wk.start()

    barrier = pltpu.get_barrier_semaphore()
    offsets = sorted(
        ((dy, dx) for dy in range(4) for dx in range(4) if dy or dx),
        key=lambda o: -min(o[0], 4 - o[0]) - min(o[1], 4 - o[1]),
    )

    def group_at(dy, dx):
        return (y + dy) % 4 * 4 + (x + dx) % 4

    for dy, dx in offsets:
        pl.semaphore_signal(barrier, inc=1, device_id=(group_at(dy, dx), h), device_id_type=MESH)
    for i in (2, 1, 3):
        pl.semaphore_signal(barrier, inc=1, device_id=(g, 2 * ((z + i) % 4) + c), device_id_type=MESH)
    pl.semaphore_signal(barrier, inc=1, device_id=sib, device_id_type=MESH)
    load_lv.start()
    load_sl.start()
    load_kt[0].start()

    qf[...] = jnp.zeros_like(qf)
    lat[...] = jnp.zeros_like(lat)
    load_qv.wait()
    load_lv.wait()
    for r in range(ROWS + 1):
        v = qv[r].astype(F32)
        qf[r, 0:STEPS, :] = v
        qf[r, PAD : PAD + STEPS, :] = v
        lat[r, 0:STEPS, :] = lv[r].astype(F32)

    load_wk.wait()
    load_kt[1].start()
    load_wv.start()
    row = lax.broadcasted_iota(jnp.int32, (72, 128), 0)
    lane = lax.broadcasted_iota(jnp.int32, (72, 128), 1)
    first = row % 8 < PAD
    low = lane < ROPE
    for quad in range(4):
        parts = []
        for p in (2 * quad, 2 * quad + 1):
            t = qf[:, :, 384 * p : 384 * p + 384].reshape(72, 384)
            t0, t1, t2 = t[:, 0:128], t[:, 128:256], t[:, 256:384]
            r1, r2 = pltpu.roll(t1, 64, 1), pltpu.roll(t2, 64, 1)
            second_nope = jnp.where(low, r1, r2)
            rope = jnp.where(low, jnp.where(first, t1, r2), 0.0)
            lhs = jnp.concatenate([jnp.where(first, t0, 0.0), jnp.where(first, 0.0, second_nope)], axis=1)
            absorbed = nn(lhs.astype(BF16), wk[2 * p : 2 * p + 2].reshape(2 * NOPE, KV))
            parts.append(jnp.concatenate([absorbed, rope], axis=1).reshape(9, 8, WIDE))
        q_all[:, 16 * quad : 16 * quad + 16, :] = jnp.concatenate(parts, axis=1).astype(BF16)

    owners = [placement[0, i] for i in range(16)]
    owner_of_lane = lax.broadcasted_iota(jnp.int32, (8, 16 * TOK), 1) // TOK
    code = jnp.zeros((8, 16 * TOK), jnp.int32)
    for i in range(16):
        rank = jnp.int32(0)
        for j in range(i):
            rank = rank + jnp.where(owners[j] == owners[i], 1, 0)
        code = jnp.where(owner_of_lane == i, owners[i] * CAP + rank, code)

    slw[:, KV:WIDE] = jnp.ones((16 * TOK, WIDE - KV), BF16)
    at0 = lax.broadcasted_iota(jnp.int32, (16 * TOK, 16 * TOK), 0)
    at1 = lax.broadcasted_iota(jnp.int32, (16 * TOK, 16 * TOK), 1)
    chosen = (at0 % TOK == at1 % TOK) & ((at0 // TOK) * CAP + c == code[0:1, :])
    selector = jnp.where(chosen, 1.0, 0.0).astype(BF16)
    load_sl.wait()
    slw[:, 0 : KV + ROPE] = sl[...].reshape(16 * TOK, KV + ROPE)
    k_send[...] = nn(selector, slw[...]).astype(BF16).reshape(16, TOK, WIDE)

    wo[448:512, :] = jnp.zeros((64, 2048), BF16)
    to_row = lax.broadcasted_iota(jnp.int32, (256, 256), 0)
    from_row = lax.broadcasted_iota(jnp.int32, (256, 256), 1)
    for b in range(3):
        back = (to_row // 16 == from_row // 16) & (to_row % 16 == from_row % 16 - 12 + 4 * b) & (from_row % 16 >= 12)
        unpack[:, 256 * b : 256 * b + 256] = jnp.where(back, 1.0, 0.0).astype(BF16)

    tight = (lax.broadcasted_iota(jnp.int32, (TIGHT, ASK), 0), lax.broadcasted_iota(jnp.int32, (TIGHT, ASK), 1))
    tight = jnp.where((tight[0] // STEPS == tight[1] // PAD) & (tight[0] % STEPS == tight[1] % PAD), 1.0, 0.0)
    q8_mine[...] = nn(tight.astype(BF16), q_all[8]).astype(BF16)

    pl.semaphore_wait(barrier, 19)

    ask_sib = remote(q_all.at[pl.ds(4 * (1 - c), 4)], q_sib, sib_s.at[0], sib_r.at[0], sib)
    ask_sib.start()

    slice_sends = []
    for i, (dy, dx) in enumerate(offsets):
        to = group_at(dy, dx)
        cp = remote(k_send.at[to], k8.at[c, pl.ds(TOK * g, TOK)], sl_s.at[i], sl_r.at[i], (to, h))
        cp.start()
        slice_sends.append(cp)
    k8[c, pl.ds(TOK * g, TOK), :] = k_send[g]

    ask_z = []
    for i in (2, 1, 3):
        to = (z + i) % 4
        cp = remote(q8_mine, q8.at[z], z_s.at[i], z_r.at[i], (g, 2 * to + c))
        cp.start()
        ask_z.append(cp)
    q8[z] = q8_mine[...]

    ask_sib.wait()

    recent_ok = step_mask(2 * ASK, 16)

    def resident(i):
        load_kt[i].wait()
        if i == 0:
            load_kt[2].start()
        if i == 1:
            load_kt[3].start()
            load_wo.start()
        q = jnp.concatenate([q_all[4 * c + i], q_sib[i]], axis=0)[:, 0 : KV + ROPE]
        recent = lat[4 * c + i].astype(BF16)
        s = nn(q, kt[i])
        s_new = jnp.where(recent_ok, nt(q, recent), LOWEST)
        ok = lax.broadcasted_iota(jnp.int32, (1, LRES), 1) < lengths[0, 4 * c + i]
        s = jnp.where(ok, s, LOWEST)
        m = jnp.maximum(jnp.max(s, axis=1, keepdims=True), jnp.max(s_new, axis=1, keepdims=True))
        e = jnp.exp((s - m) * SCALE)
        e_new = jnp.exp((s_new - m) * SCALE)
        total = jnp.sum(e, axis=1, keepdims=True) + jnp.sum(e_new, axis=1, keepdims=True)
        o = nt(e.astype(BF16), kt[i, 0:KV, :]) + nn(e_new.astype(BF16), recent[:, 0:KV])
        o = (o / total).astype(BF16)
        at = (i // 2) * 4 + c * 2 + i % 2
        lt[at] = o[0:ASK]
        o_sib[i] = o[ASK:]
        cp = remote(o_sib.at[i], lt.at[at], sib_s.at[1 + i], sib_r.at[1 + i], sib)
        cp.start()
        return cp

    def values(part):
        lo, count = (0, 4) if part == 0 else (4, 5)
        rows = 16 * count
        head_of_row = lax.broadcasted_iota(jnp.int32, (rows, 512), 0) % 16 // PAD
        head_of_lane = lax.broadcasted_iota(jnp.int32, (rows, 512), 1) // VD
        mine = head_of_row == head_of_lane
        heads_out = []
        for quad in range(4):
            lhs = lt[lo : lo + count, 16 * quad : 16 * quad + 16, :].reshape(rows, KV)
            rhs = jnp.concatenate([wv[4 * quad + j] for j in range(4)], axis=1)
            heads_out.append(jnp.where(mine, nn(lhs, rhs), 0.0).astype(BF16))
        to_row = lax.broadcasted_iota(jnp.int32, (16, rows), 0)
        from_row = lax.broadcasted_iota(jnp.int32, (16, rows), 1)

        def picks(at):
            return (at // STEPS == from_row // 16) & (at % STEPS == from_row % PAD)

        blocks = []
        if part == 0:
            direct = jnp.where((to_row < 12) & picks(to_row), 1.0, 0.0).astype(BF16)
            for b in range(3):
                under = jnp.where((to_row >= 12) & picks(4 * b + to_row - 12), 1.0, 0.0).astype(BF16)
                blocks.append(nn(direct, heads_out[b]) + nn(under, heads_out[3]))
        else:
            direct = jnp.where((to_row < 15) & picks(to_row), 1.0, 0.0).astype(BF16)
            for b in range(4):
                blocks.append(nn(direct, heads_out[b]))
        block = jnp.concatenate(blocks, axis=1).astype(BF16)
        half = WIDTH[part]
        gath[part][0, 4 * y + x] = block[:, 0:half]
        gath[part][1, 4 * x + y] = block[:, half:]

    ag_sends = []

    def along(axis, d):
        if axis == 0:
            return (4 * y + (x + d) % 4, h)
        return ((y + d) % 4 * 4 + x, h)

    def blocks_of(part, k, ring, d):
        one, two = (x, y) if k == 0 else (y, x)
        if ring == 0:
            return gath[part].at[k, pl.ds(4 * two + (one - d) % 4, 1)]
        return gath[part].at[k, pl.ds(4 * ((two - d) % 4), 4)]

    def gather_send(part, ring):
        for k in (0, 1):
            ref = blocks_of(part, k, ring, 0)
            for d in (2, 1, 3):
                n = ((part * 2 + k) * 2 + ring) * 4 + d
                cp = remote(ref, ref, ag_s.at[n], ag_r.at[n], along(ring if k == 0 else 1 - ring, d))
                cp.start()
                ag_sends.append(cp)

    def gather_wait(part, ring):
        for k in (0, 1):
            for d in (1, 3, 2):
                n = ((part * 2 + k) * 2 + ring) * 4 + d
                ref = blocks_of(part, k, ring, d)
                remote(ref, ref, ag_s.at[n], ag_r.at[n], along(ring if k == 0 else 1 - ring, d)).wait_recv()

    def one_block(part, k, d1, d2):
        one, two = (x, y) if k == 0 else (y, x)
        return gath[part].at[k, pl.ds(4 * ((two - d2) % 4) + (one - d1) % 4, 1)]

    def pass_on(part, k, d1):
        ref = one_block(part, k, d1, 0)
        for d in (2, 1, 3):
            n = 32 + (k * 4 + d1) * 4 + d
            cp = remote(ref, ref, ag_s.at[n], ag_r.at[n], along(1 - k, d))
            cp.start()
            ag_sends.append(cp)

    def gather_blocks(part):
        for d in (1, 3, 2):
            for k in (0, 1):
                n = ((part * 2 + k) * 2) * 4 + d
                ref = blocks_of(part, k, 0, d)
                remote(ref, ref, ag_s.at[n], ag_r.at[n], along(k, d)).wait_recv()
                pass_on(part, k, d)

    def gather_last(part):
        for k in (0, 1):
            for d1 in (0, 1, 3, 2):
                for d2 in (1, 3, 2):
                    n = 32 + (k * 4 + d1) * 4 + d2
                    ref = one_block(part, k, d1, d2)
                    remote(ref, ref, ag_s.at[n], ag_r.at[n], along(1 - k, d2)).wait_recv()

    def project(part):
        half = WIDTH[part]
        first_half = gath[part][0].reshape(256, half)
        second_half = jnp.concatenate([gath[part][1, 4 * (i % 4) + i // 4] for i in range(16)], axis=0)
        lhs = jnp.concatenate([first_half, second_half], axis=1)
        if part == 0:
            tall = jnp.concatenate([lhs[:, 512 * b : 512 * b + 512] for b in range(3)], axis=0)
            lhs = jnp.concatenate([lhs, nn(unpack[...], tall).astype(BF16)], axis=1)
        p_all[part] = nt(lhs, wo[...]).reshape(16, 16, 512)
        p_send[part] = p_all[part, pl.ds(8 * (1 - c), 8)].astype(BF16)
        cp = remote(p_send.at[part], p_recv.at[part], sib_s.at[6 + part], sib_r.at[6 + part], sib)
        cp.start()
        return cp

    def add_cores(part, cp):
        cp.wait()
        p_sum[part] = (p_all[part, pl.ds(8 * c, 8)] + p_recv[part].astype(F32)).astype(BF16)

    keeper = g // 2
    slot = (g % 2) * 4 + z

    def hand(part, i):
        return remote(
            p_sum.at[part, i // 4 * 4 + (x + FAR[i % 4]) % 4], red.at[part, slot], red_s.at[8 * part + i], red_r.at[8 * part + slot],
            (8 * c + i // 4 * 4 + (x + FAR[i % 4]) % 4, keeper),
        )

    def hand_out(part):
        for i in range(8):
            to = 8 * c + i // 4 * 4 + (x + FAR[i % 4]) % 4

            @pl.when(jnp.logical_or(to != g, keeper != h))
            def _():
                hand(part, i).start()

            @pl.when(jnp.logical_and(to == g, keeper == h))
            def _():
                red[part, slot] = p_sum[part, i // 4 * 4 + (x + FAR[i % 4]) % 4]

    def take_in(part):
        half_of = g // 8
        for j in range(2):
            for k in range(4):
                at = j * 4 + k

                @pl.when(jnp.logical_or(2 * h + j != g, 2 * k + half_of != h))
                def _():
                    remote(
                        p_sum.at[part, 0], red.at[part, at], red_s.at[0], red_r.at[8 * part + at], sib
                    ).wait_recv()

        sums = []
        for j in range(2):
            acc = red[part, 4 * j].astype(F32)
            for k in range(1, 4):
                acc = acc + red[part, 4 * j + k].astype(F32)
            sums.append(acc)
        shifted = pltpu.roll(sums[1], 64, 1)
        lane = lax.broadcasted_iota(jnp.int32, (16, 128), 1)
        middle = jnp.where(lane < 64, sums[0][:, 384:512], shifted[:, 0:128])
        mixed = jnp.concatenate([sums[0][:, 0:384], middle, shifted[:, 128:512]], axis=1)
        return mixed.astype(BF16)

    lat_sends = [resident(0), resident(1)]

    for cp in slice_sends:
        cp.wait()
    keys_sib = remote(k8.at[c], k8.at[c], sib_s.at[5], sib_r.at[5], sib)
    keys_sib.start()
    for cp in lat_sends:
        cp.wait()
    load_wv.wait()
    values(0)
    gather_send(0, 0)

    for cp in ask_z:
        cp.wait()
    keys_sib.wait()
    keys = k8[...].reshape(2 * 16 * TOK, WIDE)
    q = q8[...].reshape(4 * TIGHT, WIDE)
    flag = (lax.broadcasted_iota(jnp.int32, (8, WIDE), 1) == KV + ROPE).astype(BF16)
    present = nt(flag, keys)[0:1] > 0.5
    s = jnp.where(present, nt(q, keys), LOWEST)
    m = jnp.max(s, axis=1, keepdims=True)
    e = jnp.exp((s - m) * SCALE)
    total = jnp.sum(e, axis=1, keepdims=True)
    o = nn(e.astype(BF16), keys[:, 0:KV])
    lane = lax.broadcasted_iota(jnp.int32, (4 * TIGHT, 128), 1)
    stats = jnp.zeros((4 * TIGHT, 128), F32)
    for n, rest in enumerate((m, total)):
        for t in range(3):
            piece = rest.astype(BF16).astype(F32)
            rest = rest - piece
            stats = jnp.where(lane == 3 * n + t, piece, stats)
    o8_send[...] = jnp.concatenate([o, stats], axis=1).astype(BF16).reshape(4, TIGHT, WIDE)
    part_z = []
    for i in (2, 1, 3):
        to = (z + i) % 4
        cp = remote(o8_send.at[to], o8.at[z], z_s.at[3 + i], z_r.at[3 + i], (g, 2 * to + c))
        cp.start()
        part_z.append(cp)
    o8[z] = o8_send[z]

    lat_sends = [resident(2)]
    gather_wait(0, 0)
    gather_send(0, 1)
    lat_sends.append(resident(3))

    q = q8_mine[:, 0 : KV + ROPE]
    recent = lat[8].astype(BF16)
    s_new = jnp.where(step_mask(TIGHT, 16, STEPS), nt(q, recent), LOWEST)
    m_new = jnp.max(s_new, axis=1, keepdims=True)
    e_new = jnp.exp((s_new - m_new) * SCALE)
    total_new = jnp.sum(e_new, axis=1, keepdims=True)
    o_new = nn(e_new.astype(BF16), recent[:, 0:KV])
    for cp in part_z:
        cp.wait()
    m_part, total_part = [], []
    for i in range(4):
        st = o8[i][:, KV:WIDE].astype(F32)
        m_part.append(st[:, 0:1] + st[:, 1:2] + st[:, 2:3])
        total_part.append(st[:, 3:4] + st[:, 4:5] + st[:, 5:6])
    m = m_new
    for one in m_part:
        m = jnp.maximum(m, one)
    weight = jnp.exp((m_new - m) * SCALE)
    o = o_new * weight
    total = total_new * weight
    for i in range(4):
        weight = jnp.exp((m_part[i] - m) * SCALE)
        o = o + o8[i][:, 0:KV].astype(F32) * weight
        total = total + total_part[i] * weight
    loose = (lax.broadcasted_iota(jnp.int32, (ASK, TIGHT), 0), lax.broadcasted_iota(jnp.int32, (ASK, TIGHT), 1))
    loose = jnp.where((loose[0] // PAD == loose[1] // STEPS) & (loose[0] % PAD == loose[1] % STEPS), 1.0, 0.0)
    lt[8] = nn(loose.astype(BF16), (o / total).astype(BF16)).astype(BF16)
    for cp in lat_sends:
        cp.wait()
    values(1)
    gather_send(1, 0)
    for k in (0, 1):
        pass_on(1, k, 0)
    gather_blocks(1)

    load_wo.wait()
    gather_wait(0, 1)
    swap = project(0)
    add_cores(0, swap)
    hand_out(0)
    gather_last(1)
    swap = project(1)
    add_cores(1, swap)
    hand_out(1)
    sums_a = take_in(0)
    sums_b = take_in(1)

    to_row = lax.broadcasted_iota(jnp.int32, (16 * STEPS, 32), 0)
    from_row = lax.broadcasted_iota(jnp.int32, (16 * STEPS, 32), 1)
    r = to_row % 16
    source = jnp.where(r >= ROWS, 16 + 4 * STEPS, r // 2 % 2 * 16 + (r // 4 * 2 + r % 2) * STEPS) + to_row // 16
    order = jnp.where(source == from_row, 1.0, 0.0).astype(BF16)
    mixed = nn(order, jnp.concatenate([sums_a, sums_b], axis=0)).astype(BF16)
    for t in range(STEPS):
        out[t] = mixed[16 * t : 16 * t + ROWS + 1]

    for part in (0, 1):
        for i in range(8):
            pl.when(jnp.logical_or(8 * c + i // 4 * 4 + (x + FAR[i % 4]) % 4 != g, keeper != h))(hand(part, i).wait_send)
    for cp in ag_sends:
        cp.wait_send()


def body(resident_cache, lengths, slices, placement, queries, latents, w_key, w_value, w_out):
    vmem = pl.BlockSpec(memory_space=pltpu.VMEM)
    smem = pl.BlockSpec(memory_space=pltpu.SMEM)
    anywhere = pl.BlockSpec(memory_space=pl.ANY)
    sems = pltpu.SemaphoreType.DMA
    out = pl.pallas_call(
        kernel,
        out_shape=jax.ShapeDtypeStruct((STEPS, ROWS + 1, 896), BF16),
        in_specs=[smem, smem] + [anywhere] * 7,
        out_specs=vmem,
        scratch_shapes=[
            pltpu.VMEM((4, KV + ROPE, LRES), BF16),
            pltpu.VMEM((HEADS, NOPE, KV), BF16),
            pltpu.VMEM((HEADS, KV, VD), BF16),
            pltpu.VMEM((512, HEADS * VD), BF16),
            pltpu.VMEM((16, TOK, KV + ROPE), BF16),
            pltpu.VMEM((16 * TOK, WIDE), BF16),
            pltpu.VMEM((16, TOK, WIDE), BF16),
            pltpu.VMEM((ROWS + 1, STEPS, HEADS * 192), BF16),
            pltpu.VMEM((ROWS + 1, STEPS, KV + ROPE), BF16),
            pltpu.VMEM((ROWS + 1, 8, HEADS * 192), F32),
            pltpu.VMEM((ROWS + 1, 16, KV + ROPE), F32),
            pltpu.VMEM((ROWS + 1, ASK, WIDE), BF16),
            pltpu.VMEM((4, ASK, WIDE), BF16),
            pltpu.VMEM((TIGHT, WIDE), BF16),
            pltpu.VMEM((4, TIGHT, WIDE), BF16),
            pltpu.VMEM((2, 16 * TOK, WIDE), BF16),
            pltpu.VMEM((4, ASK, KV), BF16),
            pltpu.VMEM((ROWS + 1, ASK, KV), BF16),
            pltpu.VMEM((4, TIGHT, WIDE), BF16),
            pltpu.VMEM((4, TIGHT, WIDE), BF16),
            pltpu.VMEM((2, 16, 16, WIDTH[0]), BF16),
            pltpu.VMEM((2, 16, 16, WIDTH[1]), BF16),
            pltpu.VMEM((256, 768), BF16),
            pltpu.VMEM((2, 16, 16, 512), F32),
            pltpu.VMEM((2, 8, 16, 512), BF16),
            pltpu.VMEM((2, 8, 16, 512), BF16),
            pltpu.VMEM((2, 8, 16, 512), BF16),
            pltpu.VMEM((2, 8, 16, 512), BF16),
            sems((10,)),
            sems((8,)),
            sems((8,)),
            sems((16,)),
            sems((16,)),
            sems((7,)),
            sems((7,)),
            sems((64,)),
            sems((64,)),
            sems((16,)),
            sems((16,)),
        ],
        compiler_params=pltpu.CompilerParams(
            collective_id=0, has_side_effects=True, vmem_limit_bytes=56 * 1024 * 1024
        ),
        name="decode",
    )(
        lengths,
        placement.reshape(1, 16),
        jnp.swapaxes(queries[:, 0], 0, 1),
        jnp.swapaxes(latents[:, 0], 0, 1),
        jnp.swapaxes(resident_cache[0], 1, 2),
        slices,
        w_key,
        w_value,
        jnp.swapaxes(w_out, 0, 1),
    )
    return out[:, None]


def solution(mesh):
    placed = (
        P("grp", None, None, None),
        P("grp", None),
        P("grp", None, None),
        P("grp", None),
        P(None, "grp", None, "head"),
        P(None, "grp", None, None),
        P("head", None, None),
        P("head", None, None),
        P("head", "grp"),
    )
    return jax.shard_map(
        body, mesh=mesh, in_specs=placed, out_specs=P(None, "grp", None, "head"), check_vma=False
    )
```
